32 devices in a mesh: shard: 4 (over y, x), context: 4 (over z), tensor: 2 (over core).
Axes of the slice: x: 2, y: 2, z: 4, core: 2. Of those that a mesh axis runs over, the one named last changes fastest.
Arguments:
- clips_in: bfloat16 [32, 8, 196, 768], P(('shard', 'tensor'), 'context'), may hold values from -6 to 6
- valid_clips: int32 [32], P(('shard', 'tensor')), may hold values 0 or 1
- norm_gains: float32 [3, 768], replicated, may hold values from 0.25 to 1.75
- norm_shifts: float32 [3, 768], replicated, may hold values from -4 to 4
- temporal_qkv: float32 [768, 3, 768], P(('shard', 'context', 'tensor')), may hold values from -0.21875 to 0.21875
- temporal_proj: float32 [768, 768], P(('shard', 'context', 'tensor')), may hold values from -0.4375 to 0.4375
- temporal_fc: float32 [768, 768], P(('shard', 'context', 'tensor')), may hold values from -0.21875 to 0.21875
- spatial_qkv: float32 [768, 3, 768], P(('shard', 'context', 'tensor')), may hold values from -0.21875 to 0.21875
- spatial_proj: float32 [768, 768], P(('shard', 'context', 'tensor')), may hold values from -1.75 to 1.75
- mlp_in: float32 [768, 3072], P(('shard', 'context'), 'tensor'), may hold values from -0.21875 to 0.21875
- mlp_out: float32 [768, 3072], P(('shard', 'context'), 'tensor'), may hold values from -0.3125 to 0.3125
- head_bias: float32 [2, 2, 768], replicated, may hold values from -6 to 6
- width_bias: float32 [3, 768], replicated, may hold values from -6 to 6
- fc_bias: float32 [768], replicated, may hold values from -6 to 6
- hidden_bias: float32 [3072], replicated, may hold values from -6 to 6
- cotangent: bfloat16 [32, 8, 196, 768], P(('shard', 'tensor'), 'context'), may hold values from -6 to 6
Outputs:
- output: bfloat16 [32, 8, 196, 768], P(('shard', 'tensor'), 'context')
- input_grad: bfloat16 [32, 8, 196, 768], P(('shard', 'tensor'), 'context')
- norm_gains_grad: float32 [3, 768], replicated
- norm_shifts_grad: float32 [3, 768], replicated
- temporal_qkv_grad: float32 [768, 3, 768], P(('shard', 'context', 'tensor'))
- temporal_proj_grad: float32 [768, 768], P(('shard', 'context', 'tensor'))
- temporal_fc_grad: float32 [768, 768], P(('shard', 'context', 'tensor'))
- spatial_qkv_grad: float32 [768, 3, 768], P(('shard', 'context', 'tensor'))
- spatial_proj_grad: float32 [768, 768], P(('shard', 'context', 'tensor'))
- mlp_in_grad: float32 [768, 3072], P(('shard', 'context'), 'tensor')
- mlp_out_grad: float32 [768, 3072], P(('shard', 'context'), 'tensor')
- head_bias_grad: float32 [2, 2, 768], replicated
- width_bias_grad: float32 [3, 768], replicated
- fc_bias_grad: float32 [768], replicated
- hidden_bias_grad: float32 [3072], replicated
The draws below stay inside these ranges and needn't reach their ends.
Inputs may be any that keep to these rules, and one draw needn't show every extreme that they name: `valid_clips`: 1 marks a real clip, 0 a padding clip.
All inputs are finite; a program needn't handle non-finite values. No bound on the sum of `valid_clips` on one device may be relied on, other than what follows from the above.
Results may differ from the reference program's by a relative error of at most 0.02.
Values may be sent and summed in bfloat16 or wider, within the bound.
No kernel may reach another device: no remote copies, remote signals or barrier semaphores. Data moves between devices by JAX's collectives and lax.ppermute only.
A program may use at most 384 MiB of HBM per device.

```python
import jax
import jax.numpy as jnp
from jax import lax

D = 768
HEADS = 12
FF = 3072
FRAMES = 8
PLACES = 196
CLIPS = 32


def with_ends(array, own_key, smallest, high):
    place = [jax.random.randint(jax.random.fold_in(own_key, axis), (), 0, length) for axis, length in enumerate(array.shape)]
    widest = array.shape.index(max(array.shape))
    beside = place[:widest] + [(place[widest] + 1) % array.shape[widest]] + place[widest + 1:]
    return array.at[tuple(place)].set(smallest).at[tuple(beside)].set(high)


def block_levels(stream_key, extent, pieces, smallest, largest):
    factor_of, own = 1.0, jax.random.fold_in(stream_key, 6)
    for position, shards_of in pieces:
        heights = jnp.exp(jax.random.uniform(jax.random.fold_in(own, position), (shards_of,), jnp.float32, smallest / len(pieces), largest / len(pieces)))
        factor_of = factor_of * jnp.repeat(heights, extent[position] // shards_of).reshape([-1 if axis == position else 1 for axis in range(len(extent))])
    return factor_of


def normal_values(stream_key, dims, deviation, limit, shards=(), held_as=jnp.bfloat16):
    drawn = deviation * jax.random.normal(stream_key, dims, jnp.float32)
    if shards:
        drawn = drawn * block_levels(stream_key, dims, shards, -0.22, 0.18)
    return jnp.clip(drawn, -limit, limit).astype(held_as)


def setup_inputs(seed: int = 0) -> dict:
    key_list = jax.random.split(jax.random.key(seed), 17)
    return {
        "clips_in": normal_values(key_list[0], (CLIPS, FRAMES, PLACES, D), 1.0, 6.0, ((0, 8), (1, 4))),
        "valid_clips": with_ends((jax.random.randint(key_list[1], (CLIPS,), 0, 4) < 3).astype(jnp.int32), jax.random.fold_in(key_list[1], 1), 0, 1),
        "norm_gains": jnp.clip(1.0 + 0.15 * jax.random.normal(key_list[2], (3, D), jnp.float32), 0.25, 1.75),
        "norm_shifts": normal_values(key_list[3], (3, D), 0.3, 4.0, (), jnp.float32),
        "temporal_qkv": normal_values(key_list[4], (D, 3, D), D ** -0.5, 0.21875, ((0, 32),), jnp.float32),
        "temporal_proj": normal_values(key_list[5], (D, D), (D // 4) ** -0.5, 0.4375, ((0, 32),), jnp.float32),
        "temporal_fc": normal_values(key_list[6], (D, D), D ** -0.5, 0.21875, ((0, 32),), jnp.float32),
        "spatial_qkv": normal_values(key_list[7], (D, 3, D), D ** -0.5, 0.21875, ((0, 32),), jnp.float32),
        "spatial_proj": normal_values(key_list[8], (D, D), (max(D // 64, 1)) ** -0.5, 1.75, ((0, 32),), jnp.float32),
        "mlp_in": normal_values(key_list[9], (D, FF), D ** -0.5, 0.21875, ((0, 16), (1, 2)), jnp.float32),
        "mlp_out": normal_values(key_list[10], (D, FF), (FF // 8) ** -0.5, 0.3125, ((0, 16), (1, 2)), jnp.float32),
        "head_bias": normal_values(key_list[11], (2, 2, D), 0.5, 6.0, (), jnp.float32),
        "width_bias": normal_values(key_list[12], (3, D), 0.5, 6.0, (), jnp.float32),
        "fc_bias": normal_values(key_list[13], (D,), 0.5, 6.0, (), jnp.float32),
        "hidden_bias": normal_values(key_list[14], (FF,), 0.5, 6.0, (), jnp.float32),
        "cotangent": normal_values(key_list[15], (CLIPS, FRAMES, PLACES, D), 1.0, 6.0, ((0, 8), (1, 4))),
    }


@jax.custom_vjp
def low(v):
    return lax.optimization_barrier(v.astype(jnp.bfloat16)).astype(jnp.float32)

@jax.custom_vjp
def low_back(v):
    return v

def low_keep(v):
    return (low(v), None)

def low_pass(kept, grad):
    return (grad,)

def back_keep(v):
    return (v, None)

def back_low(kept, grad):
    return (low(grad),)
low.defvjp(low_keep, low_pass)
low_back.defvjp(back_keep, back_low)
exact_mode = lax.Precision.HIGHEST
norm_eps = 1e-05

def norm_apply(values_in, gain_row, shift_row):
    center_mean = lax.optimization_barrier(jnp.mean(values_in, axis=-1, keepdims=True))
    centered = values_in - center_mean
    variance = lax.optimization_barrier(jnp.mean(centered * centered, axis=-1, keepdims=True))
    return centered * lax.rsqrt(variance + norm_eps) * gain_row + shift_row

def split_heads(tensor_in):
    return tensor_in.reshape(tensor_in.shape[:-1] + (HEADS, tensor_in.shape[-1] // HEADS))

def project_qkv(normed, weight_all, bias_pair):
    packed = jnp.einsum('fpd,dkn->kfpn', normed, weight_all, precision=exact_mode)
    query_pre = packed[0] + bias_pair[0]
    keys_pre = packed[1]
    values_pre = packed[2] + bias_pair[1]
    return tuple((split_heads(low_back(low(item_pre))) for item_pre in (query_pre, keys_pre, values_pre)))

def clip_forward(params, clip_rows, keep_flag):
    gains, shifts, t_qkv, t_proj, t_fc, s_qkv, s_proj, w_in, w_out, head_b, width_b, fc_b, hid_b = params
    scale_factor = (clip_rows.shape[-1] // HEADS) ** (-0.5)
    normed_t = low(norm_apply(clip_rows, gains[0], shifts[0]))
    query_t, keys_t, values_t = project_qkv(normed_t, low(t_qkv), head_b[0])
    scores_t = low_back(jnp.einsum('fphe,gphe->phfg', query_t, keys_t, precision=exact_mode) * scale_factor)
    probs_t = low(jax.nn.softmax(scores_t, axis=-1))
    mixed_t = jnp.einsum('phfg,gphe->fphe', probs_t, values_t, precision=exact_mode)
    mixed_t = low_back(low(mixed_t.reshape(clip_rows.shape)))
    proj_t = jnp.einsum('fpn,en->fpe', mixed_t, low(t_proj), precision=exact_mode) + width_b[0]
    proj_t = low_back(low(proj_t))
    fc_out = low_back(low(jnp.einsum('fpd,de->fpe', proj_t, low(t_fc), precision=exact_mode) + fc_b))
    after_t = clip_rows + fc_out
    normed_s = low(norm_apply(after_t, gains[1], shifts[1]))
    query_s, keys_s, values_s = project_qkv(normed_s, low(s_qkv), head_b[1])
    scores_s = low_back(jnp.einsum('fphe,fqhe->fhpq', query_s, keys_s, precision=exact_mode) * scale_factor)
    probs_s = low(jax.nn.softmax(scores_s, axis=-1))
    mixed_s = jnp.einsum('fhpq,fqhe->fphe', probs_s, values_s, precision=exact_mode)
    mixed_s = low_back(low(mixed_s.reshape(clip_rows.shape)))
    branch_s = low_back(jnp.einsum('fpn,en->fpe', mixed_s, low(s_proj), precision=exact_mode) + width_b[1])
    after_s = after_t + branch_s
    normed_m = low(norm_apply(after_s, gains[2], shifts[2]))
    hidden_pre = low_back(jnp.einsum('fpd,dh->fph', normed_m, low(w_in), precision=exact_mode) + hid_b)
    hidden_act = low(jax.nn.gelu(hidden_pre, approximate=False))
    branch_m = low_back(jnp.einsum('fph,eh->fpe', hidden_act, low(w_out), precision=exact_mode) + width_b[2])
    after_m = after_s + branch_m
    return keep_flag * after_m

def reference(clips_in, valid_clips, norm_gains, norm_shifts, temporal_qkv, temporal_proj, temporal_fc, spatial_qkv, spatial_proj, mlp_in, mlp_out, head_bias, width_bias, fc_bias, hidden_bias, cotangent):
    params = tuple((item_arr.astype(jnp.float32) for item_arr in (norm_gains, norm_shifts, temporal_qkv, temporal_proj, temporal_fc, spatial_qkv, spatial_proj, mlp_in, mlp_out, head_bias, width_bias, fc_bias, hidden_bias)))
    inputs_all = clips_in.astype(jnp.float32)
    pulls_all = cotangent.astype(jnp.float32)
    keeps_all = valid_clips.astype(jnp.float32)

    def one_clip(running, entry):
        clip_rows, keep_flag, pull_rows = entry
        result, back_fn = jax.vjp(lambda param_set, rows_in: clip_forward(param_set, rows_in, keep_flag), params, clip_rows)
        param_grads, rows_grad = back_fn(pull_rows)
        running = jax.tree.map(lambda left_sum, right_sum: left_sum + right_sum, running, param_grads)
        return (running, (result.astype(jnp.bfloat16), rows_grad.astype(jnp.bfloat16)))
    zero_grads = jax.tree.map(jnp.zeros_like, params)
    grads, (outputs, input_grads) = lax.scan(one_clip, zero_grads, (inputs_all, keeps_all, pulls_all))
    return (outputs, input_grads, grads[0], grads[1], grads[2], grads[3], grads[4], grads[5], grads[6], grads[7], grads[8], grads[9], grads[10], grads[11], grads[12])
```

```python
from functools import partial

import jax
import jax.numpy as jnp
from jax import lax
from jax.experimental import pallas as pl
from jax.experimental.pallas import tpu as pltpu
from jax.sharding import PartitionSpec as P

HEADS = 12
EPS = 1e-05
ALL = ("shard", "context", "tensor")
BF = jnp.bfloat16
F32 = jnp.float32
VMEM = 60 * 2**20

def mm(left, right, left_dim, right_dim):
    return lax.dot_general(left, right, (((left_dim,), (right_dim,)), ((), ())), preferred_element_type=F32)

def norm_stats(rows):
    centered = rows - jnp.mean(rows, axis=-1, keepdims=True)
    inv = lax.rsqrt(jnp.mean(centered * centered, axis=-1, keepdims=True) + EPS)
    return centered * inv, inv

def mlp_kernel(x_ref, cot_ref, keep_ref, gain_ref, shift_ref, w_ref, hb_ref, wb_ref,
               out_ref, g2_ref, db_ref, dw_ref, dhb_ref, sums_ref,
               a_ref, at_ref, dm_ref, dmt_ref, m_ref, da_ref, h_ref, du_ref, *, rb, chunks):
    step = pl.program_id(0)
    T, D = x_ref.shape
    nb = T // rb
    blocks, _, both, hc = w_ref.shape
    half = both // 2

    @pl.when(step == 0)
    def _():
        def body(i, c):
            r = pl.ds(pl.multiple_of(i * rb, 16), rb)
            unit, _ = norm_stats(x_ref[r, :])
            a = (unit * gain_ref[...] + shift_ref[...]).astype(BF)
            a_ref[r, :] = a
            dm = (keep_ref[0, 0] * cot_ref[r, :].astype(F32)).astype(BF)
            dm_ref[r, :] = dm
            return c
        lax.fori_loop(0, nb, body, 0)
        at_ref[...] = a_ref[...].T
        dmt_ref[...] = dm_ref[...].T

    win = w_ref[:, 0, :half, :].reshape(D, hc)
    wout = w_ref[:, 0, half:, :].reshape(D, hc)
    hb = hb_ref[...]
    tot = jnp.zeros((1, hc), F32)
    for i in range(nb):
        r = slice(i * rb, (i + 1) * rb)
        u = mm(a_ref[r, :], win, 1, 0) + hb
        cdf = 0.5 * (1.0 + lax.erf(u * (2 ** -0.5)))
        h = (u * cdf).astype(BF)
        pdf = jnp.exp(-0.5 * u * u) * ((2 * jnp.pi) ** -0.5)
        dh = mm(dm_ref[r, :], wout, 1, 0)
        du = ((cdf + u * pdf) * dh).astype(BF)
        h_ref[r, :] = h
        du_ref[r, :] = du
        tot += jnp.sum(du.astype(F32), axis=0, keepdims=True)
        m = mm(h, wout, 1, 1)
        da = mm(du, win, 1, 1)
        @pl.when(step == 0)
        def _():
            m_ref[r, :] = m
            da_ref[r, :] = da
        @pl.when(step > 0)
        def _():
            m_ref[r, :] += m
            da_ref[r, :] += da
    dhb_ref[...] = tot
    dw_ref[0, :, :half, :] = mm(at_ref[...], du_ref[...], 1, 0).astype(BF).reshape(blocks, half, hc)
    dw_ref[0, :, half:, :] = mm(dmt_ref[...], h_ref[...], 1, 0).astype(BF).reshape(blocks, half, hc)

    @pl.when(step == chunks - 1)
    def _():
        k = keep_ref[0, 0]
        def body(i, c):
            r = pl.ds(pl.multiple_of(i * rb, 16), rb)
            x = x_ref[r, :]
            out_ref[r, :] = (k * (x + (m_ref[r, :] + wb_ref[...]))).astype(BF)
            g3 = k * cot_ref[r, :].astype(F32)
            da = da_ref[r, :]
            unit, inv = norm_stats(x)
            sc = da * gain_ref[...]
            into = inv * (sc - jnp.mean(sc, axis=-1, keepdims=True) - unit * jnp.mean(sc * unit, axis=-1, keepdims=True))
            g2 = g3 + into
            g2_ref[r, :] = g2
            low = g2.astype(BF)
            db_ref[r, :] = low
            return (c[0] + jnp.sum(da * unit, axis=0, keepdims=True),
                    c[1] + jnp.sum(da, axis=0, keepdims=True),
                    c[2] + jnp.sum(dm_ref[r, :].astype(F32), axis=0, keepdims=True),
                    c[3] + jnp.sum(low.astype(F32), axis=0, keepdims=True))
        z = jnp.zeros((1, D), F32)
        c = lax.fori_loop(0, nb, body, (z, z, z, z))
        for j in range(4):
            sums_ref[j:j+1, :] = c[j]

def mlp(x2, cot, keep, gain, shift, w4, hb, wb):
    T, D = x2.shape
    B, H2, R, C = w4.shape
    rb = T // 4 if T % 64 == 0 else T
    hc = next(w for w in (768, 512, 384, 256, 128) if C % w == 0)
    per = C // hc
    chunks = H2 * per
    full = lambda *s: pl.BlockSpec(s, lambda j: (0,) * len(s), pipeline_mode=pl.Buffered(1))
    wspec = pl.BlockSpec((B, 1, R, hc), lambda j: (0, j // per, 0, j % per))
    dspec = pl.BlockSpec((1, B, R, hc), lambda j: (j // per, 0, 0, j % per))
    hspec = pl.BlockSpec((1, hc), lambda j: (0, j))
    return pl.pallas_call(
        partial(mlp_kernel, rb=rb, chunks=chunks),
        grid=(chunks,),
        in_specs=[full(T, D), full(T, D), pl.BlockSpec(memory_space=pltpu.SMEM), full(1, D), full(1, D), wspec, hspec, full(1, D)],
        out_specs=[full(T, D), full(T, D), full(T, D), dspec, hspec, full(8, D)],
        out_shape=(sds(T, D), sds(T, D, t=F32), sds(T, D), sds(H2, B, R, C), sds(1, H2 * C, t=F32), sds(8, D, t=F32)),
        scratch_shapes=[pltpu.VMEM((T, D), BF), pltpu.VMEM((D, T), BF), pltpu.VMEM((T, D), BF), pltpu.VMEM((D, T), BF),
                        pltpu.VMEM((T, D), F32), pltpu.VMEM((T, D), F32), pltpu.VMEM((T, hc), BF), pltpu.VMEM((T, hc), BF)],
        compiler_params=pltpu.CompilerParams(vmem_limit_bytes=VMEM),
        cost_estimate=cost(75),
    )(x2, cot, keep, gain, shift, w4, hb, wb)
LANES = 128
LOW = -1e30

def once(*s):
    return pl.BlockSpec(s, lambda j: (0,) * len(s), pipeline_mode=pl.Buffered(1))

def column(rows, cols, at):
    return pl.BlockSpec((rows, cols), lambda j: (0, at), pipeline_mode=pl.Buffered(1))

def sds(*s, t=BF):
    return jax.ShapeDtypeStruct(s, t)

def cost(us):
    return pl.CostEstimate(flops=us * 10**9, bytes_accessed=0, transcendentals=0)

def call(body, us, grid, ins, outs, shapes, scratch=()):
    return pl.pallas_call(body, grid=(grid,), in_specs=ins, out_specs=outs, out_shape=shapes, scratch_shapes=list(scratch),
                          compiler_params=pltpu.CompilerParams(vmem_limit_bytes=VMEM), cost_estimate=cost(us))

def qkv_store(a, wqkv, hb_ref, dst, rows, D):
    packed = mm(a, wqkv, 1, 0)
    dst[rows, :D] = (packed[:, :D] + hb_ref[0:1, :]).astype(BF)
    dst[rows, D:2 * D] = packed[:, D:2 * D].astype(BF)
    dst[rows, 2 * D:] = (packed[:, 2 * D:] + hb_ref[1:2, :]).astype(BF)

def lane_masks(head, value):
    lane = lax.broadcasted_iota(jnp.int32, (1, LANES), 1)
    return [jnp.where(lane // head == i, value, 0.0).astype(BF) for i in range(LANES // head)]

def sf_kernel(x_ref, gain_ref, shift_ref, wqkv_ref, wproj_ref, hb_ref, wb_ref, a_ref, qkv_ref, o_ref, x2_ref, *, fb, real, head, scale):
    M, D = x_ref.shape
    P = M // fb
    unit, _ = norm_stats(x_ref[...])
    a = (unit * gain_ref[...] + shift_ref[...]).astype(BF)
    a_ref[...] = a
    qkv_store(a, wqkv_ref[...], hb_ref, qkv_ref, slice(0, M), D)
    col = lax.broadcasted_iota(jnp.int32, (1, P), 1)
    hide = jnp.where(col < real, 0.0, LOW)
    ones = lane_masks(head, 1.0)
    for f in range(fb):
        r = slice(f * P, (f + 1) * P)
        for j in range(D // LANES):
            q = qkv_ref[r, j * LANES:(j + 1) * LANES]
            k = qkv_ref[r, D + j * LANES:D + (j + 1) * LANES]
            v = qkv_ref[r, 2 * D + j * LANES:2 * D + (j + 1) * LANES]
            o = None
            for m in ones:
                s = mm(q * m, k, 1, 1) * scale + hide
                p = jnp.exp(s - jnp.max(s, axis=-1, keepdims=True))
                p = (p * (1.0 / jnp.sum(p, axis=-1, keepdims=True))).astype(BF)
                part = mm(p, v * m, 1, 0)
                o = part if o is None else o + part
            o_ref[r, j * LANES:(j + 1) * LANES] = o.astype(BF)
    x2_ref[...] = x_ref[...] + (mm(o_ref[...], wproj_ref[...], 1, 1) + wb_ref[...])

def spatial_forward(x1, gain, shift, w, hb, wb, *, frames, real, head, scale, fb=2):
    T, D = x1.shape
    M = T // frames * fb
    blk = lambda w: pl.BlockSpec((M, w), lambda j: (j, 0))
    return call(partial(sf_kernel, fb=fb, real=real, head=head, scale=scale), 30, frames // fb,
        [blk(D), once(1, D), once(1, D), column(D, 3 * D, 0), column(D, D, 3), once(2, D), once(1, D)],
        [blk(D), blk(3 * D), blk(D), blk(D)], (sds(T, D), sds(T, 3 * D), sds(T, D), sds(T, D, t=F32)))(
        x1, gain, shift, w, w, hb, wb)

def norm_back_store(x, gain, da, base, sums_ref, at):
    unit, inv = norm_stats(x)
    sc = da * gain
    into = inv * (sc - jnp.mean(sc, axis=-1, keepdims=True) - unit * jnp.mean(sc * unit, axis=-1, keepdims=True))
    sums_ref[at:at + 1, :] += jnp.sum(da * unit, axis=0, keepdims=True)
    sums_ref[at + 1:at + 2, :] += jnp.sum(da, axis=0, keepdims=True)
    return base + into

def add_sum(sums_ref, at, rows):
    sums_ref[at:at + 1, :] += jnp.sum(rows.astype(F32), axis=0, keepdims=True)

def sb_kernel(g2_ref, db_ref, qkv_ref, x_ref, gain_ref, wqkv_ref, wproj_ref, *rest, fb, real, head, scale):
    dqkv_ref, g1_ref, dz_ref, sums_ref, do_ref = rest[-5:]
    M, D = x_ref.shape
    P = M // fb
    @pl.when(pl.program_id(0) == 0)
    def _():
        sums_ref[...] = jnp.zeros_like(sums_ref)
    do_ref[...] = mm(db_ref[...], wproj_ref[...], 1, 0).astype(BF)
    row = lax.broadcasted_iota(jnp.int32, (P, 1), 0)
    hide = jnp.where(row < real, 0.0, LOW)
    ones = lane_masks(head, 1.0)
    for f in range(fb):
        r = slice(f * P, (f + 1) * P)
        for j in range(D // LANES):
            ls = [slice(i * D + j * LANES, i * D + (j + 1) * LANES) for i in range(3)]
            q, k, v = [qkv_ref[r, l] for l in ls]
            do = do_ref[r, ls[0]]
            dq = dk = dv = 0.0
            for m in ones:
                qm = q * m
                dom = do * m
                s = mm(k, qm, 1, 1) * scale + hide
                p = jnp.exp(s - jnp.max(s, axis=0, keepdims=True))
                p = p * (1.0 / jnp.sum(p, axis=0, keepdims=True))
                dp = mm(v, dom, 1, 1)
                ds = (p * (dp - jnp.sum(p * dp, axis=0, keepdims=True))).astype(BF)
                dv = dv + mm(p.astype(BF), dom, 1, 0)
                dk = dk + mm(ds, qm, 1, 0)
                dq = dq + mm(ds, k * m, 0, 0)
            dqkv_ref[r, ls[0]] = (dq * scale).astype(BF)
            dqkv_ref[r, ls[1]] = (dk * scale).astype(BF)
            dqkv_ref[r, ls[2]] = dv.astype(BF)
    add_sum(sums_ref, 2, dqkv_ref[:, :D])
    add_sum(sums_ref, 3, dqkv_ref[:, 2 * D:])
    da = mm(dqkv_ref[...], wqkv_ref[...], 1, 1)
    g1 = norm_back_store(x_ref[...], gain_ref[...], da, g2_ref[...], sums_ref, 0)
    g1_ref[...] = g1
    low = g1.astype(BF)
    dz_ref[...] = low
    add_sum(sums_ref, 4, low)

def spatial_backward(g2, db, qkv, x1, *, gain, w, frames, real, head, scale, part, held=None, fb=2):
    T, D = x1.shape
    M = T // frames * fb
    nb = frames // fb // 2
    blk = lambda w: pl.BlockSpec((M, w), lambda j: (j + part * nb, 0))
    kept = [] if held is None else list(held[:3])
    return pl.pallas_call(
        partial(sb_kernel, fb=fb, real=real, head=head, scale=scale), grid=(nb,),
        in_specs=[blk(D), blk(D), blk(3 * D), blk(D), once(1, D), column(D, 3 * D, 0), column(D, D, 3)]
        + [pl.BlockSpec(memory_space=pl.ANY)] * len(kept),
        out_specs=[blk(3 * D), blk(D), blk(D), once(8, D)],
        out_shape=(sds(T, 3 * D), sds(T, D, t=F32), sds(T, D), sds(8, D, t=F32)),
        scratch_shapes=[pltpu.VMEM((M, D), BF)],
        input_output_aliases={7 + i: i for i in range(len(kept))},
        compiler_params=pltpu.CompilerParams(vmem_limit_bytes=VMEM), cost_estimate=cost(24),
    )(g2, db, qkv, x1, gain, w, w, *kept)

def over_frames(op, rows, slot):
    shift = slot
    while shift < LANES:
        rows = op(rows, pltpu.roll(rows, shift, 1))
        shift *= 2
    return rows

def tf_kernel(x_ref, gain_ref, shift_ref, wqkv_ref, wproj_ref, wfc_ref, hb_ref, wb_ref, fcb_ref, e_ref, b_ref,
              a_ref, qkv_ref, p_ref, o_ref, y_ref, x1_ref, all_ref, prod_ref, xs_ref, *, fb, nb, frames, slot, scale):
    M, D = x_ref.shape
    P = M // fb
    step = pl.program_id(0)
    @pl.when(step < nb)
    def _():
        x = x_ref[...].astype(F32)
        unit, _ = norm_stats(x)
        a = (unit * gain_ref[...] + shift_ref[...]).astype(BF)
        a_ref[...] = a
        qkv_store(a, wqkv_ref[...], hb_ref, qkv_ref, slice(0, M), D)
        all_ref[pl.ds(pl.multiple_of(step * M, M), M), :] = qkv_ref[...]
        xs_ref[pl.ds(pl.multiple_of(step * M, M), M), :] = x_ref[...]
    @pl.when(step >= nb)
    def _():
        base = pl.multiple_of((step - nb) * M, M)
        for f in range(fb):
            q = all_ref[pl.ds(base + f * P, P), :D]
            for g in range(frames):
                prod_ref[f * P:(f + 1) * P, g * D:(g + 1) * D] = q * all_ref[g * P:(g + 1) * P, D:2 * D]
        s = mm(prod_ref[...], e_ref[...], 1, 0) * scale
        p = jnp.exp(s - over_frames(jnp.maximum, s, slot))
        p = p * (1.0 / over_frames(jnp.add, p, slot))
        p_ref[...] = p
        low = p.astype(BF)
        o = [None] * fb
        for g in range(frames):
            wide = mm(low, b_ref[:, g * D:(g + 1) * D], 1, 0)
            v = all_ref[g * P:(g + 1) * P, 2 * D:].astype(F32)
            for f in range(fb):
                part = wide[f * P:(f + 1) * P] * v
                o[f] = part if g == 0 else o[f] + part
        for f in range(fb):
            o_ref[f * P:(f + 1) * P, :] = o[f].astype(BF)
        y = (mm(o_ref[...], wproj_ref[...], 1, 1) + wb_ref[...]).astype(BF)
        y_ref[...] = y
        z = (mm(y, wfc_ref[...], 1, 0) + fcb_ref[...]).astype(BF)
        x1_ref[...] = xs_ref[pl.ds(base, M), :].astype(F32) + z.astype(F32)

def temporal_tables(D, head, frames):
    slot = LANES // frames
    lane = jnp.arange(LANES)
    feat = jnp.arange(frames * D)
    e = ((feat[:, None] // D == lane[None, :] // slot) & ((feat[:, None] % D) // head == lane[None, :] % slot)).astype(BF)
    return e, e.T

def temporal_forward(x, gain, shift, w, hb, wb, fcb, e, b, *, frames, scale, fb=2):
    T, D = x.shape
    M = T // frames * fb
    nb = frames // fb
    first = lambda w: pl.BlockSpec((M, w), lambda j: (jnp.minimum(j, nb - 1), 0))
    last = lambda w: pl.BlockSpec((M, w), lambda j: (jnp.maximum(j - nb, 0), 0))
    return call(partial(tf_kernel, fb=fb, nb=nb, frames=frames, slot=LANES // frames, scale=scale), 44, 2 * nb,
        [first(D), once(1, D), once(1, D), column(D, 3 * D, 0), column(D, D, 3), column(D, D, 4), once(2, D), once(1, D), once(1, D), once(*e.shape), once(*b.shape)],
        [first(D), first(3 * D), last(LANES), last(D), last(D), last(D)],
        (sds(T, D), sds(T, 3 * D), sds(T, LANES, t=F32), sds(T, D), sds(T, D), sds(T, D, t=F32)),
        [pltpu.VMEM((T, 3 * D), BF), pltpu.VMEM((M, frames * D), BF), pltpu.VMEM((T, D), BF)])(
        x, gain, shift, w, w, w, hb, wb, fcb, e, b)

def zero_first(*refs):
    @pl.when(pl.program_id(0) == 0)
    def _():
        for ref in refs:
            ref[...] = jnp.zeros_like(ref)

def pull_kernel(dz_ref, wproj_ref, wfc_ref, dy_ref, do_ref, sums_ref):
    zero_first(sums_ref)
    dy = mm(dz_ref[...], wfc_ref[...], 1, 1).astype(BF)
    dy_ref[...] = dy
    add_sum(sums_ref, 4, dy)
    do_ref[...] = mm(dy, wproj_ref[...], 1, 0).astype(BF)

def temporal_pull(dz, w, *, blocks=4):
    T, D = dz.shape
    blk = pl.BlockSpec((T // blocks, D), lambda j: (j, 0))
    return call(pull_kernel, 8, blocks, [blk, column(D, D, 3), column(D, D, 4)], [blk, blk, once(8, D)],
                (sds(T, D), sds(T, D), sds(8, D, t=F32)))(dz, w, w)

def tb_kernel(do_ref, qkv_ref, p_ref, e_ref, b_ref, dqkv_ref, sums_ref, dk_ref, dv_ref, prod_ref, *, fb, nb, frames, slot, scale):
    M = p_ref.shape[0]
    T, D = do_ref.shape
    P = M // fb
    step = pl.program_id(0)
    zero_first(sums_ref, dk_ref, dv_ref)
    base = pl.multiple_of(step * M, M)
    for f in range(fb):
        do = do_ref[pl.ds(base + f * P, P), :]
        for g in range(frames):
            prod_ref[f * P:(f + 1) * P, g * D:(g + 1) * D] = do * qkv_ref[g * P:(g + 1) * P, 2 * D:]
    dp = mm(prod_ref[...], e_ref[...], 1, 0)
    p = p_ref[...]
    ds = (p * (dp - over_frames(jnp.add, p * dp, slot))).astype(BF)
    low = p.astype(BF)
    dq = [0.0] * fb
    for g in range(frames):
        gr = slice(g * P, (g + 1) * P)
        wide_p = mm(low, b_ref[:, g * D:(g + 1) * D], 1, 0)
        wide_s = mm(ds, b_ref[:, g * D:(g + 1) * D], 1, 0)
        k = qkv_ref[gr, D:2 * D].astype(F32)
        dk, dv = dk_ref[gr, :], dv_ref[gr, :]
        for f in range(fb):
            fr = pl.ds(base + f * P, P)
            wp, ws = wide_p[f * P:(f + 1) * P], wide_s[f * P:(f + 1) * P]
            dv = dv + wp * do_ref[fr, :].astype(F32)
            dk = dk + ws * qkv_ref[fr, :D].astype(F32)
            dq[f] = dq[f] + ws * k
        dk_ref[gr, :] = dk
        dv_ref[gr, :] = dv
    for f in range(fb):
        low = (dq[f] * scale).astype(BF)
        add_sum(sums_ref, 2, low)
        dqkv_ref[pl.ds(base + f * P, P), :D] = low
    @pl.when(step == nb - 1)
    def _():
        for g in range(frames):
            gr = slice(g * P, (g + 1) * P)
            dqkv_ref[gr, D:2 * D] = (dk_ref[gr, :] * scale).astype(BF)
            low = dv_ref[gr, :].astype(BF)
            add_sum(sums_ref, 3, low)
            dqkv_ref[gr, 2 * D:] = low

def temporal_backward(do, qkv, p, e, b, *, frames, scale, fb=2):
    T, D = do.shape
    M = T // frames * fb
    nb = frames // fb
    return call(partial(tb_kernel, fb=fb, nb=nb, frames=frames, slot=LANES // frames, scale=scale), 40, nb,
        [once(T, D), once(T, 3 * D), pl.BlockSpec((M, LANES), lambda j: (j, 0)), once(*e.shape), once(*b.shape)],
        [once(T, 3 * D), once(8, D)], (sds(T, 3 * D), sds(8, D, t=F32)),
        [pltpu.VMEM((T, D), F32), pltpu.VMEM((T, D), F32), pltpu.VMEM((M, frames * D), BF)])(do, qkv, p, e, b)

def end_kernel(dqkv_ref, x_ref, g1_ref, gain_ref, wqkv_ref, out_ref, sums_ref):
    zero_first(sums_ref)
    da = mm(dqkv_ref[...], wqkv_ref[...], 1, 1)
    out = norm_back_store(x_ref[...].astype(F32), gain_ref[...], da, g1_ref[...], sums_ref, 0)
    out_ref[...] = out.astype(BF)

def temporal_end(dqkv, x, g1, gain, w, *, blocks=4):
    T, D = x.shape
    blk = lambda w: pl.BlockSpec((T // blocks, w), lambda j: (j, 0))
    return call(end_kernel, 12, blocks, [blk(3 * D), blk(D), blk(D), once(1, D), column(D, 3 * D, 0)], [blk(D), once(8, D)],
                (sds(T, D), sds(8, D, t=F32)))(dqkv, x, g1, gain, w)

def wg_kernel(*refs, starts, halves, rows):
    n = len(starts)
    a_refs, b_refs, out_ref, t_ref = refs[:n], refs[n:2 * n], refs[2 * n], refs[2 * n + 1]
    step = pl.program_id(0)
    for i in range(n):
        @pl.when(step == starts[i])
        def _():
            t_ref[...] = a_refs[i][...].T
        stop = starts[i + 1] if i + 1 < n else step + 1
        @pl.when((step >= starts[i]) & (step < stop))
        def _():
            res = mm(t_ref[...], b_refs[i][...], 1, 0)
            if rows:
                parts = res.reshape(-1, halves, rows, res.shape[-1])
                for h in range(halves):
                    out_ref[h] = parts[:, h].reshape(-1, res.shape[-1]).astype(BF)
            else:
                out_ref[0] = res.astype(BF)

def weight_grads(pairs, halves, rows, us):
    T, D = pairs[0][0].shape
    starts, steps = [], 0
    for a, b in pairs:
        starts.append(steps)
        steps += b.shape[1] // D
    cols = steps * D
    fits = rows % 8 == 0
    def chunk(i):
        many = pairs[i][1].shape[1] // D
        return pl.BlockSpec((T, D), lambda j: (0, jnp.clip(j - starts[i], 0, many - 1)))
    groups = halves if fits else 1
    out = call(partial(wg_kernel, starts=starts, halves=halves, rows=rows if fits else 0), us, steps,
        [once(T, D)] * len(pairs) + [chunk(i) for i in range(len(pairs))],
        [pl.BlockSpec((groups, D // groups, D), lambda j: (0, 0, j))], (sds(groups, D // groups, cols),),
        [pltpu.VMEM((D, T), BF)])(*[a for a, _ in pairs], *[b for _, b in pairs])[0]
    if fits:
        return out.reshape(halves, -1, rows, cols)
    return jnp.swapaxes(out.reshape(-1, halves, rows, cols), 0, 1)


def exchange(pieces, axis):
    size = len(pieces)
    return [pieces[0]] + [
        lax.ppermute(pieces[d], axis, [(i, i ^ d) for i in range(size)]) for d in range(1, size)
    ]


def in_order(pieces, axis, step=1):
    while step < len(pieces):
        swap = (lax.axis_index(axis) // step) % 2 == 1
        pieces = [jnp.where(swap, pieces[c ^ step], pieces[c]) for c in range(len(pieces))]
        step *= 2
    return pieces


def collect(array, axis, at=0, hold=()):
    pieces = exchange([array] * lax.axis_size(axis), axis)
    pieces = pieces[:1] + [after(piece, *hold) for piece in pieces[1:]]
    return jnp.stack(in_order(pieces, axis), axis=at)


def partner(array, axis, step):
    size = lax.axis_size(axis)
    return lax.ppermute(array, axis, [(i, i ^ step) for i in range(size)])


def far_first(array, axis):
    size = lax.axis_size(axis)
    step = size // 2
    out = array[None]
    while step:
        other = partner(out, axis, step)
        low = (lax.axis_index(axis) // step) % 2 == 0
        out = jnp.stack((jnp.where(low, out, other), jnp.where(low, other, out)), axis=1)
        out = out.reshape((-1,) + array.shape)
        step //= 2
    return out


def near_first(array, axis):
    size = lax.axis_size(axis)
    step = 1
    while step < size:
        blocks = array.reshape((-1, 2) + array.shape[1:])
        mine = (lax.axis_index(axis) // step) % 2
        send = lax.dynamic_index_in_dim(blocks, 1 - mine, 1, keepdims=False).astype(BF)
        keep = lax.dynamic_index_in_dim(blocks, mine, 1, keepdims=False)
        array = keep.astype(F32) + partner(send, axis, step).astype(F32)
        step *= 2
    return array[0]


def split_off(array, axis):
    place = lax.axis_index(axis)
    pieces = [
        lax.dynamic_index_in_dim(array, place ^ d, 0, keepdims=False)
        for d in range(lax.axis_size(axis))
    ]
    return exchange(pieces[:1] + [piece.astype(BF) for piece in pieces[1:]], axis)


def added(pieces, *hold):
    out = pieces[0].astype(F32)
    for piece in pieces[1:]:
        out = out + after(piece, *hold).astype(F32)
    return out


def shed(array, axis, hold=()):
    return added(split_off(array, axis), *hold)


def shed_at_once(array, axis):
    came = lax.all_to_all(array.astype(BF), axis, split_axis=0, concat_axis=0, tiled=True)
    return jnp.sum(came.astype(F32), axis=0)


def after(array, *others):
    return lax.optimization_barrier((array,) + others)[0]


def plus_others(array, axis):
    came = exchange([array] * lax.axis_size(axis), axis)
    return sum(came[1:], came[0])


def local(
    clips_in,
    valid_clips,
    norm_gains,
    norm_shifts,
    temporal_qkv,
    temporal_proj,
    temporal_fc,
    spatial_qkv,
    spatial_proj,
    mlp_in,
    mlp_out,
    head_bias,
    width_bias,
    fc_bias,
    hidden_bias,
    cotangent,
):
    held, frames_held, places, width = clips_in.shape
    head = width // HEADS
    scale = head ** (-0.5)
    across = lax.axis_size("context")
    halves = lax.axis_size("tensor")
    place = lax.axis_index("context")
    own_rows = temporal_qkv.shape[0]
    in_rows, in_cols = mlp_in.shape
    spread = held % across == 0
    clips = held // across if spread else held
    share = 1.0 if spread else 1.0 / across
    frames = frames_held * across
    padded = -(-places // 16) * 16

    def to_clips(array):
        array = jnp.swapaxes(array, 1, 2)
        if spread:
            array = lax.all_to_all(array, "context", split_axis=0, concat_axis=0, tiled=True)
            return array.reshape((across, clips) + array.shape[1:])
        return lax.all_gather(array, "context", axis=0)

    def fill(array):
        array = jnp.swapaxes(array, 1, 2).reshape(frames, places, width)
        array = jnp.pad(array, ((0, 0), (0, padded - places), (0, 0)))
        return array.reshape(frames * padded, width)

    def by_place(array):
        array = array.reshape(across, frames_held, padded, width)[:, :, :places]
        return jnp.swapaxes(array, 1, 2)

    def from_clips(array):
        array = by_place(array)
        if spread:
            array = lax.all_to_all(array, "context", split_axis=0, concat_axis=0, tiled=True)
        else:
            array = lax.dynamic_slice_in_dim(array, place, 1, 0)
        return jnp.swapaxes(array, 1, 2)

    def send_back(array):
        array = by_place(array)
        if spread:
            return split_off(array, "context")
        return [lax.dynamic_index_in_dim(array, place, 0, keepdims=False)]

    def sent_back(pieces):
        return jnp.swapaxes(jnp.stack(in_order(pieces, "context")), 1, 2)

    if spread:
        valid = lax.dynamic_slice_in_dim(valid_clips, place * clips, clips, 0)
    else:
        valid = valid_clips
    keep = valid.astype(F32)

    def flat3(weight):
        return weight.reshape(own_rows, 3 * width)

    def by_shard(d):
        return d.reshape((lax.axis_size("shard"), across) + d.shape[1:])

    t_own = jnp.concatenate((flat3(temporal_qkv), temporal_proj, temporal_fc), axis=1).astype(BF)
    s_own = jnp.concatenate((flat3(spatial_qkv), spatial_proj), axis=1).astype(BF)
    mlp_own = jnp.concatenate((mlp_in, mlp_out), axis=0).astype(BF)
    first = collect(jnp.concatenate((t_own, s_own), axis=1), "context")
    t_first, s_first = first[..., : t_own.shape[1]], first[..., t_own.shape[1] :]
    mlp_all = lax.all_gather(after(mlp_own, first), ALL, axis=0, tiled=True)
    mlp_all = mlp_all.reshape(-1, halves, 2 * in_rows, in_cols)

    rows_in = to_clips(after(clips_in, first))
    t_chips = collect(t_first, "shard", hold=(rows_in,))
    t_all = collect(t_chips, "tensor", 2).reshape(-1, t_own.shape[1])
    pulled = to_clips(after(cotangent, rows_in))
    ones, spread_ones = temporal_tables(width, head, frames)

    def one_clip(x, pull, keep_one):
        sizes = dict(frames=frames, scale=scale)
        gain = [norm_gains[i : i + 1] for i in range(3)]
        shift = [norm_shifts[i : i + 1] for i in range(3)]
        wide = [width_bias[i : i + 1] for i in range(3)]
        x = fill(x)
        a_t, qkv_t, probs, o_t, y, x1 = temporal_forward(
            x, gain[0], shift[0], t_all, head_bias[0], wide[0], fc_bias[None], ones, spread_ones,
            **sizes,
        )
        s_all = collect(after(s_first, rows_in), "shard", hold=(x1,))
        s_all = collect(s_all, "tensor", 2).reshape(-1, s_own.shape[1])
        sizes_s = dict(sizes, real=places, head=head)
        a_s, qkv_s, o_s, x2 = spatial_forward(
            x1, gain[1], shift[1], s_all, head_bias[1], wide[1], **sizes_s
        )
        out, g2, db, d_m, d_hidden, sums_m = mlp(
            x2, fill(after(pull, x1)), keep_one.reshape(1, 1), gain[2], shift[2], mlp_all, hidden_bias[None], wide[2]
        )
        back_s = partial(spatial_backward, gain=gain[1], w=s_all, **sizes_s)
        grads_of = partial(weight_grads, halves=halves, rows=own_rows)
        d_m = split_off(share * d_m if share != 1.0 else d_m, "tensor")
        back = send_back(out)
        half = back_s(g2, db, qkv_s, x1, part=0)
        d_m = added(d_m, half[0]).astype(BF)
        tied = after(db, d_m, half[0], *back[1:2])
        d_m = split_off(by_shard(d_m), "shard")
        d_qkv_s, g1, dz, sums_s = back_s(g2, tied, qkv_s, x1, part=1, held=half)
        sums_s = sums_s + half[3]
        tied = after(d_qkv_s, *d_m[1:3], *back[2:3])
        d_s = share * grads_of([(a_s, tied), (db, o_s)], us=12)
        tied = after(dz, d_s, *d_m[3:])
        d_s = split_off(d_s, "tensor")
        dy, do, sums_y = temporal_pull(tied, t_all)
        d_s = added(d_s, dy).astype(BF)
        tied = after(dy, d_s, *back[3:])
        d_s = split_off(by_shard(d_s), "shard")
        d_r = share * grads_of([(tied, o_t), (y, dz)], us=6)
        output = sent_back([after(piece, d_r) for piece in back])
        d_s = added(d_s, d_r).astype(BF)
        d_m = added(d_m, d_r).astype(BF)
        tied = after(do, d_m, d_s, output)
        d_m = shed_at_once(d_m, "context")
        d_s = split_off(d_s, "context")
        d_r = split_off(d_r, "tensor")
        d_qkv_t, sums_q = temporal_backward(tied, qkv_t, probs, ones, spread_ones, **sizes)
        d_s = added(d_s, d_qkv_t)
        d_r = added(d_r, d_qkv_t).astype(BF)
        tied = after(d_qkv_t, d_r, d_s, d_m)
        d_r = split_off(by_shard(d_r), "shard")
        d_q = share * grads_of([(a_t, tied)], us=9)
        d_r = added(d_r, d_q)
        tied, d_q = lax.optimization_barrier((d_qkv_t, d_q, d_r))[:2]
        d_q = split_off(d_q, "tensor")
        into, sums_x = temporal_end(tied, x, g1, gain[0], t_all)
        d_q = added(d_q, into).astype(BF)
        into = from_clips(after(into, d_q))
        small = share * jnp.concatenate(
            (sums_m, sums_s, sums_y + sums_q + sums_x, d_hidden.reshape(-1, width)), axis=0
        )
        d_q = added(split_off(by_shard(d_q), "shard"))
        small = plus_others(plus_others(small, "tensor"), "shard")
        d_r = jnp.concatenate((d_r.astype(BF), d_q.astype(BF)), axis=-1)
        d_r = shed(d_r, "context")
        small = plus_others(after(small, d_q), "context")
        return output, into, (d_r, d_s, d_m, small)

    parts = [one_clip(rows_in[:, i], pulled[:, i], keep[i]) for i in range(clips)]
    output, input_grad = [
        jnp.stack([part[n] for part in parts], axis=1).reshape(clips_in.shape) for n in (0, 1)
    ]
    grads = parts[0][2]
    for part in parts[1:]:
        grads = jax.tree.map(jnp.add, grads, part[2])
    d_t, d_s, d_mlp, small = grads
    d_t_rest, d_t_qkv = d_t[:, : 2 * width], d_t[:, 2 * width :]
    m, s, t = small[0:8], small[8:16], small[16:24]
    return (
        output,
        input_grad,
        jnp.stack((t[0], s[0], m[0])),
        jnp.stack((t[1], s[1], m[1])),
        d_t_qkv.reshape(own_rows, 3, width),
        d_t_rest[:, :width],
        d_t_rest[:, width:],
        d_s[:, : 3 * width].reshape(own_rows, 3, width),
        d_s[:, 3 * width :],
        d_mlp[:in_rows],
        d_mlp[in_rows:],
        jnp.stack((t[2:4], s[2:4])),
        jnp.stack((t[4], m[3], m[2])),
        s[4],
        small[24:].reshape(-1),
    )


def solution(mesh):
    clip = P(("shard", "tensor"), "context", None, None)
    row, block = P(ALL, None), P(("shard", "context"), "tensor")
    deep, whole = P(ALL, None, None), P()
    weights = (deep, row, row, deep, row, block, block)
    in_specs = (clip, P(("shard", "tensor")), whole, whole) + weights + (whole,) * 4 + (clip,)
    out_specs = (clip, clip, whole, whole) + weights + (whole,) * 4
    return jax.shard_map(local, mesh=mesh, in_specs=in_specs, out_specs=out_specs, check_vma=False)
```

```python
from functools import partial

import jax
import jax.numpy as jnp
from jax import lax
from jax.experimental import pallas as pl
from jax.experimental.pallas import tpu as pltpu
from jax.sharding import PartitionSpec as P

HEADS = 12
EPS = 1e-05
ALL = ("shard", "context", "tensor")
BF = jnp.bfloat16
F32 = jnp.float32
VMEM = 60 * 2**20

def mm(left, right, left_dim, right_dim):
    return lax.dot_general(left, right, (((left_dim,), (right_dim,)), ((), ())), preferred_element_type=F32)

def norm_stats(rows):
    centered = rows - jnp.mean(rows, axis=-1, keepdims=True)
    inv = lax.rsqrt(jnp.mean(centered * centered, axis=-1, keepdims=True) + EPS)
    return centered * inv, inv

def mlp_kernel(x_ref, cot_ref, keep_ref, gain_ref, shift_ref, w_ref, hb_ref, wb_ref,
               out_ref, g2_ref, db_ref, dw_ref, dhb_ref, sums_ref,
               a_ref, at_ref, dm_ref, dmt_ref, m_ref, da_ref, h_ref, du_ref, *, rb, chunks):
    step = pl.program_id(0)
    T, D = x_ref.shape
    nb = T // rb
    blocks, _, both, hc = w_ref.shape
    half = both // 2

    @pl.when(step == 0)
    def _():
        def body(i, c):
            r = pl.ds(pl.multiple_of(i * rb, 16), rb)
            unit, _ = norm_stats(x_ref[r, :])
            a = (unit * gain_ref[...] + shift_ref[...]).astype(BF)
            a_ref[r, :] = a
            dm = (keep_ref[0, 0] * cot_ref[r, :].astype(F32)).astype(BF)
            dm_ref[r, :] = dm
            return c
        lax.fori_loop(0, nb, body, 0)
        at_ref[...] = a_ref[...].T
        dmt_ref[...] = dm_ref[...].T

    win = w_ref[:, 0, :half, :].reshape(D, hc)
    wout = w_ref[:, 0, half:, :].reshape(D, hc)
    hb = hb_ref[...]
    tot = jnp.zeros((1, hc), F32)
    for i in range(nb):
        r = slice(i * rb, (i + 1) * rb)
        u = mm(a_ref[r, :], win, 1, 0) + hb
        cdf = 0.5 * (1.0 + lax.erf(u * (2 ** -0.5)))
        h = (u * cdf).astype(BF)
        pdf = jnp.exp(-0.5 * u * u) * ((2 * jnp.pi) ** -0.5)
        dh = mm(dm_ref[r, :], wout, 1, 0)
        du = ((cdf + u * pdf) * dh).astype(BF)
        h_ref[r, :] = h
        du_ref[r, :] = du
        tot += jnp.sum(du.astype(F32), axis=0, keepdims=True)
        m = mm(h, wout, 1, 1)
        da = mm(du, win, 1, 1)
        @pl.when(step == 0)
        def _():
            m_ref[r, :] = m
            da_ref[r, :] = da
        @pl.when(step > 0)
        def _():
            m_ref[r, :] += m
            da_ref[r, :] += da
    dhb_ref[...] = tot
    dw_ref[0, :, :half, :] = mm(at_ref[...], du_ref[...], 1, 0).astype(BF).reshape(blocks, half, hc)
    dw_ref[0, :, half:, :] = mm(dmt_ref[...], h_ref[...], 1, 0).astype(BF).reshape(blocks, half, hc)

    @pl.when(step == chunks - 1)
    def _():
        k = keep_ref[0, 0]
        def body(i, c):
            r = pl.ds(pl.multiple_of(i * rb, 16), rb)
            x = x_ref[r, :]
            out_ref[r, :] = (k * (x + (m_ref[r, :] + wb_ref[...]))).astype(BF)
            g3 = k * cot_ref[r, :].astype(F32)
            da = da_ref[r, :]
            unit, inv = norm_stats(x)
            sc = da * gain_ref[...]
            into = inv * (sc - jnp.mean(sc, axis=-1, keepdims=True) - unit * jnp.mean(sc * unit, axis=-1, keepdims=True))
            g2 = g3 + into
            g2_ref[r, :] = g2
            low = g2.astype(BF)
            db_ref[r, :] = low
            return (c[0] + jnp.sum(da * unit, axis=0, keepdims=True),
                    c[1] + jnp.sum(da, axis=0, keepdims=True),
                    c[2] + jnp.sum(dm_ref[r, :].astype(F32), axis=0, keepdims=True),
                    c[3] + jnp.sum(low.astype(F32), axis=0, keepdims=True))
        z = jnp.zeros((1, D), F32)
        c = lax.fori_loop(0, nb, body, (z, z, z, z))
        for j in range(4):
            sums_ref[j:j+1, :] = c[j]

def mlp(x2, cot, keep, gain, shift, w4, hb, wb):
    T, D = x2.shape
    B, H2, R, C = w4.shape
    rb = T // 4 if T % 64 == 0 else T
    hc = next(w for w in (768, 512, 384, 256, 128) if C % w == 0)
    per = C // hc
    chunks = H2 * per
    full = lambda *s: pl.BlockSpec(s, lambda j: (0,) * len(s), pipeline_mode=pl.Buffered(1))
    wspec = pl.BlockSpec((B, 1, R, hc), lambda j: (0, j // per, 0, j % per))
    dspec = pl.BlockSpec((1, B, R, hc), lambda j: (j // per, 0, 0, j % per))
    hspec = pl.BlockSpec((1, hc), lambda j: (0, j))
    return pl.pallas_call(
        partial(mlp_kernel, rb=rb, chunks=chunks),
        grid=(chunks,),
        in_specs=[full(T, D), full(T, D), pl.BlockSpec(memory_space=pltpu.SMEM), full(1, D), full(1, D), wspec, hspec, full(1, D)],
        out_specs=[full(T, D), full(T, D), full(T, D), dspec, hspec, full(8, D)],
        out_shape=(sds(T, D), sds(T, D, t=F32), sds(T, D), sds(H2, B, R, C), sds(1, H2 * C, t=F32), sds(8, D, t=F32)),
        scratch_shapes=[pltpu.VMEM((T, D), BF), pltpu.VMEM((D, T), BF), pltpu.VMEM((T, D), BF), pltpu.VMEM((D, T), BF),
                        pltpu.VMEM((T, D), F32), pltpu.VMEM((T, D), F32), pltpu.VMEM((T, hc), BF), pltpu.VMEM((T, hc), BF)],
        compiler_params=pltpu.CompilerParams(vmem_limit_bytes=VMEM),
        cost_estimate=cost(75),
    )(x2, cot, keep, gain, shift, w4, hb, wb)
LANES = 128
LOW = -1e30

def once(*s):
    return pl.BlockSpec(s, lambda j: (0,) * len(s), pipeline_mode=pl.Buffered(1))

def column(rows, cols, at):
    return pl.BlockSpec((rows, cols), lambda j: (0, at), pipeline_mode=pl.Buffered(1))

def sds(*s, t=BF):
    return jax.ShapeDtypeStruct(s, t)

def cost(us):
    return pl.CostEstimate(flops=us * 10**9, bytes_accessed=0, transcendentals=0)

def call(body, us, grid, ins, outs, shapes, scratch=()):
    return pl.pallas_call(body, grid=(grid,), in_specs=ins, out_specs=outs, out_shape=shapes, scratch_shapes=list(scratch),
                          compiler_params=pltpu.CompilerParams(vmem_limit_bytes=VMEM), cost_estimate=cost(us))

def qkv_store(a, wqkv, hb_ref, dst, rows, D):
    packed = mm(a, wqkv, 1, 0)
    dst[rows, :D] = (packed[:, :D] + hb_ref[0:1, :]).astype(BF)
    dst[rows, D:2 * D] = packed[:, D:2 * D].astype(BF)
    dst[rows, 2 * D:] = (packed[:, 2 * D:] + hb_ref[1:2, :]).astype(BF)

def lane_masks(head, value):
    lane = lax.broadcasted_iota(jnp.int32, (1, LANES), 1)
    return [jnp.where(lane // head == i, value, 0.0).astype(BF) for i in range(LANES // head)]

def sf_kernel(x_ref, gain_ref, shift_ref, wqkv_ref, wproj_ref, hb_ref, wb_ref, a_ref, qkv_ref, o_ref, x2_ref, *, fb, real, head, scale):
    M, D = x_ref.shape
    P = M // fb
    unit, _ = norm_stats(x_ref[...])
    a = (unit * gain_ref[...] + shift_ref[...]).astype(BF)
    a_ref[...] = a
    qkv_store(a, wqkv_ref[...], hb_ref, qkv_ref, slice(0, M), D)
    col = lax.broadcasted_iota(jnp.int32, (1, P), 1)
    hide = jnp.where(col < real, 0.0, LOW)
    ones = lane_masks(head, 1.0)
    for f in range(fb):
        r = slice(f * P, (f + 1) * P)
        for j in range(D // LANES):
            q = qkv_ref[r, j * LANES:(j + 1) * LANES]
            k = qkv_ref[r, D + j * LANES:D + (j + 1) * LANES]
            v = qkv_ref[r, 2 * D + j * LANES:2 * D + (j + 1) * LANES]
            o = None
            for m in ones:
                s = mm(q * m, k, 1, 1) * scale + hide
                p = jnp.exp(s - jnp.max(s, axis=-1, keepdims=True))
                p = (p * (1.0 / jnp.sum(p, axis=-1, keepdims=True))).astype(BF)
                part = mm(p, v * m, 1, 0)
                o = part if o is None else o + part
            o_ref[r, j * LANES:(j + 1) * LANES] = o.astype(BF)
    x2_ref[...] = x_ref[...] + (mm(o_ref[...], wproj_ref[...], 1, 1) + wb_ref[...])

def spatial_forward(x1, gain, shift, w, hb, wb, *, frames, real, head, scale, fb=2):
    T, D = x1.shape
    M = T // frames * fb
    blk = lambda w: pl.BlockSpec((M, w), lambda j: (j, 0))
    return call(partial(sf_kernel, fb=fb, real=real, head=head, scale=scale), 30, frames // fb,
        [blk(D), once(1, D), once(1, D), column(D, 3 * D, 0), column(D, D, 3), once(2, D), once(1, D)],
        [blk(D), blk(3 * D), blk(D), blk(D)], (sds(T, D), sds(T, 3 * D), sds(T, D), sds(T, D, t=F32)))(
        x1, gain, shift, w, w, hb, wb)

def norm_back_store(x, gain, da, base, sums_ref, at):
    unit, inv = norm_stats(x)
    sc = da * gain
    into = inv * (sc - jnp.mean(sc, axis=-1, keepdims=True) - unit * jnp.mean(sc * unit, axis=-1, keepdims=True))
    sums_ref[at:at + 1, :] += jnp.sum(da * unit, axis=0, keepdims=True)
    sums_ref[at + 1:at + 2, :] += jnp.sum(da, axis=0, keepdims=True)
    return base + into

def add_sum(sums_ref, at, rows):
    sums_ref[at:at + 1, :] += jnp.sum(rows.astype(F32), axis=0, keepdims=True)

def sb_kernel(g2_ref, db_ref, qkv_ref, x_ref, gain_ref, wqkv_ref, wproj_ref, *rest, fb, real, head, scale):
    dqkv_ref, g1_ref, dz_ref, sums_ref, do_ref = rest[-5:]
    M, D = x_ref.shape
    P = M // fb
    @pl.when(pl.program_id(0) == 0)
    def _():
        sums_ref[...] = jnp.zeros_like(sums_ref)
    do_ref[...] = mm(db_ref[...], wproj_ref[...], 1, 0).astype(BF)
    row = lax.broadcasted_iota(jnp.int32, (P, 1), 0)
    hide = jnp.where(row < real, 0.0, LOW)
    ones = lane_masks(head, 1.0)
    for f in range(fb):
        r = slice(f * P, (f + 1) * P)
        for j in range(D // LANES):
            ls = [slice(i * D + j * LANES, i * D + (j + 1) * LANES) for i in range(3)]
            q, k, v = [qkv_ref[r, l] for l in ls]
            do = do_ref[r, ls[0]]
            dq = dk = dv = 0.0
            for m in ones:
                qm = q * m
                dom = do * m
                s = mm(k, qm, 1, 1) * scale + hide
                p = jnp.exp(s - jnp.max(s, axis=0, keepdims=True))
                p = p * (1.0 / jnp.sum(p, axis=0, keepdims=True))
                dp = mm(v, dom, 1, 1)
                ds = (p * (dp - jnp.sum(p * dp, axis=0, keepdims=True))).astype(BF)
                dv = dv + mm(p.astype(BF), dom, 1, 0)
                dk = dk + mm(ds, qm, 1, 0)
                dq = dq + mm(ds, k * m, 0, 0)
            dqkv_ref[r, ls[0]] = (dq * scale).astype(BF)
            dqkv_ref[r, ls[1]] = (dk * scale).astype(BF)
            dqkv_ref[r, ls[2]] = dv.astype(BF)
    add_sum(sums_ref, 2, dqkv_ref[:, :D])
    add_sum(sums_ref, 3, dqkv_ref[:, 2 * D:])
    da = mm(dqkv_ref[...], wqkv_ref[...], 1, 1)
    g1 = norm_back_store(x_ref[...], gain_ref[...], da, g2_ref[...], sums_ref, 0)
    g1_ref[...] = g1
    low = g1.astype(BF)
    dz_ref[...] = low
    add_sum(sums_ref, 4, low)

def spatial_backward(g2, db, qkv, x1, *, gain, w, frames, real, head, scale, part, held=None, fb=2):
    T, D = x1.shape
    M = T // frames * fb
    nb = frames // fb // 2
    blk = lambda w: pl.BlockSpec((M, w), lambda j: (j + part * nb, 0))
    kept = [] if held is None else list(held[:3])
    return pl.pallas_call(
        partial(sb_kernel, fb=fb, real=real, head=head, scale=scale), grid=(nb,),
        in_specs=[blk(D), blk(D), blk(3 * D), blk(D), once(1, D), column(D, 3 * D, 0), column(D, D, 3)]
        + [pl.BlockSpec(memory_space=pl.ANY)] * len(kept),
        out_specs=[blk(3 * D), blk(D), blk(D), once(8, D)],
        out_shape=(sds(T, 3 * D), sds(T, D, t=F32), sds(T, D), sds(8, D, t=F32)),
        scratch_shapes=[pltpu.VMEM((M, D), BF)],
        input_output_aliases={7 + i: i for i in range(len(kept))},
        compiler_params=pltpu.CompilerParams(vmem_limit_bytes=VMEM), cost_estimate=cost(24),
    )(g2, db, qkv, x1, gain, w, w, *kept)

def over_frames(op, rows, slot):
    shift = slot
    while shift < LANES:
        rows = op(rows, pltpu.roll(rows, shift, 1))
        shift *= 2
    return rows

def tf_kernel(x_ref, gain_ref, shift_ref, wqkv_ref, wproj_ref, wfc_ref, hb_ref, wb_ref, fcb_ref,
              a_ref, qkv_ref, p_ref, o_ref, y_ref, x1_ref, all_ref, prod_ref, xs_ref, e_ref, b_ref, *, fb, nb, frames, slot, head, scale):
    M, D = x_ref.shape
    P = M // fb
    step = pl.program_id(0)
    @pl.when(step == 0)
    def _():
        fill_tables(e_ref, b_ref, slot, head)
    @pl.when(step < nb)
    def _():
        x = x_ref[...].astype(F32)
        unit, _ = norm_stats(x)
        a = (unit * gain_ref[...] + shift_ref[...]).astype(BF)
        a_ref[...] = a
        qkv_store(a, wqkv_ref[...], hb_ref, qkv_ref, slice(0, M), D)
        all_ref[pl.ds(pl.multiple_of(step * M, M), M), :] = qkv_ref[...]
        xs_ref[pl.ds(pl.multiple_of(step * M, M), M), :] = x_ref[...]
    @pl.when(step >= nb)
    def _():
        base = pl.multiple_of((step - nb) * M, M)
        for f in range(fb):
            q = all_ref[pl.ds(base + f * P, P), :D]
            for g in range(frames):
                prod_ref[f * P:(f + 1) * P, g * D:(g + 1) * D] = q * all_ref[g * P:(g + 1) * P, D:2 * D]
        s = mm(prod_ref[...], e_ref[...], 1, 0) * scale
        p = jnp.exp(s - over_frames(jnp.maximum, s, slot))
        p = p * (1.0 / over_frames(jnp.add, p, slot))
        p_ref[...] = p
        low = p.astype(BF)
        o = [None] * fb
        for g in range(frames):
            wide = mm(low, b_ref[:, g * D:(g + 1) * D], 1, 0)
            v = all_ref[g * P:(g + 1) * P, 2 * D:].astype(F32)
            for f in range(fb):
                part = wide[f * P:(f + 1) * P] * v
                o[f] = part if g == 0 else o[f] + part
        for f in range(fb):
            o_ref[f * P:(f + 1) * P, :] = o[f].astype(BF)
        y = (mm(o_ref[...], wproj_ref[...], 1, 1) + wb_ref[...]).astype(BF)
        y_ref[...] = y
        z = (mm(y, wfc_ref[...], 1, 0) + fcb_ref[...]).astype(BF)
        x1_ref[...] = xs_ref[pl.ds(base, M), :].astype(F32) + z.astype(F32)

def fill_tables(e_ref, b_ref, slot, head):
    D = e_ref.shape[0] * slot // LANES
    for g in range(LANES // slot):
        for ref, at, wide in ((e_ref, 1, 0), (b_ref, 0, 1)):
            shape = (D, LANES) if wide == 0 else (LANES, D)
            lane = lax.broadcasted_iota(jnp.int32, shape, at)
            feature = lax.broadcasted_iota(jnp.int32, shape, wide)
            hit = ((lane // slot == g) & (lane % slot == feature // head)).astype(F32).astype(BF)
            if wide == 0:
                ref[g * D:(g + 1) * D, :] = hit
            else:
                ref[:, g * D:(g + 1) * D] = hit

def temporal_forward(x, gain, shift, w, hb, wb, fcb, *, frames, head, scale, fb=2):
    T, D = x.shape
    M = T // frames * fb
    nb = frames // fb
    first = lambda w: pl.BlockSpec((M, w), lambda j: (jnp.minimum(j, nb - 1), 0))
    last = lambda w: pl.BlockSpec((M, w), lambda j: (jnp.maximum(j - nb, 0), 0))
    return call(partial(tf_kernel, fb=fb, nb=nb, frames=frames, slot=LANES // frames, head=head, scale=scale), 44, 2 * nb,
        [first(D), once(1, D), once(1, D), column(D, 3 * D, 0), column(D, D, 3), column(D, D, 4), once(2, D), once(1, D), once(1, D)],
        [first(D), first(3 * D), last(LANES), last(D), last(D), last(D)],
        (sds(T, D), sds(T, 3 * D), sds(T, LANES, t=F32), sds(T, D), sds(T, D), sds(T, D, t=F32)),
        [pltpu.VMEM((T, 3 * D), BF), pltpu.VMEM((M, frames * D), BF), pltpu.VMEM((T, D), BF),
         pltpu.VMEM((frames * D, LANES), BF), pltpu.VMEM((LANES, frames * D), BF)])(
        x, gain, shift, w, w, w, hb, wb, fcb)

def zero_first(*refs):
    @pl.when(pl.program_id(0) == 0)
    def _():
        for ref in refs:
            ref[...] = jnp.zeros_like(ref)

def pull_kernel(dz_ref, wproj_ref, wfc_ref, dy_ref, do_ref, sums_ref):
    zero_first(sums_ref)
    dy = mm(dz_ref[...], wfc_ref[...], 1, 1).astype(BF)
    dy_ref[...] = dy
    add_sum(sums_ref, 4, dy)
    do_ref[...] = mm(dy, wproj_ref[...], 1, 0).astype(BF)

def temporal_pull(dz, w, *, blocks=4):
    T, D = dz.shape
    blk = pl.BlockSpec((T // blocks, D), lambda j: (j, 0))
    return call(pull_kernel, 8, blocks, [blk, column(D, D, 3), column(D, D, 4)], [blk, blk, once(8, D)],
                (sds(T, D), sds(T, D), sds(8, D, t=F32)))(dz, w, w)

def tb_kernel(do_ref, qkv_ref, p_ref, dqkv_ref, sums_ref, dk_ref, dv_ref, prod_ref, e_ref, b_ref, *, fb, nb, frames, slot, head, scale):
    M = p_ref.shape[0]
    T, D = do_ref.shape
    P = M // fb
    step = pl.program_id(0)
    zero_first(sums_ref, dk_ref, dv_ref)
    @pl.when(step == 0)
    def _():
        fill_tables(e_ref, b_ref, slot, head)
    base = pl.multiple_of(step * M, M)
    for f in range(fb):
        do = do_ref[pl.ds(base + f * P, P), :]
        for g in range(frames):
            prod_ref[f * P:(f + 1) * P, g * D:(g + 1) * D] = do * qkv_ref[g * P:(g + 1) * P, 2 * D:]
    dp = mm(prod_ref[...], e_ref[...], 1, 0)
    p = p_ref[...]
    ds = (p * (dp - over_frames(jnp.add, p * dp, slot))).astype(BF)
    low = p.astype(BF)
    dq = [0.0] * fb
    for g in range(frames):
        gr = slice(g * P, (g + 1) * P)
        wide_p = mm(low, b_ref[:, g * D:(g + 1) * D], 1, 0)
        wide_s = mm(ds, b_ref[:, g * D:(g + 1) * D], 1, 0)
        k = qkv_ref[gr, D:2 * D].astype(F32)
        dk, dv = dk_ref[gr, :], dv_ref[gr, :]
        for f in range(fb):
            fr = pl.ds(base + f * P, P)
            wp, ws = wide_p[f * P:(f + 1) * P], wide_s[f * P:(f + 1) * P]
            dv = dv + wp * do_ref[fr, :].astype(F32)
            dk = dk + ws * qkv_ref[fr, :D].astype(F32)
            dq[f] = dq[f] + ws * k
        dk_ref[gr, :] = dk
        dv_ref[gr, :] = dv
    for f in range(fb):
        low = (dq[f] * scale).astype(BF)
        add_sum(sums_ref, 2, low)
        dqkv_ref[pl.ds(base + f * P, P), :D] = low
    @pl.when(step == nb - 1)
    def _():
        for g in range(frames):
            gr = slice(g * P, (g + 1) * P)
            dqkv_ref[gr, D:2 * D] = (dk_ref[gr, :] * scale).astype(BF)
            low = dv_ref[gr, :].astype(BF)
            add_sum(sums_ref, 3, low)
            dqkv_ref[gr, 2 * D:] = low

def temporal_backward(do, qkv, p, *, frames, head, scale, fb=2):
    T, D = do.shape
    M = T // frames * fb
    nb = frames // fb
    return call(partial(tb_kernel, fb=fb, nb=nb, frames=frames, slot=LANES // frames, head=head, scale=scale), 40, nb,
        [once(T, D), once(T, 3 * D), pl.BlockSpec((M, LANES), lambda j: (j, 0))],
        [once(T, 3 * D), once(8, D)], (sds(T, 3 * D), sds(8, D, t=F32)),
        [pltpu.VMEM((T, D), F32), pltpu.VMEM((T, D), F32), pltpu.VMEM((M, frames * D), BF),
         pltpu.VMEM((frames * D, LANES), BF), pltpu.VMEM((LANES, frames * D), BF)])(do, qkv, p)

def end_kernel(dqkv_ref, x_ref, g1_ref, gain_ref, wqkv_ref, out_ref, sums_ref):
    zero_first(sums_ref)
    da = mm(dqkv_ref[...], wqkv_ref[...], 1, 1)
    out = norm_back_store(x_ref[...].astype(F32), gain_ref[...], da, g1_ref[...], sums_ref, 0)
    out_ref[...] = out.astype(BF)

def temporal_end(dqkv, x, g1, gain, w, *, blocks=4):
    T, D = x.shape
    blk = lambda w: pl.BlockSpec((T // blocks, w), lambda j: (j, 0))
    return call(end_kernel, 12, blocks, [blk(3 * D), blk(D), blk(D), once(1, D), column(D, 3 * D, 0)], [blk(D), once(8, D)],
                (sds(T, D), sds(8, D, t=F32)))(dqkv, x, g1, gain, w)

def wg_kernel(*refs, starts, halves, rows):
    n = len(starts)
    a_refs, b_refs, out_ref, t_ref = refs[:n], refs[n:2 * n], refs[2 * n], refs[2 * n + 1]
    step = pl.program_id(0)
    for i in range(n):
        @pl.when(step == starts[i])
        def _():
            t_ref[...] = a_refs[i][...].T
        stop = starts[i + 1] if i + 1 < n else step + 1
        @pl.when((step >= starts[i]) & (step < stop))
        def _():
            res = mm(t_ref[...], b_refs[i][...], 1, 0)
            if rows:
                parts = res.reshape(-1, halves, rows, res.shape[-1])
                for h in range(halves):
                    out_ref[h] = parts[:, h].reshape(-1, res.shape[-1]).astype(BF)
            else:
                out_ref[0] = res.astype(BF)

def weight_grads(pairs, halves, rows, us):
    T, D = pairs[0][0].shape
    starts, steps = [], 0
    for a, b in pairs:
        starts.append(steps)
        steps += b.shape[1] // D
    cols = steps * D
    fits = rows % 8 == 0
    def chunk(i):
        many = pairs[i][1].shape[1] // D
        return pl.BlockSpec((T, D), lambda j: (0, jnp.clip(j - starts[i], 0, many - 1)))
    groups = halves if fits else 1
    out = call(partial(wg_kernel, starts=starts, halves=halves, rows=rows if fits else 0), us, steps,
        [once(T, D)] * len(pairs) + [chunk(i) for i in range(len(pairs))],
        [pl.BlockSpec((groups, D // groups, D), lambda j: (0, 0, j))], (sds(groups, D // groups, cols),),
        [pltpu.VMEM((D, T), BF)])(*[a for a, _ in pairs], *[b for _, b in pairs])[0]
    if fits:
        return out.reshape(halves, -1, rows, cols)
    return jnp.swapaxes(out.reshape(-1, halves, rows, cols), 0, 1)


def exchange(pieces, axis):
    size = len(pieces)
    return [pieces[0]] + [
        lax.ppermute(pieces[d], axis, [(i, i ^ d) for i in range(size)]) for d in range(1, size)
    ]


def in_order(pieces, axis, step=1):
    while step < len(pieces):
        swap = (lax.axis_index(axis) // step) % 2 == 1
        pieces = [jnp.where(swap, pieces[c ^ step], pieces[c]) for c in range(len(pieces))]
        step *= 2
    return pieces


def collect(array, axis, at=0, hold=()):
    pieces = exchange([array] * lax.axis_size(axis), axis)
    pieces = pieces[:1] + [after(piece, *hold) for piece in pieces[1:]]
    return jnp.stack(in_order(pieces, axis), axis=at)


def partner(array, axis, step):
    size = lax.axis_size(axis)
    return lax.ppermute(array, axis, [(i, i ^ step) for i in range(size)])


def far_first(array, axis):
    size = lax.axis_size(axis)
    step = size // 2
    out = array[None]
    while step:
        other = partner(out, axis, step)
        low = (lax.axis_index(axis) // step) % 2 == 0
        out = jnp.stack((jnp.where(low, out, other), jnp.where(low, other, out)), axis=1)
        out = out.reshape((-1,) + array.shape)
        step //= 2
    return out


def near_first(array, axis):
    size = lax.axis_size(axis)
    step = 1
    while step < size:
        blocks = array.reshape((-1, 2) + array.shape[1:])
        mine = (lax.axis_index(axis) // step) % 2
        send = lax.dynamic_index_in_dim(blocks, 1 - mine, 1, keepdims=False).astype(BF)
        keep = lax.dynamic_index_in_dim(blocks, mine, 1, keepdims=False)
        array = keep.astype(F32) + partner(send, axis, step).astype(F32)
        step *= 2
    return array[0]


def split_off(array, axis):
    place = lax.axis_index(axis)
    pieces = [
        lax.dynamic_index_in_dim(array, place ^ d, 0, keepdims=False)
        for d in range(lax.axis_size(axis))
    ]
    return exchange(pieces[:1] + [piece.astype(BF) for piece in pieces[1:]], axis)


def added(pieces, *hold):
    out = pieces[0].astype(F32)
    for piece in pieces[1:]:
        out = out + after(piece, *hold).astype(F32)
    return out


def shed(array, axis, hold=()):
    return added(split_off(array, axis), *hold)


def shed_at_once(array, axis, *hold):
    came = lax.all_to_all(array.astype(BF), axis, split_axis=0, concat_axis=0, tiled=True)
    came = after(came, *hold)
    return jnp.sum(came.astype(F32), axis=0)


def after(array, *others):
    return lax.optimization_barrier((array,) + others)[0]


def plus_others(array, axis):
    came = exchange([array] * lax.axis_size(axis), axis)
    return sum(came[1:], came[0])


def local(
    clips_in,
    valid_clips,
    norm_gains,
    norm_shifts,
    temporal_qkv,
    temporal_proj,
    temporal_fc,
    spatial_qkv,
    spatial_proj,
    mlp_in,
    mlp_out,
    head_bias,
    width_bias,
    fc_bias,
    hidden_bias,
    cotangent,
):
    held, frames_held, places, width = clips_in.shape
    head = width // HEADS
    scale = head ** (-0.5)
    across = lax.axis_size("context")
    halves = lax.axis_size("tensor")
    place = lax.axis_index("context")
    own_rows = temporal_qkv.shape[0]
    in_rows, in_cols = mlp_in.shape
    spread = held % across == 0
    clips = held // across if spread else held
    share = 1.0 if spread else 1.0 / across
    frames = frames_held * across
    padded = -(-places // 16) * 16

    def to_clips(array):
        array = jnp.swapaxes(array, 1, 2)
        if spread:
            array = lax.all_to_all(array, "context", split_axis=0, concat_axis=0, tiled=True)
            return array.reshape((across, clips) + array.shape[1:])
        return lax.all_gather(array, "context", axis=0)

    def fill(array):
        array = jnp.swapaxes(array, 1, 2).reshape(frames, places, width)
        array = jnp.pad(array, ((0, 0), (0, padded - places), (0, 0)))
        return array.reshape(frames * padded, width)

    def by_place(array):
        array = array.reshape(across, frames_held, padded, width)[:, :, :places]
        return jnp.swapaxes(array, 1, 2)

    def from_clips(array):
        if spread:
            array = lax.all_to_all(array, "context", split_axis=0, concat_axis=0, tiled=True)
        else:
            array = lax.dynamic_slice_in_dim(array, place, 1, 0)
        return jnp.swapaxes(array, 1, 2)

    def send_back(array):
        array = by_place(array)
        if spread:
            return split_off(array, "context")
        return [lax.dynamic_index_in_dim(array, place, 0, keepdims=False)]

    def sent_back(pieces):
        return jnp.swapaxes(jnp.stack(in_order(pieces, "context")), 1, 2)

    if spread:
        valid = lax.dynamic_slice_in_dim(valid_clips, place * clips, clips, 0)
    else:
        valid = valid_clips
    keep = valid.astype(F32)

    def flat3(weight):
        return weight.reshape(own_rows, 3 * width)

    def by_shard(d):
        return d.reshape((lax.axis_size("shard"), across) + d.shape[1:])

    t_own = jnp.concatenate((flat3(temporal_qkv), temporal_proj, temporal_fc), axis=1).astype(BF)
    s_own = jnp.concatenate((flat3(spatial_qkv), spatial_proj), axis=1).astype(BF)
    mlp_own = jnp.concatenate((mlp_in, mlp_out), axis=0).astype(BF)
    first = collect(jnp.concatenate((t_own, s_own), axis=1), "context")
    t_first, s_first = first[..., : t_own.shape[1]], first[..., t_own.shape[1] :]
    mlp_all = lax.all_gather(after(mlp_own, first), ALL, axis=0, tiled=True)
    mlp_all = mlp_all.reshape(-1, halves, 2 * in_rows, in_cols)

    rows_in = to_clips(after(clips_in, first))
    t_chips = collect(t_first, "shard", hold=(rows_in,))
    t_all = collect(t_chips, "tensor", 2).reshape(-1, t_own.shape[1])
    pulled = to_clips(after(cotangent, rows_in))

    def one_clip(x, pull, keep_one):
        sizes = dict(frames=frames, head=head, scale=scale)
        gain = [norm_gains[i : i + 1] for i in range(3)]
        shift = [norm_shifts[i : i + 1] for i in range(3)]
        wide = [width_bias[i : i + 1] for i in range(3)]
        x = fill(x)
        a_t, qkv_t, probs, o_t, y, x1 = temporal_forward(
            x, gain[0], shift[0], t_all, head_bias[0], wide[0], fc_bias[None], **sizes,
        )
        s_all = collect(after(s_first, rows_in), "shard", hold=(x1,))
        s_all = collect(s_all, "tensor", 2).reshape(-1, s_own.shape[1])
        sizes_s = dict(sizes, real=places)
        a_s, qkv_s, o_s, x2 = spatial_forward(
            x1, gain[1], shift[1], s_all, head_bias[1], wide[1], **sizes_s
        )
        out, g2, db, d_m, d_hidden, sums_m = mlp(
            x2, fill(after(pull, x1)), keep_one.reshape(1, 1), gain[2], shift[2], mlp_all, hidden_bias[None], wide[2]
        )
        back_s = partial(spatial_backward, gain=gain[1], w=s_all, **sizes_s)
        grads_of = partial(weight_grads, halves=halves, rows=own_rows)
        d_m = split_off(share * d_m if share != 1.0 else d_m, "tensor")
        back = send_back(out)
        half = back_s(g2, db, qkv_s, x1, part=0)
        d_m = added(d_m, half[0]).astype(BF)
        tied = after(db, d_m, half[0], *back[1:2])
        d_m = split_off(by_shard(d_m), "shard")
        d_qkv_s, g1, dz, sums_s = back_s(g2, tied, qkv_s, x1, part=1, held=half)
        sums_s = sums_s + half[3]
        tied = after(d_qkv_s, *d_m[1:3], *back[2:3])
        d_s = share * grads_of([(a_s, tied), (db, o_s)], us=12)
        tied = after(dz, d_s)
        d_s = split_off(d_s, "tensor")
        dy, do, sums_y = temporal_pull(tied, t_all)
        d_s = added(d_s, dy).astype(BF)
        tied = after(dy, d_s, *back[3:], *d_m[3:])
        d_s = split_off(by_shard(d_s), "shard")
        d_r = share * grads_of([(tied, o_t), (y, dz)], us=6)
        d_m = added(d_m, d_r).astype(BF)
        tied = after(do, d_m, d_r)
        d_m = lax.all_to_all(d_m, "context", split_axis=0, concat_axis=0, tiled=True)
        d_r = split_off(d_r, "tensor")
        d_qkv_t, sums_q = temporal_backward(tied, qkv_t, probs, **sizes)
        d_m = jnp.sum(after(d_m, d_qkv_t).astype(F32), axis=0)
        d_s = added(d_s, d_qkv_t).astype(BF)
        d_r = added(d_r, d_qkv_t).astype(BF)
        tied = after(d_qkv_t, d_r, d_s, d_m)
        d_r = split_off(by_shard(d_r), "shard")
        d_q = share * grads_of([(a_t, tied)], us=9)
        d_r = added(d_r, d_q).astype(BF)
        d_s = shed_at_once(d_s, "context", d_q)
        tied, d_q, d_r, d_s = lax.optimization_barrier((d_qkv_t, d_q, d_r, d_s))
        d_q = split_off(d_q, "tensor")
        d_r = split_off(d_r, "context")
        into, sums_x = temporal_end(tied, x, g1, gain[0], t_all)
        d_r = added(d_r, into)
        swapped = after(by_place(into), d_r)
        into = from_clips(swapped)
        output = sent_back([after(piece, swapped) for piece in back])
        small = share * jnp.concatenate(
            (sums_m, sums_s, sums_y + sums_q + sums_x, d_hidden.reshape(-1, width)), axis=0
        )
        d_q = added(d_q, swapped).astype(BF)
        small = plus_others(small, "tensor")
        d_q = added(split_off(by_shard(after(d_q, small)), "shard")).astype(BF)
        small = plus_others(after(small, d_q), "shard")
        d_q = shed(after(d_q, small), "context")
        small = plus_others(small, "context")
        return output, into, (d_q, d_r, d_s, d_m, small)

    parts = [one_clip(rows_in[:, i], pulled[:, i], keep[i]) for i in range(clips)]
    output, input_grad = [
        jnp.stack([part[n] for part in parts], axis=1).reshape(clips_in.shape) for n in (0, 1)
    ]
    grads = parts[0][2]
    for part in parts[1:]:
        grads = jax.tree.map(jnp.add, grads, part[2])
    d_t_qkv, d_t_rest, d_s, d_mlp, small = grads
    m, s, t = small[0:8], small[8:16], small[16:24]
    return (
        output,
        input_grad,
        jnp.stack((t[0], s[0], m[0])),
        jnp.stack((t[1], s[1], m[1])),
        d_t_qkv.reshape(own_rows, 3, width),
        d_t_rest[:, :width],
        d_t_rest[:, width:],
        d_s[:, : 3 * width].reshape(own_rows, 3, width),
        d_s[:, 3 * width :],
        d_mlp[:in_rows],
        d_mlp[in_rows:],
        jnp.stack((t[2:4], s[2:4])),
        jnp.stack((t[4], m[3], m[2])),
        s[4],
        small[24:].reshape(-1),
    )


def solution(mesh):
    clip = P(("shard", "tensor"), "context", None, None)
    row, block = P(ALL, None), P(("shard", "context"), "tensor")
    deep, whole = P(ALL, None, None), P()
    weights = (deep, row, row, deep, row, block, block)
    in_specs = (clip, P(("shard", "tensor")), whole, whole) + weights + (whole,) * 4 + (clip,)
    out_specs = (clip, clip, whole, whole) + weights + (whole,) * 4
    return jax.shard_map(local, mesh=mesh, in_specs=in_specs, out_specs=out_specs, check_vma=False)
```

```python
from functools import partial

import jax
import jax.numpy as jnp
from jax import lax
from jax.experimental import pallas as pl
from jax.experimental.pallas import tpu as pltpu
from jax.sharding import PartitionSpec as P

HEADS = 12
EPS = 1e-05
ALL = ("shard", "context", "tensor")
BF = jnp.bfloat16
F32 = jnp.float32
VMEM = 60 * 2**20

def mm(left, right, left_dim, right_dim):
    return lax.dot_general(left, right, (((left_dim,), (right_dim,)), ((), ())), preferred_element_type=F32)

def norm_stats(rows):
    centered = rows - jnp.mean(rows, axis=-1, keepdims=True)
    inv = lax.rsqrt(jnp.mean(centered * centered, axis=-1, keepdims=True) + EPS)
    return centered * inv, inv

def mlp_kernel(x_ref, cota_ref, cotb_ref, keep_ref, gain_ref, shift_ref, w_ref, hb_ref, wb_ref,
               out_ref, g2_ref, db_ref, dw_ref, dhb_ref, sums_ref,
               a_ref, at_ref, dm_ref, dmt_ref, m_ref, da_ref, h_ref, du_ref, *, rb, chunks, frames):
    step = pl.program_id(0)
    T, D = x_ref.shape
    cot_ref = out_ref
    nb = T // rb
    blocks, _, both, hc = w_ref.shape
    half = both // 2

    @pl.when(step == 0)
    def _():
        merge(cot_ref, (cota_ref, cotb_ref), frames)
        def body(i, c):
            r = pl.ds(pl.multiple_of(i * rb, 16), rb)
            unit, _ = norm_stats(x_ref[r, :])
            a = (unit * gain_ref[...] + shift_ref[...]).astype(BF)
            a_ref[r, :] = a
            dm = (keep_ref[0, 0] * cot_ref[r, :].astype(F32)).astype(BF)
            dm_ref[r, :] = dm
            return c
        lax.fori_loop(0, nb, body, 0)
        at_ref[...] = a_ref[...].T
        dmt_ref[...] = dm_ref[...].T

    win = w_ref[:, 0, :half, :].reshape(D, hc)
    wout = w_ref[:, 0, half:, :].reshape(D, hc)
    hb = hb_ref[...]
    tot = jnp.zeros((1, hc), F32)
    for i in range(nb):
        r = slice(i * rb, (i + 1) * rb)
        u = mm(a_ref[r, :], win, 1, 0) + hb
        cdf = 0.5 * (1.0 + lax.erf(u * (2 ** -0.5)))
        h = (u * cdf).astype(BF)
        pdf = jnp.exp(-0.5 * u * u) * ((2 * jnp.pi) ** -0.5)
        dh = mm(dm_ref[r, :], wout, 1, 0)
        du = ((cdf + u * pdf) * dh).astype(BF)
        h_ref[r, :] = h
        du_ref[r, :] = du
        tot += jnp.sum(du.astype(F32), axis=0, keepdims=True)
        m = mm(h, wout, 1, 1)
        da = mm(du, win, 1, 1)
        @pl.when(step == 0)
        def _():
            m_ref[r, :] = m
            da_ref[r, :] = da
        @pl.when(step > 0)
        def _():
            m_ref[r, :] += m
            da_ref[r, :] += da
    dhb_ref[...] = tot
    dw_ref[:, 0, :half, :] = mm(at_ref[...], du_ref[...], 1, 0).astype(BF).reshape(blocks, half, hc)
    dw_ref[:, 0, half:, :] = mm(dmt_ref[...], h_ref[...], 1, 0).astype(BF).reshape(blocks, half, hc)

    @pl.when(step == chunks - 1)
    def _():
        k = keep_ref[0, 0]
        def body(i, c):
            r = pl.ds(pl.multiple_of(i * rb, 16), rb)
            x = x_ref[r, :]
            g3 = k * cot_ref[r, :].astype(F32)
            out_ref[r, :] = (k * (x + (m_ref[r, :] + wb_ref[...]))).astype(BF)
            da = da_ref[r, :]
            unit, inv = norm_stats(x)
            sc = da * gain_ref[...]
            into = inv * (sc - jnp.mean(sc, axis=-1, keepdims=True) - unit * jnp.mean(sc * unit, axis=-1, keepdims=True))
            g2 = g3 + into
            g2_ref[r, :] = g2
            low = g2.astype(BF)
            db_ref[r, :] = low
            return (c[0] + jnp.sum(da * unit, axis=0, keepdims=True),
                    c[1] + jnp.sum(da, axis=0, keepdims=True),
                    c[2] + jnp.sum(dm_ref[r, :].astype(F32), axis=0, keepdims=True),
                    c[3] + jnp.sum(low.astype(F32), axis=0, keepdims=True))
        z = jnp.zeros((1, D), F32)
        c = lax.fori_loop(0, nb, body, (z, z, z, z))
        for j in range(4):
            sums_ref[j:j+1, :] = c[j]

def mlp(x2, cot_a, cot_b, keep, gain, shift, w4, hb, wb, *, frames):
    T, D = x2.shape
    B, H2, R, C = w4.shape
    rb = T // 4 if T % 64 == 0 else T
    hc = next(w for w in (768, 512, 384, 256, 128) if C % w == 0)
    per = C // hc
    chunks = H2 * per
    full = lambda *s: pl.BlockSpec(s, lambda j: (0,) * len(s), pipeline_mode=pl.Buffered(1))
    wspec = pl.BlockSpec((B, 1, R, hc), lambda j: (0, j // per, 0, j % per))
    hspec = pl.BlockSpec((1, hc), lambda j: (0, j))
    return pl.pallas_call(
        partial(mlp_kernel, rb=rb, chunks=chunks, frames=frames),
        grid=(chunks,),
        in_specs=[full(T, D), full(*cot_a.shape), full(*cot_b.shape), pl.BlockSpec(memory_space=pltpu.SMEM), full(1, D), full(1, D), wspec, hspec, full(1, D)],
        out_specs=[full(T, D), full(T, D), full(T, D), wspec, hspec, full(8, D)],
        out_shape=(sds(T, D), sds(T, D, t=F32), sds(T, D), sds(*w4.shape), sds(1, H2 * C, t=F32), sds(8, D, t=F32)),
        scratch_shapes=[pltpu.VMEM((T, D), BF), pltpu.VMEM((D, T), BF), pltpu.VMEM((T, D), BF), pltpu.VMEM((D, T), BF),
                        pltpu.VMEM((T, D), F32), pltpu.VMEM((T, D), F32), pltpu.VMEM((T, hc), BF), pltpu.VMEM((T, hc), BF)],
        compiler_params=pltpu.CompilerParams(vmem_limit_bytes=VMEM),
        cost_estimate=cost(75),
    )(x2, cot_a, cot_b, keep, gain, shift, w4, hb, wb)
LANES = 128
LOW = -1e30

def once(*s):
    return pl.BlockSpec(s, lambda j: (0,) * len(s), pipeline_mode=pl.Buffered(1))

def column(rows, cols, at):
    return pl.BlockSpec((rows, cols), lambda j: (0, at), pipeline_mode=pl.Buffered(1))

def sds(*s, t=BF):
    return jax.ShapeDtypeStruct(s, t)

def cost(us):
    return pl.CostEstimate(flops=us * 10**9, bytes_accessed=0, transcendentals=0)

def call(body, us, grid, ins, outs, shapes, scratch=()):
    return pl.pallas_call(body, grid=(grid,), in_specs=ins, out_specs=outs, out_shape=shapes, scratch_shapes=list(scratch),
                          compiler_params=pltpu.CompilerParams(vmem_limit_bytes=VMEM), cost_estimate=cost(us))

def qkv_store(a, wqkv, hb_ref, dst, rows, D):
    packed = mm(a, wqkv, 1, 0)
    dst[rows, :D] = (packed[:, :D] + hb_ref[0:1, :]).astype(BF)
    dst[rows, D:2 * D] = packed[:, D:2 * D].astype(BF)
    dst[rows, 2 * D:] = (packed[:, 2 * D:] + hb_ref[1:2, :]).astype(BF)

def lane_masks(head, value):
    lane = lax.broadcasted_iota(jnp.int32, (1, LANES), 1)
    return [jnp.where(lane // head == i, value, 0.0).astype(BF) for i in range(LANES // head)]

def merge(dst_ref, parts, fb):
    P = dst_ref.shape[0] // fb
    for f in range(fb):
        at = f * P
        for part in parts:
            n = part.shape[0] // fb
            dst_ref[at:at + n, :] = part[f * n:(f + 1) * n, :]
            at += n

def split(value, dst_refs, fb):
    P = value.shape[0] // fb
    for f in range(fb):
        at = f * P
        for dst in dst_refs:
            n = dst.shape[0] // fb
            dst[f * n:(f + 1) * n, :] = value[at:at + n, :]
            at += n

def sf_kernel(xa_ref, xb_ref, gain_ref, shift_ref, wqkv_ref, wproj_ref, hb_ref, wb_ref, a_ref, qkv_ref, o_ref, x2_ref, x_ref, *, fb, real, head, scale):
    M, D = x_ref.shape
    P = M // fb
    merge(x_ref, (xa_ref, xb_ref), fb)
    unit, _ = norm_stats(x_ref[...])
    a = (unit * gain_ref[...] + shift_ref[...]).astype(BF)
    a_ref[...] = a
    qkv_store(a, wqkv_ref[...], hb_ref, qkv_ref, slice(0, M), D)
    col = lax.broadcasted_iota(jnp.int32, (1, P), 1)
    hide = jnp.where(col < real, 0.0, LOW)
    ones = lane_masks(head, 1.0)
    for f in range(fb):
        r = slice(f * P, (f + 1) * P)
        for j in range(D // LANES):
            q = qkv_ref[r, j * LANES:(j + 1) * LANES]
            k = qkv_ref[r, D + j * LANES:D + (j + 1) * LANES]
            v = qkv_ref[r, 2 * D + j * LANES:2 * D + (j + 1) * LANES]
            o = None
            for m in ones:
                s = mm(q * m, k, 1, 1) * scale + hide
                p = jnp.exp(s - jnp.max(s, axis=-1, keepdims=True))
                p = (p * (1.0 / jnp.sum(p, axis=-1, keepdims=True))).astype(BF)
                part = mm(p, v * m, 1, 0)
                o = part if o is None else o + part
            o_ref[r, j * LANES:(j + 1) * LANES] = o.astype(BF)
    x2_ref[...] = x_ref[...] + (mm(o_ref[...], wproj_ref[...], 1, 1) + wb_ref[...])

def frame_blocks(rows, width, at=0):
    return pl.BlockSpec((rows, width), lambda j: (j + at, 0))

def spatial_forward(xa, xb, gain, shift, w, hb, wb, *, frames, real, head, scale, fb=2):
    D = xa.shape[1]
    steps = frames // fb
    T = xa.shape[0] + xb.shape[0]
    blk = lambda width, rows=T: frame_blocks(rows // steps, width)
    return call(partial(sf_kernel, fb=fb, real=real, head=head, scale=scale), 30, steps,
        [blk(D, xa.shape[0]), blk(D, xb.shape[0]), once(1, D), once(1, D), column(D, 3 * D, 0), column(D, D, 3), once(2, D), once(1, D)],
        [blk(D), blk(3 * D), blk(D), blk(D), blk(D)], (sds(T, D), sds(T, 3 * D), sds(T, D), sds(T, D, t=F32), sds(T, D, t=F32)))(
        xa, xb, gain, shift, w, w, hb, wb)

def norm_back_store(x, gain, da, base, sums_ref, at):
    unit, inv = norm_stats(x)
    sc = da * gain
    into = inv * (sc - jnp.mean(sc, axis=-1, keepdims=True) - unit * jnp.mean(sc * unit, axis=-1, keepdims=True))
    sums_ref[at:at + 1, :] += jnp.sum(da * unit, axis=0, keepdims=True)
    sums_ref[at + 1:at + 2, :] += jnp.sum(da, axis=0, keepdims=True)
    return base + into

def add_sum(sums_ref, at, rows):
    sums_ref[at:at + 1, :] += jnp.sum(rows.astype(F32), axis=0, keepdims=True)

def sb_kernel(g2_ref, db_ref, qkv_ref, x_ref, gain_ref, wqkv_ref, wproj_ref, *rest, fb, real, head, scale):
    dqkv_ref, g1a_ref, g1b_ref, dza_ref, dzb_ref, sums_ref, do_ref = rest[-7:]
    M, D = x_ref.shape
    P = M // fb
    @pl.when(pl.program_id(0) == 0)
    def _():
        sums_ref[...] = jnp.zeros_like(sums_ref)
    do_ref[...] = mm(db_ref[...], wproj_ref[...], 1, 0).astype(BF)
    row = lax.broadcasted_iota(jnp.int32, (P, 1), 0)
    hide = jnp.where(row < real, 0.0, LOW)
    ones = lane_masks(head, 1.0)
    for f in range(fb):
        r = slice(f * P, (f + 1) * P)
        for j in range(D // LANES):
            ls = [slice(i * D + j * LANES, i * D + (j + 1) * LANES) for i in range(3)]
            q, k, v = [qkv_ref[r, l] for l in ls]
            do = do_ref[r, ls[0]]
            dq = dk = dv = 0.0
            for m in ones:
                qm = q * m
                dom = do * m
                s = mm(k, qm, 1, 1) * scale + hide
                p = jnp.exp(s - jnp.max(s, axis=0, keepdims=True))
                p = p * (1.0 / jnp.sum(p, axis=0, keepdims=True))
                dp = mm(v, dom, 1, 1)
                ds = (p * (dp - jnp.sum(p * dp, axis=0, keepdims=True))).astype(BF)
                dv = dv + mm(p.astype(BF), dom, 1, 0)
                dk = dk + mm(ds, qm, 1, 0)
                dq = dq + mm(ds, k * m, 0, 0)
            dqkv_ref[r, ls[0]] = (dq * scale).astype(BF)
            dqkv_ref[r, ls[1]] = (dk * scale).astype(BF)
            dqkv_ref[r, ls[2]] = dv.astype(BF)
    add_sum(sums_ref, 2, dqkv_ref[:, :D])
    add_sum(sums_ref, 3, dqkv_ref[:, 2 * D:])
    da = mm(dqkv_ref[...], wqkv_ref[...], 1, 1)
    g1 = norm_back_store(x_ref[...], gain_ref[...], da, g2_ref[...], sums_ref, 0)
    split(g1, (g1a_ref, g1b_ref), fb)
    low = g1.astype(BF)
    split(low, (dza_ref, dzb_ref), fb)
    add_sum(sums_ref, 4, low)

def spatial_backward(g2, db, qkv, x1, *, gain, w, first, frames, real, head, scale, part, held=None, fb=2):
    T, D = x1.shape
    M = T // frames * fb
    nb = frames // fb // 2
    blk = lambda width, rows=M: frame_blocks(rows, width, part * nb)
    kept = [] if held is None else list(held[:5])
    low, high = frames * first, T - frames * first
    ends = [blk(D, first * fb), blk(D, M - first * fb)]
    return pl.pallas_call(
        partial(sb_kernel, fb=fb, real=real, head=head, scale=scale), grid=(nb,),
        in_specs=[blk(D), blk(D), blk(3 * D), blk(D), once(1, D), column(D, 3 * D, 0), column(D, D, 3)]
        + [pl.BlockSpec(memory_space=pl.ANY)] * len(kept),
        out_specs=[blk(3 * D)] + ends + ends + [once(8, D)],
        out_shape=(sds(T, 3 * D), sds(low, D, t=F32), sds(high, D, t=F32), sds(low, D), sds(high, D), sds(8, D, t=F32)),
        scratch_shapes=[pltpu.VMEM((M, D), BF)],
        input_output_aliases={7 + i: i for i in range(len(kept))},
        compiler_params=pltpu.CompilerParams(vmem_limit_bytes=VMEM), cost_estimate=cost(24),
    )(g2, db, qkv, x1, gain, w, w, *kept)

def over_frames(op, rows, slot):
    shift = slot
    while shift < LANES:
        rows = op(rows, pltpu.roll(rows, shift, 1))
        shift *= 2
    return rows

def tf_kernel(x_ref, gain_ref, shift_ref, wqkv_ref, wproj_ref, wfc_ref, hb_ref, wb_ref, fcb_ref,
              a_ref, qkv_ref, p_ref, o_ref, y_ref, x1_ref, all_ref, prod_ref, xs_ref, e_ref, b_ref, *, fb, nb, frames, slot, head, scale):
    M, D = x_ref.shape
    P = M // fb
    step = pl.program_id(0)
    @pl.when(step == 0)
    def _():
        fill_tables(e_ref, b_ref, slot, head)
    @pl.when(step < nb)
    def _():
        x = x_ref[...].astype(F32)
        unit, _ = norm_stats(x)
        a = (unit * gain_ref[...] + shift_ref[...]).astype(BF)
        a_ref[...] = a
        qkv_store(a, wqkv_ref[...], hb_ref, qkv_ref, slice(0, M), D)
        all_ref[pl.ds(pl.multiple_of(step * M, M), M), :] = qkv_ref[...]
        xs_ref[pl.ds(pl.multiple_of(step * M, M), M), :] = x_ref[...]
    @pl.when(step >= nb)
    def _():
        base = pl.multiple_of((step - nb) * M, M)
        for f in range(fb):
            q = all_ref[pl.ds(base + f * P, P), :D]
            for g in range(frames):
                prod_ref[f * P:(f + 1) * P, g * D:(g + 1) * D] = q * all_ref[g * P:(g + 1) * P, D:2 * D]
        s = mm(prod_ref[...], e_ref[...], 1, 0) * scale
        p = jnp.exp(s - over_frames(jnp.maximum, s, slot))
        p = p * (1.0 / over_frames(jnp.add, p, slot))
        p_ref[...] = p
        low = p.astype(BF)
        o = [None] * fb
        for g in range(frames):
            wide = mm(low, b_ref[:, g * D:(g + 1) * D], 1, 0)
            v = all_ref[g * P:(g + 1) * P, 2 * D:].astype(F32)
            for f in range(fb):
                part = wide[f * P:(f + 1) * P] * v
                o[f] = part if g == 0 else o[f] + part
        for f in range(fb):
            o_ref[f * P:(f + 1) * P, :] = o[f].astype(BF)
        y = (mm(o_ref[...], wproj_ref[...], 1, 1) + wb_ref[...]).astype(BF)
        y_ref[...] = y
        z = (mm(y, wfc_ref[...], 1, 0) + fcb_ref[...]).astype(BF)
        x1_ref[...] = xs_ref[pl.ds(base, M), :].astype(F32) + z.astype(F32)

def fill_tables(e_ref, b_ref, slot, head):
    D = e_ref.shape[0] * slot // LANES
    for g in range(LANES // slot):
        for ref, at, wide in ((e_ref, 1, 0), (b_ref, 0, 1)):
            shape = (D, LANES) if wide == 0 else (LANES, D)
            lane = lax.broadcasted_iota(jnp.int32, shape, at)
            feature = lax.broadcasted_iota(jnp.int32, shape, wide)
            hit = ((lane // slot == g) & (lane % slot == feature // head)).astype(F32).astype(BF)
            if wide == 0:
                ref[g * D:(g + 1) * D, :] = hit
            else:
                ref[:, g * D:(g + 1) * D] = hit

def temporal_forward(x, gain, shift, w, hb, wb, fcb, *, frames, head, scale, fb=4):
    T, D = x.shape
    M = T // frames * fb
    nb = frames // fb
    first = lambda w: pl.BlockSpec((M, w), lambda j: (jnp.minimum(j, nb - 1), 0))
    last = lambda w: pl.BlockSpec((M, w), lambda j: (jnp.maximum(j - nb, 0), 0))
    return call(partial(tf_kernel, fb=fb, nb=nb, frames=frames, slot=LANES // frames, head=head, scale=scale), 22, 2 * nb,
        [first(D), once(1, D), once(1, D), column(D, 3 * D, 0), column(D, D, 3), column(D, D, 4), once(2, D), once(1, D), once(1, D)],
        [first(D), first(3 * D), last(LANES), last(D), last(D), last(D)],
        (sds(T, D), sds(T, 3 * D), sds(T, LANES, t=F32), sds(T, D), sds(T, D), sds(T, D, t=F32)),
        [pltpu.VMEM((T, 3 * D), BF), pltpu.VMEM((M, frames * D), BF), pltpu.VMEM((T, D), BF),
         pltpu.VMEM((frames * D, LANES), BF), pltpu.VMEM((LANES, frames * D), BF)])(
        x, gain, shift, w, w, w, hb, wb, fcb)

def zero_first(*refs):
    @pl.when(pl.program_id(0) == 0)
    def _():
        for ref in refs:
            ref[...] = jnp.zeros_like(ref)

def pull_kernel(dz_ref, wproj_ref, wfc_ref, dy_ref, do_ref, sums_ref):
    zero_first(sums_ref)
    dy = mm(dz_ref[...], wfc_ref[...], 1, 1).astype(BF)
    dy_ref[...] = dy
    add_sum(sums_ref, 4, dy)
    do_ref[...] = mm(dy, wproj_ref[...], 1, 0).astype(BF)

def temporal_pull(dz, w, *, blocks=2):
    T, D = dz.shape
    blk = pl.BlockSpec((T // blocks, D), lambda j: (j, 0))
    return call(pull_kernel, 4, blocks, [blk, column(D, D, 3), column(D, D, 4)], [blk, blk, once(8, D)],
                (sds(T, D), sds(T, D), sds(8, D, t=F32)))(dz, w, w)

def tb_kernel(do_ref, qkv_ref, p_ref, dqkv_ref, sums_ref, dk_ref, dv_ref, prod_ref, e_ref, b_ref, *, fb, nb, frames, slot, head, scale):
    M = p_ref.shape[0]
    T, D = do_ref.shape
    P = M // fb
    step = pl.program_id(0)
    zero_first(sums_ref, dk_ref, dv_ref)
    @pl.when(step == 0)
    def _():
        fill_tables(e_ref, b_ref, slot, head)
    base = pl.multiple_of(step * M, M)
    for f in range(fb):
        do = do_ref[pl.ds(base + f * P, P), :]
        for g in range(frames):
            prod_ref[f * P:(f + 1) * P, g * D:(g + 1) * D] = do * qkv_ref[g * P:(g + 1) * P, 2 * D:]
    dp = mm(prod_ref[...], e_ref[...], 1, 0)
    p = p_ref[...]
    ds = (p * (dp - over_frames(jnp.add, p * dp, slot))).astype(BF)
    low = p.astype(BF)
    dq = [0.0] * fb
    for g in range(frames):
        gr = slice(g * P, (g + 1) * P)
        wide_p = mm(low, b_ref[:, g * D:(g + 1) * D], 1, 0)
        wide_s = mm(ds, b_ref[:, g * D:(g + 1) * D], 1, 0)
        k = qkv_ref[gr, D:2 * D].astype(F32)
        dk, dv = dk_ref[gr, :], dv_ref[gr, :]
        for f in range(fb):
            fr = pl.ds(base + f * P, P)
            wp, ws = wide_p[f * P:(f + 1) * P], wide_s[f * P:(f + 1) * P]
            dv = dv + wp * do_ref[fr, :].astype(F32)
            dk = dk + ws * qkv_ref[fr, :D].astype(F32)
            dq[f] = dq[f] + ws * k
        dk_ref[gr, :] = dk
        dv_ref[gr, :] = dv
    for f in range(fb):
        low = (dq[f] * scale).astype(BF)
        add_sum(sums_ref, 2, low)
        dqkv_ref[pl.ds(base + f * P, P), :D] = low
    @pl.when(step == nb - 1)
    def _():
        for g in range(frames):
            gr = slice(g * P, (g + 1) * P)
            dqkv_ref[gr, D:2 * D] = (dk_ref[gr, :] * scale).astype(BF)
            low = dv_ref[gr, :].astype(BF)
            add_sum(sums_ref, 3, low)
            dqkv_ref[gr, 2 * D:] = low

def temporal_backward(do, qkv, p, *, frames, head, scale, fb=4):
    T, D = do.shape
    M = T // frames * fb
    nb = frames // fb
    return call(partial(tb_kernel, fb=fb, nb=nb, frames=frames, slot=LANES // frames, head=head, scale=scale), 20, nb,
        [once(T, D), once(T, 3 * D), pl.BlockSpec((M, LANES), lambda j: (j, 0))],
        [once(T, 3 * D), once(8, D)], (sds(T, 3 * D), sds(8, D, t=F32)),
        [pltpu.VMEM((T, D), F32), pltpu.VMEM((T, D), F32), pltpu.VMEM((M, frames * D), BF),
         pltpu.VMEM((frames * D, LANES), BF), pltpu.VMEM((LANES, frames * D), BF)])(do, qkv, p)

def end_kernel(dqkv_ref, x_ref, g1_ref, gain_ref, wqkv_ref, out_ref, sums_ref):
    zero_first(sums_ref)
    da = mm(dqkv_ref[...], wqkv_ref[...], 1, 1)
    out = norm_back_store(x_ref[...].astype(F32), gain_ref[...], da, g1_ref[...], sums_ref, 0)
    out_ref[...] = out.astype(BF)

def temporal_end(dqkv, x, g1, gain, w, *, blocks=2):
    T, D = x.shape
    blk = lambda w: pl.BlockSpec((T // blocks, w), lambda j: (j, 0))
    return call(end_kernel, 7, blocks, [blk(3 * D), blk(D), blk(D), once(1, D), column(D, 3 * D, 0)], [blk(D), once(8, D)],
                (sds(T, D), sds(8, D, t=F32)))(dqkv, x, g1, gain, w)

def wg_kernel(*refs, starts, counts, halves, rows):
    n = sum(counts)
    a_refs, b_refs, out_ref, t_refs = refs[:n], refs[n:2 * n], refs[2 * n], refs[2 * n + 1:]
    step = pl.program_id(0)
    at = 0
    for i, many in enumerate(counts):
        mine = range(at, at + many)
        at += many
        @pl.when(step == starts[i])
        def _():
            for t_ref, n_at in zip(t_refs, mine):
                t_ref[...] = a_refs[n_at][...].T
        stop = starts[i + 1] if i + 1 < len(counts) else step + 1
        @pl.when((step >= starts[i]) & (step < stop))
        def _():
            res = sum(mm(t_ref[...], b_refs[n_at][...], 1, 0) for t_ref, n_at in zip(t_refs, mine))
            if rows:
                parts = res.reshape(-1, halves, rows, res.shape[-1])
                for h in range(halves):
                    out_ref[h] = parts[:, h].reshape(-1, res.shape[-1]).astype(BF)
            else:
                out_ref[0] = res.astype(BF)

def weight_grads(pairs, halves, rows, us):
    D = pairs[0][0][0].shape[1]
    starts, steps, specs, b_specs = [], 0, [], []
    for many_a, many_b in pairs:
        starts.append(steps)
        chunks = many_b[0].shape[1] // D
        for a in many_a:
            specs.append(once(*a.shape))
            b_specs.append(chunk_spec(a.shape[0], D, steps, chunks))
        steps += chunks
    cols = steps * D
    fits = rows % 8 == 0
    groups = halves if fits else 1
    counts = [len(many_a) for many_a, _ in pairs]
    lefts = [a for many_a, _ in pairs for a in many_a]
    rights = [b for _, many_b in pairs for b in many_b]
    out = call(partial(wg_kernel, starts=starts, counts=counts, halves=halves, rows=rows if fits else 0), us, steps,
        specs + b_specs, [pl.BlockSpec((groups, D // groups, D), lambda j: (0, 0, j))], (sds(groups, D // groups, cols),),
        [pltpu.VMEM((D, a.shape[0]), BF) for a in pairs[0][0]])(*lefts, *rights)[0]
    if fits:
        return out.reshape(halves, -1, rows, cols)
    return jnp.swapaxes(out.reshape(-1, halves, rows, cols), 0, 1)

def chunk_spec(rows, cols, start, many):
    return pl.BlockSpec((rows, cols), lambda j: (0, jnp.clip(j - start, 0, many - 1)))


def exchange(pieces, axis):
    size = len(pieces)
    return [pieces[0]] + [
        lax.ppermute(pieces[d], axis, [(i, i ^ d) for i in range(size)]) for d in range(1, size)
    ]


def in_order(pieces, axis, step=1):
    while step < len(pieces):
        swap = (lax.axis_index(axis) // step) % 2 == 1
        pieces = [jnp.where(swap, pieces[c ^ step], pieces[c]) for c in range(len(pieces))]
        step *= 2
    return pieces


def collect(array, axis, at=0, hold=()):
    pieces = exchange([array] * lax.axis_size(axis), axis)
    pieces = pieces[:1] + [after(piece, *hold) for piece in pieces[1:]]
    return jnp.stack(in_order(pieces, axis), axis=at)


def partner(array, axis, step):
    size = lax.axis_size(axis)
    return lax.ppermute(array, axis, [(i, i ^ step) for i in range(size)])


def far_first(array, axis):
    size = lax.axis_size(axis)
    step = size // 2
    out = array[None]
    while step:
        other = partner(out, axis, step)
        low = (lax.axis_index(axis) // step) % 2 == 0
        out = jnp.stack((jnp.where(low, out, other), jnp.where(low, other, out)), axis=1)
        out = out.reshape((-1,) + array.shape)
        step //= 2
    return out


def near_first(array, axis):
    size = lax.axis_size(axis)
    step = 1
    while step < size:
        blocks = array.reshape((-1, 2) + array.shape[1:])
        mine = (lax.axis_index(axis) // step) % 2
        send = lax.dynamic_index_in_dim(blocks, 1 - mine, 1, keepdims=False).astype(BF)
        keep = lax.dynamic_index_in_dim(blocks, mine, 1, keepdims=False)
        array = keep.astype(F32) + partner(send, axis, step).astype(F32)
        step *= 2
    return array[0]


def split_off(array, axis):
    place = lax.axis_index(axis)
    pieces = [
        lax.dynamic_index_in_dim(array, place ^ d, 0, keepdims=False)
        for d in range(lax.axis_size(axis))
    ]
    return exchange(pieces[:1] + [piece.astype(BF) for piece in pieces[1:]], axis)


def added(pieces, *hold):
    out = pieces[0].astype(F32)
    for piece in pieces[1:]:
        out = out + after(piece, *hold).astype(F32)
    return out


def shed(array, axis, hold=()):
    return added(split_off(array, axis), *hold)


def shed_at_once(array, axis, *hold):
    came = lax.all_to_all(array.astype(BF), axis, split_axis=0, concat_axis=0, tiled=True)
    came = after(came, *hold)
    return jnp.sum(came.astype(F32), axis=0)


def after(array, *others):
    return lax.optimization_barrier((array,) + others)[0]


def plus_others(array, axis):
    came = exchange([array] * lax.axis_size(axis), axis)
    return sum(came[1:], came[0])


def local(
    clips_in,
    valid_clips,
    norm_gains,
    norm_shifts,
    temporal_qkv,
    temporal_proj,
    temporal_fc,
    spatial_qkv,
    spatial_proj,
    mlp_in,
    mlp_out,
    head_bias,
    width_bias,
    fc_bias,
    hidden_bias,
    cotangent,
):
    held, frames_held, places, width = clips_in.shape
    head = width // HEADS
    scale = head ** (-0.5)
    across = lax.axis_size("context")
    halves = lax.axis_size("tensor")
    place = lax.axis_index("context")
    own_rows = temporal_qkv.shape[0]
    in_rows, in_cols = mlp_in.shape
    spread = held % across == 0
    clips = held // across if spread else held
    share = 1.0 if spread else 1.0 / across
    frames = frames_held * across
    first_places = places // 32 * 16
    cuts = (slice(0, first_places), slice(first_places, places))

    def to_clips(array):
        array = jnp.swapaxes(array, 1, 2)
        if spread:
            array = lax.all_to_all(array, "context", split_axis=0, concat_axis=0, tiled=True)
            return array.reshape((across, clips) + array.shape[1:])
        return lax.all_gather(array, "context", axis=0)

    def fill(array):
        array = jnp.swapaxes(array, 1, 2).reshape(frames, array.shape[1], width)
        array = jnp.pad(array, ((0, 0), (0, -array.shape[1] % 16), (0, 0)))
        return array.reshape(-1, width)

    def by_place(array, real):
        array = array.reshape(across, frames_held, -1, width)[:, :, :real]
        return jnp.swapaxes(array, 1, 2)

    def from_clips(array):
        if spread:
            array = lax.all_to_all(array, "context", split_axis=0, concat_axis=0, tiled=True)
        else:
            array = lax.dynamic_slice_in_dim(array, place, 1, 0)
        return array

    def send_back(array):
        array = by_place(array, places)
        if spread:
            return split_off(array, "context")
        return [lax.dynamic_index_in_dim(array, place, 0, keepdims=False)]

    def sent_back(pieces):
        return jnp.swapaxes(jnp.stack(in_order(pieces, "context")), 1, 2)

    if spread:
        valid = lax.dynamic_slice_in_dim(valid_clips, place * clips, clips, 0)
    else:
        valid = valid_clips
    keep = valid.astype(F32)

    def flat3(weight):
        return weight.reshape(own_rows, 3 * width)

    def by_shard(d):
        return d.reshape((lax.axis_size("shard"), across) + d.shape[1:])

    t_own = jnp.concatenate((flat3(temporal_qkv), temporal_proj, temporal_fc), axis=1).astype(BF)
    s_own = jnp.concatenate((flat3(spatial_qkv), spatial_proj), axis=1).astype(BF)
    mlp_own = jnp.concatenate((mlp_in, mlp_out), axis=0).astype(BF)
    clip_parts = [clips_in[:, :, cut] for cut in cuts]
    pull_parts = [cotangent[:, :, cut] for cut in cuts]
    gain = [norm_gains[i : i + 1] for i in range(3)]
    shift = [norm_shifts[i : i + 1] for i in range(3)]
    wide = [width_bias[i : i + 1] for i in range(3)]
    head_pairs, fc_row, hidden_row = [head_bias[0], head_bias[1]], fc_bias[None], hidden_bias[None]
    early = clip_parts + pull_parts + gain + shift + wide + head_pairs + [fc_row, hidden_row]
    first = collect(jnp.concatenate((t_own, s_own), axis=1), "context", hold=early)
    t_first, s_first = first[..., : t_own.shape[1]], first[..., t_own.shape[1] :]
    rows_a = to_clips(after(clip_parts[0], first))
    mlp_all = lax.all_gather(after(mlp_own, first), ALL, axis=0, tiled=True)
    mlp_all = mlp_all.reshape(-1, halves, 2 * in_rows, in_cols)
    t_chips = collect(t_first, "shard", hold=(rows_a,))
    t_all = collect(t_chips, "tensor", 2).reshape(-1, t_own.shape[1])
    rows_b = to_clips(after(clip_parts[1], rows_a))
    pull_a = to_clips(after(pull_parts[0], rows_b))
    pull_b = to_clips(after(pull_parts[1], pull_a))

    def one_clip(x_a, x_b, pull_a, pull_b, keep_one):
        sizes = dict(frames=frames, head=head, scale=scale)
        forward_t = partial(
            temporal_forward, gain=gain[0], shift=shift[0], w=t_all, hb=head_pairs[0], wb=wide[0],
            fcb=fc_row, **sizes,
        )
        x_a = fill(x_a)
        at_a, qkv_a, probs_a, o_a, y_a, x1_a = forward_t(x_a)
        s_all = collect(after(s_first, rows_a), "shard", hold=(x1_a,))
        x_b = fill(after(x_b, x1_a, s_all))
        at_b, qkv_b, probs_b, o_b, y_b, x1_b = forward_t(x_b)
        s_all = collect(s_all, "tensor", 2, hold=(x1_b,)).reshape(-1, s_own.shape[1])
        pull_a = after(pull_a, x1_b)
        sizes_s = dict(sizes, real=places)
        a_s, qkv_s, o_s, x2, x1 = spatial_forward(
            x1_a, after(x1_b, pull_a), gain[1], shift[1], s_all, head_pairs[1], wide[1], **sizes_s
        )
        out, g2, db, d_m, d_hidden, sums_m = mlp(
            x2, fill(pull_a), fill(after(pull_b, x2)), keep_one.reshape(1, 1), gain[2], shift[2], mlp_all, hidden_row, wide[2],
            frames=frames,
        )
        back_s = partial(spatial_backward, gain=gain[1], w=s_all, first=first_places, **sizes_s)
        grads_of = partial(weight_grads, halves=halves, rows=own_rows)
        d_m = (share * d_m if share != 1.0 else d_m).astype(BF).reshape(-1, in_cols)
        d_m = lax.psum_scatter(d_m, ALL, scatter_dimension=0, tiled=True)
        back = send_back(out)
        half = back_s(g2, db, qkv_s, x1, part=0)
        tied = after(db, half[0], *back[1:2])
        d_qkv_s, g1_a, g1_b, dz_a, dz_b, sums_s = back_s(g2, tied, qkv_s, x1, part=1, held=half)
        sums_s = sums_s + half[5]
        tied = after(d_qkv_s, *back[2:3])
        d_s = share * grads_of([([a_s], [tied]), ([db], [o_s])], us=12)
        tied = after(dz_a, d_s)
        d_s = split_off(d_s, "tensor")
        dy_a, do_a, sums_y = temporal_pull(tied, t_all)
        dy_b, do_b, sums_yb = temporal_pull(after(dz_b, dy_a), t_all)
        d_s = added(d_s, dy_b).astype(BF)
        tied = after(dy_b, d_s, *back[3:])
        d_s = split_off(by_shard(d_s), "shard")
        d_r = share * grads_of([([dy_a, tied], [o_a, o_b]), ([y_a, y_b], [dz_a, dz_b])], us=6)
        tied = after(do_a, d_r)
        d_r = split_off(d_r, "tensor")
        d_qkv_a, sums_q = temporal_backward(tied, qkv_a, probs_a, **sizes)
        d_s = added(d_s, d_qkv_a).astype(BF)
        d_r = added(d_r, d_qkv_a).astype(BF)
        tied = after(d_qkv_a, d_r, d_s)
        d_s = split_off(d_s, "context")
        into_a, sums_x = temporal_end(tied, x_a, g1_a, gain[0], t_all)
        swap_a = by_place(into_a, first_places)
        into_a = from_clips(swap_a)
        tied = after(do_b, swap_a, d_r, d_m)
        d_m = d_m.astype(F32)
        d_r = split_off(by_shard(d_r), "shard")
        d_qkv_b, sums_qb = temporal_backward(tied, qkv_b, probs_b, **sizes)
        d_s = added(d_s, d_qkv_b)
        d_r = added(d_r, d_qkv_b).astype(BF)
        tied = after(d_qkv_b, d_r, d_s)
        d_q = share * grads_of([([at_a, at_b], [d_qkv_a, tied])], us=9)
        tied, d_q = lax.optimization_barrier((d_qkv_b, d_q, into_a))[:2]
        d_q = split_off(d_q, "tensor")
        into_b, sums_xb = temporal_end(tied, x_b, g1_b, gain[0], t_all)
        swap_b = by_place(into_b, places - first_places)
        into_b = from_clips(after(swap_b, into_a))
        t, m = sums_y + sums_yb + sums_q + sums_qb + sums_x + sums_xb, sums_m
        rows = [v[n : n + 1] for n in (0, 1) for v in (t, sums_s, m)] + [t[2:4], sums_s[2:4]]
        rows = rows + [t[4:5], m[3:4], m[2:3], sums_s[4:5], d_hidden.reshape(-1, width)]
        small = plus_others(share * jnp.concatenate(rows, axis=0), "tensor")
        d_q = added(d_q, swap_b).astype(BF)
        small = plus_others(small, "shard")
        d_q = added(split_off(by_shard(d_q), "shard"), small).astype(BF)
        output = sent_back([after(piece, d_q) for piece in back])
        small = plus_others(after(small, d_q), "context")
        d_q = shed(jnp.concatenate((d_r, d_q), axis=-1), "context")
        into = jnp.swapaxes(jnp.concatenate((into_a, after(into_b, output)), axis=1), 1, 2)
        return output, into, (d_q, d_s, d_m, small)

    given = (rows_a, rows_b, pull_a, pull_b)
    parts = [one_clip(*[v[:, i] for v in given], keep[i]) for i in range(clips)]
    output, input_grad = [
        jnp.stack([part[n] for part in parts], axis=1).reshape(clips_in.shape) for n in (0, 1)
    ]
    grads = parts[0][2]
    for part in parts[1:]:
        grads = jax.tree.map(jnp.add, grads, part[2])
    d_t, d_s, d_mlp, small = grads
    d_t_rest, d_t_qkv = d_t[:, : 2 * width], d_t[:, 2 * width :]
    return (
        output,
        input_grad,
        small[0:3],
        small[3:6],
        d_t_qkv.reshape(own_rows, 3, width),
        d_t_rest[:, :width],
        d_t_rest[:, width:],
        d_s[:, : 3 * width].reshape(own_rows, 3, width),
        d_s[:, 3 * width :],
        d_mlp[:in_rows],
        d_mlp[in_rows:],
        small[6:10].reshape(2, 2, width),
        small[10:13],
        small[13],
        small[14:].reshape(-1),
    )


def solution(mesh):
    clip = P(("shard", "tensor"), "context", None, None)
    row, block = P(ALL, None), P(("shard", "context"), "tensor")
    deep, whole = P(ALL, None, None), P()
    weights = (deep, row, row, deep, row, block, block)
    in_specs = (clip, P(("shard", "tensor")), whole, whole) + weights + (whole,) * 4 + (clip,)
    out_specs = (clip, clip, whole, whole) + weights + (whole,) * 4
    return jax.shard_map(local, mesh=mesh, in_specs=in_specs, out_specs=out_specs, check_vma=False)
```

```python
from functools import partial

import jax
import jax.numpy as jnp
from jax import lax
from jax.experimental import pallas as pl
from jax.experimental.pallas import tpu as pltpu
from jax.sharding import PartitionSpec as P

HEADS = 12
EPS = 1e-05
ALL = ("shard", "context", "tensor")
BF = jnp.bfloat16
F32 = jnp.float32
VMEM = 60 * 2**20

def mm(left, right, left_dim, right_dim):
    return lax.dot_general(left, right, (((left_dim,), (right_dim,)), ((), ())), preferred_element_type=F32)

def norm_stats(rows):
    centered = rows - jnp.mean(rows, axis=-1, keepdims=True)
    inv = lax.rsqrt(jnp.mean(centered * centered, axis=-1, keepdims=True) + EPS)
    return centered * inv, inv

def mlp_kernel(x_ref, cota_ref, cotb_ref, keep_ref, gain_ref, shift_ref, w_ref, hb_ref, wb_ref,
               out_ref, g2_ref, db_ref, dw_ref, dhb_ref, sums_ref,
               a_ref, at_ref, dm_ref, dmt_ref, m_ref, da_ref, h_ref, du_ref, *, rb, chunks, frames):
    step = pl.program_id(0)
    T, D = x_ref.shape
    cot_ref = out_ref
    nb = T // rb
    blocks, _, both, hc = w_ref.shape
    half = both // 2

    @pl.when(step == 0)
    def _():
        merge(cot_ref, (cota_ref, cotb_ref), frames)
        def body(i, c):
            r = pl.ds(pl.multiple_of(i * rb, 16), rb)
            unit, _ = norm_stats(x_ref[r, :])
            a = (unit * gain_ref[...] + shift_ref[...]).astype(BF)
            a_ref[r, :] = a
            dm = (keep_ref[0, 0] * cot_ref[r, :].astype(F32)).astype(BF)
            dm_ref[r, :] = dm
            return c
        lax.fori_loop(0, nb, body, 0)
        at_ref[...] = a_ref[...].T
        dmt_ref[...] = dm_ref[...].T

    win = w_ref[:, 0, :half, :].reshape(D, hc)
    wout = w_ref[:, 0, half:, :].reshape(D, hc)
    hb = hb_ref[...]
    tot = jnp.zeros((1, hc), F32)
    for i in range(nb):
        r = slice(i * rb, (i + 1) * rb)
        u = mm(a_ref[r, :], win, 1, 0) + hb
        cdf = 0.5 * (1.0 + lax.erf(u * (2 ** -0.5)))
        h = (u * cdf).astype(BF)
        pdf = jnp.exp(-0.5 * u * u) * ((2 * jnp.pi) ** -0.5)
        dh = mm(dm_ref[r, :], wout, 1, 0)
        du = ((cdf + u * pdf) * dh).astype(BF)
        h_ref[r, :] = h
        du_ref[r, :] = du
        tot += jnp.sum(du.astype(F32), axis=0, keepdims=True)
        m = mm(h, wout, 1, 1)
        da = mm(du, win, 1, 1)
        @pl.when(step == 0)
        def _():
            m_ref[r, :] = m
            da_ref[r, :] = da
        @pl.when(step > 0)
        def _():
            m_ref[r, :] += m
            da_ref[r, :] += da
    dhb_ref[...] = tot
    dw_ref[:, 0, :half, :] = mm(at_ref[...], du_ref[...], 1, 0).astype(BF).reshape(blocks, half, hc)
    dw_ref[:, 0, half:, :] = mm(dmt_ref[...], h_ref[...], 1, 0).astype(BF).reshape(blocks, half, hc)

    @pl.when(step == chunks - 1)
    def _():
        k = keep_ref[0, 0]
        def body(i, c):
            r = pl.ds(pl.multiple_of(i * rb, 16), rb)
            x = x_ref[r, :]
            g3 = k * cot_ref[r, :].astype(F32)
            out_ref[r, :] = (k * (x + (m_ref[r, :] + wb_ref[...]))).astype(BF)
            da = da_ref[r, :]
            unit, inv = norm_stats(x)
            sc = da * gain_ref[...]
            into = inv * (sc - jnp.mean(sc, axis=-1, keepdims=True) - unit * jnp.mean(sc * unit, axis=-1, keepdims=True))
            g2 = g3 + into
            g2_ref[r, :] = g2
            low = g2.astype(BF)
            db_ref[r, :] = low
            return (c[0] + jnp.sum(da * unit, axis=0, keepdims=True),
                    c[1] + jnp.sum(da, axis=0, keepdims=True),
                    c[2] + jnp.sum(dm_ref[r, :].astype(F32), axis=0, keepdims=True),
                    c[3] + jnp.sum(low.astype(F32), axis=0, keepdims=True))
        z = jnp.zeros((1, D), F32)
        c = lax.fori_loop(0, nb, body, (z, z, z, z))
        for j in range(4):
            sums_ref[j:j+1, :] = c[j]

def mlp(x2, cot_a, cot_b, keep, gain, shift, w4, hb, wb, *, frames):
    T, D = x2.shape
    B, H2, R, C = w4.shape
    rb = T // 4 if T % 64 == 0 else T
    hc = next(w for w in (768, 512, 384, 256, 128) if C % w == 0)
    per = C // hc
    chunks = H2 * per
    full = lambda *s: pl.BlockSpec(s, lambda j: (0,) * len(s), pipeline_mode=pl.Buffered(1))
    wspec = pl.BlockSpec((B, 1, R, hc), lambda j: (0, j // per, 0, j % per))
    hspec = pl.BlockSpec((1, hc), lambda j: (0, j))
    return pl.pallas_call(
        partial(mlp_kernel, rb=rb, chunks=chunks, frames=frames),
        grid=(chunks,),
        in_specs=[full(T, D), full(*cot_a.shape), full(*cot_b.shape), pl.BlockSpec(memory_space=pltpu.SMEM), full(1, D), full(1, D), wspec, hspec, full(1, D)],
        out_specs=[full(T, D), full(T, D), full(T, D), wspec, hspec, full(8, D)],
        out_shape=(sds(T, D), sds(T, D, t=F32), sds(T, D), sds(*w4.shape), sds(1, H2 * C, t=F32), sds(8, D, t=F32)),
        scratch_shapes=[pltpu.VMEM((T, D), BF), pltpu.VMEM((D, T), BF), pltpu.VMEM((T, D), BF), pltpu.VMEM((D, T), BF),
                        pltpu.VMEM((T, D), F32), pltpu.VMEM((T, D), F32), pltpu.VMEM((T, hc), BF), pltpu.VMEM((T, hc), BF)],
        compiler_params=pltpu.CompilerParams(vmem_limit_bytes=VMEM),
        cost_estimate=cost(75),
    )(x2, cot_a, cot_b, keep, gain, shift, w4, hb, wb)
LANES = 128
LOW = -1e30

def once(*s):
    return pl.BlockSpec(s, lambda j: (0,) * len(s), pipeline_mode=pl.Buffered(1))

def column(rows, cols, at):
    return pl.BlockSpec((rows, cols), lambda j: (0, at), pipeline_mode=pl.Buffered(1))

def sds(*s, t=BF):
    return jax.ShapeDtypeStruct(s, t)

def cost(us):
    return pl.CostEstimate(flops=us * 10**9, bytes_accessed=0, transcendentals=0)

def call(body, us, grid, ins, outs, shapes, scratch=()):
    return pl.pallas_call(body, grid=(grid,), in_specs=ins, out_specs=outs, out_shape=shapes, scratch_shapes=list(scratch),
                          compiler_params=pltpu.CompilerParams(vmem_limit_bytes=VMEM), cost_estimate=cost(us))

def qkv_store(a, wqkv, hb_ref, dst, rows, D):
    packed = mm(a, wqkv, 1, 0)
    dst[rows, :D] = (packed[:, :D] + hb_ref[0:1, :]).astype(BF)
    dst[rows, D:2 * D] = packed[:, D:2 * D].astype(BF)
    dst[rows, 2 * D:] = (packed[:, 2 * D:] + hb_ref[1:2, :]).astype(BF)

def lane_masks(head, value):
    lane = lax.broadcasted_iota(jnp.int32, (1, LANES), 1)
    return [jnp.where(lane // head == i, value, 0.0).astype(BF) for i in range(LANES // head)]

def merge(dst_ref, parts, fb):
    P = dst_ref.shape[0] // fb
    for f in range(fb):
        at = f * P
        for part in parts:
            n = part.shape[0] // fb
            dst_ref[at:at + n, :] = part[f * n:(f + 1) * n, :]
            at += n

def split(value, dst_refs, fb):
    P = value.shape[0] // fb
    for f in range(fb):
        at = f * P
        for dst in dst_refs:
            n = dst.shape[0] // fb
            dst[f * n:(f + 1) * n, :] = value[at:at + n, :]
            at += n

def sf_kernel(xa_ref, xb_ref, gain_ref, shift_ref, wqkv_ref, wproj_ref, hb_ref, wb_ref, a_ref, qkv_ref, o_ref, x2_ref, x_ref, *, fb, real, head, scale):
    M, D = x_ref.shape
    P = M // fb
    merge(x_ref, (xa_ref, xb_ref), fb)
    unit, _ = norm_stats(x_ref[...])
    a = (unit * gain_ref[...] + shift_ref[...]).astype(BF)
    a_ref[...] = a
    qkv_store(a, wqkv_ref[...], hb_ref, qkv_ref, slice(0, M), D)
    col = lax.broadcasted_iota(jnp.int32, (1, P), 1)
    hide = jnp.where(col < real, 0.0, LOW)
    ones = lane_masks(head, 1.0)
    for f in range(fb):
        r = slice(f * P, (f + 1) * P)
        for j in range(D // LANES):
            q = qkv_ref[r, j * LANES:(j + 1) * LANES]
            k = qkv_ref[r, D + j * LANES:D + (j + 1) * LANES]
            v = qkv_ref[r, 2 * D + j * LANES:2 * D + (j + 1) * LANES]
            o = None
            for m in ones:
                s = mm(q * m, k, 1, 1) * scale + hide
                p = jnp.exp(s - jnp.max(s, axis=-1, keepdims=True))
                p = (p * (1.0 / jnp.sum(p, axis=-1, keepdims=True))).astype(BF)
                part = mm(p, v * m, 1, 0)
                o = part if o is None else o + part
            o_ref[r, j * LANES:(j + 1) * LANES] = o.astype(BF)
    x2_ref[...] = x_ref[...] + (mm(o_ref[...], wproj_ref[...], 1, 1) + wb_ref[...])

def frame_blocks(rows, width, at=0):
    return pl.BlockSpec((rows, width), lambda j: (j + at, 0))

def spatial_forward(xa, xb, gain, shift, w, hb, wb, *, frames, real, head, scale, fb=2):
    D = xa.shape[1]
    steps = frames // fb
    T = xa.shape[0] + xb.shape[0]
    blk = lambda width, rows=T: frame_blocks(rows // steps, width)
    return call(partial(sf_kernel, fb=fb, real=real, head=head, scale=scale), 30, steps,
        [blk(D, xa.shape[0]), blk(D, xb.shape[0]), once(1, D), once(1, D), column(D, 3 * D, 0), column(D, D, 3), once(2, D), once(1, D)],
        [blk(D), blk(3 * D), blk(D), blk(D), blk(D)], (sds(T, D), sds(T, 3 * D), sds(T, D), sds(T, D, t=F32), sds(T, D, t=F32)))(
        xa, xb, gain, shift, w, w, hb, wb)

def norm_back_store(x, gain, da, base, sums_ref, at):
    unit, inv = norm_stats(x)
    sc = da * gain
    into = inv * (sc - jnp.mean(sc, axis=-1, keepdims=True) - unit * jnp.mean(sc * unit, axis=-1, keepdims=True))
    sums_ref[at:at + 1, :] += jnp.sum(da * unit, axis=0, keepdims=True)
    sums_ref[at + 1:at + 2, :] += jnp.sum(da, axis=0, keepdims=True)
    return base + into

def add_sum(sums_ref, at, rows):
    sums_ref[at:at + 1, :] += jnp.sum(rows.astype(F32), axis=0, keepdims=True)

def sb_kernel(g2_ref, db_ref, qkv_ref, x_ref, gain_ref, wqkv_ref, wproj_ref, *rest, fb, real, head, scale):
    dqkv_ref, g1a_ref, g1b_ref, dza_ref, dzb_ref, sums_ref, do_ref = rest[-7:]
    M, D = x_ref.shape
    P = M // fb
    @pl.when(pl.program_id(0) == 0)
    def _():
        sums_ref[...] = jnp.zeros_like(sums_ref)
    do_ref[...] = mm(db_ref[...], wproj_ref[...], 1, 0).astype(BF)
    row = lax.broadcasted_iota(jnp.int32, (P, 1), 0)
    hide = jnp.where(row < real, 0.0, LOW)
    ones = lane_masks(head, 1.0)
    for f in range(fb):
        r = slice(f * P, (f + 1) * P)
        for j in range(D // LANES):
            ls = [slice(i * D + j * LANES, i * D + (j + 1) * LANES) for i in range(3)]
            q, k, v = [qkv_ref[r, l] for l in ls]
            do = do_ref[r, ls[0]]
            dq = dk = dv = 0.0
            for m in ones:
                qm = q * m
                dom = do * m
                s = mm(k, qm, 1, 1) * scale + hide
                p = jnp.exp(s - jnp.max(s, axis=0, keepdims=True))
                p = p * (1.0 / jnp.sum(p, axis=0, keepdims=True))
                dp = mm(v, dom, 1, 1)
                ds = (p * (dp - jnp.sum(p * dp, axis=0, keepdims=True))).astype(BF)
                dv = dv + mm(p.astype(BF), dom, 1, 0)
                dk = dk + mm(ds, qm, 1, 0)
                dq = dq + mm(ds, k * m, 0, 0)
            dqkv_ref[r, ls[0]] = (dq * scale).astype(BF)
            dqkv_ref[r, ls[1]] = (dk * scale).astype(BF)
            dqkv_ref[r, ls[2]] = dv.astype(BF)
    add_sum(sums_ref, 2, dqkv_ref[:, :D])
    add_sum(sums_ref, 3, dqkv_ref[:, 2 * D:])
    da = mm(dqkv_ref[...], wqkv_ref[...], 1, 1)
    g1 = norm_back_store(x_ref[...], gain_ref[...], da, g2_ref[...], sums_ref, 0)
    split(g1, (g1a_ref, g1b_ref), fb)
    low = g1.astype(BF)
    split(low, (dza_ref, dzb_ref), fb)
    add_sum(sums_ref, 4, low)

def spatial_backward(g2, db, qkv, x1, *, gain, w, first, frames, real, head, scale, part, held=None, fb=2):
    T, D = x1.shape
    M = T // frames * fb
    nb = frames // fb // 2
    blk = lambda width, rows=M: frame_blocks(rows, width, part * nb)
    kept = [] if held is None else list(held[:5])
    low, high = frames * first, T - frames * first
    ends = [blk(D, first * fb), blk(D, M - first * fb)]
    return pl.pallas_call(
        partial(sb_kernel, fb=fb, real=real, head=head, scale=scale), grid=(nb,),
        in_specs=[blk(D), blk(D), blk(3 * D), blk(D), once(1, D), column(D, 3 * D, 0), column(D, D, 3)]
        + [pl.BlockSpec(memory_space=pl.ANY)] * len(kept),
        out_specs=[blk(3 * D)] + ends + ends + [once(8, D)],
        out_shape=(sds(T, 3 * D), sds(low, D, t=F32), sds(high, D, t=F32), sds(low, D), sds(high, D), sds(8, D, t=F32)),
        scratch_shapes=[pltpu.VMEM((M, D), BF)],
        input_output_aliases={7 + i: i for i in range(len(kept))},
        compiler_params=pltpu.CompilerParams(vmem_limit_bytes=VMEM), cost_estimate=cost(24),
    )(g2, db, qkv, x1, gain, w, w, *kept)

def over_frames(op, rows, slot):
    shift = slot
    while shift < LANES:
        rows = op(rows, pltpu.roll(rows, shift, 1))
        shift *= 2
    return rows

def tf_kernel(x_ref, gain_ref, shift_ref, wqkv_ref, wproj_ref, wfc_ref, hb_ref, wb_ref, fcb_ref,
              a_ref, qkv_ref, p_ref, o_ref, y_ref, x1_ref, all_ref, prod_ref, xs_ref, e_ref, b_ref, *, fb, nb, frames, slot, head, scale):
    M, D = x_ref.shape
    P = M // fb
    step = pl.program_id(0)
    @pl.when(step == 0)
    def _():
        fill_tables(e_ref, b_ref, slot, head)
    @pl.when(step < nb)
    def _():
        x = x_ref[...].astype(F32)
        unit, _ = norm_stats(x)
        a = (unit * gain_ref[...] + shift_ref[...]).astype(BF)
        a_ref[...] = a
        qkv_store(a, wqkv_ref[...], hb_ref, qkv_ref, slice(0, M), D)
        all_ref[pl.ds(pl.multiple_of(step * M, M), M), :] = qkv_ref[...]
        xs_ref[pl.ds(pl.multiple_of(step * M, M), M), :] = x_ref[...]
    @pl.when(step >= nb)
    def _():
        base = pl.multiple_of((step - nb) * M, M)
        for f in range(fb):
            q = all_ref[pl.ds(base + f * P, P), :D]
            for g in range(frames):
                prod_ref[f * P:(f + 1) * P, g * D:(g + 1) * D] = q * all_ref[g * P:(g + 1) * P, D:2 * D]
        s = mm(prod_ref[...], e_ref[...], 1, 0) * scale
        p = jnp.exp(s - over_frames(jnp.maximum, s, slot))
        p = p * (1.0 / over_frames(jnp.add, p, slot))
        p_ref[...] = p
        low = p.astype(BF)
        o = [None] * fb
        for g in range(frames):
            wide = mm(low, b_ref[:, g * D:(g + 1) * D], 1, 0)
            v = all_ref[g * P:(g + 1) * P, 2 * D:].astype(F32)
            for f in range(fb):
                part = wide[f * P:(f + 1) * P] * v
                o[f] = part if g == 0 else o[f] + part
        for f in range(fb):
            o_ref[f * P:(f + 1) * P, :] = o[f].astype(BF)
        y = (mm(o_ref[...], wproj_ref[...], 1, 1) + wb_ref[...]).astype(BF)
        y_ref[...] = y
        z = (mm(y, wfc_ref[...], 1, 0) + fcb_ref[...]).astype(BF)
        x1_ref[...] = xs_ref[pl.ds(base, M), :].astype(F32) + z.astype(F32)

def fill_tables(e_ref, b_ref, slot, head):
    D = e_ref.shape[0] * slot // LANES
    for g in range(LANES // slot):
        for ref, at, wide in ((e_ref, 1, 0), (b_ref, 0, 1)):
            shape = (D, LANES) if wide == 0 else (LANES, D)
            lane = lax.broadcasted_iota(jnp.int32, shape, at)
            feature = lax.broadcasted_iota(jnp.int32, shape, wide)
            hit = ((lane // slot == g) & (lane % slot == feature // head)).astype(F32).astype(BF)
            if wide == 0:
                ref[g * D:(g + 1) * D, :] = hit
            else:
                ref[:, g * D:(g + 1) * D] = hit

def temporal_forward(x, gain, shift, w, hb, wb, fcb, *, frames, head, scale, fb=4):
    T, D = x.shape
    M = T // frames * fb
    nb = frames // fb
    first = lambda w: pl.BlockSpec((M, w), lambda j: (jnp.minimum(j, nb - 1), 0))
    last = lambda w: pl.BlockSpec((M, w), lambda j: (jnp.maximum(j - nb, 0), 0))
    return call(partial(tf_kernel, fb=fb, nb=nb, frames=frames, slot=LANES // frames, head=head, scale=scale), 22, 2 * nb,
        [first(D), once(1, D), once(1, D), column(D, 3 * D, 0), column(D, D, 3), column(D, D, 4), once(2, D), once(1, D), once(1, D)],
        [first(D), first(3 * D), last(LANES), last(D), last(D), last(D)],
        (sds(T, D), sds(T, 3 * D), sds(T, LANES, t=F32), sds(T, D), sds(T, D), sds(T, D, t=F32)),
        [pltpu.VMEM((T, 3 * D), BF), pltpu.VMEM((M, frames * D), BF), pltpu.VMEM((T, D), BF),
         pltpu.VMEM((frames * D, LANES), BF), pltpu.VMEM((LANES, frames * D), BF)])(
        x, gain, shift, w, w, w, hb, wb, fcb)

def zero_first(*refs):
    @pl.when(pl.program_id(0) == 0)
    def _():
        for ref in refs:
            ref[...] = jnp.zeros_like(ref)

def pull_kernel(dz_ref, wproj_ref, wfc_ref, dy_ref, do_ref, sums_ref):
    zero_first(sums_ref)
    dy = mm(dz_ref[...], wfc_ref[...], 1, 1).astype(BF)
    dy_ref[...] = dy
    add_sum(sums_ref, 4, dy)
    do_ref[...] = mm(dy, wproj_ref[...], 1, 0).astype(BF)

def temporal_pull(dz, w, *, blocks=2):
    T, D = dz.shape
    blk = pl.BlockSpec((T // blocks, D), lambda j: (j, 0))
    return call(pull_kernel, 4, blocks, [blk, column(D, D, 3), column(D, D, 4)], [blk, blk, once(8, D)],
                (sds(T, D), sds(T, D), sds(8, D, t=F32)))(dz, w, w)

def tb_kernel(do_ref, qkv_ref, p_ref, dqkv_ref, sums_ref, dk_ref, dv_ref, prod_ref, e_ref, b_ref, *, fb, nb, frames, slot, head, scale):
    M = p_ref.shape[0]
    T, D = do_ref.shape
    P = M // fb
    step = pl.program_id(0)
    zero_first(sums_ref, dk_ref, dv_ref)
    @pl.when(step == 0)
    def _():
        fill_tables(e_ref, b_ref, slot, head)
    base = pl.multiple_of(step * M, M)
    for f in range(fb):
        do = do_ref[pl.ds(base + f * P, P), :]
        for g in range(frames):
            prod_ref[f * P:(f + 1) * P, g * D:(g + 1) * D] = do * qkv_ref[g * P:(g + 1) * P, 2 * D:]
    dp = mm(prod_ref[...], e_ref[...], 1, 0)
    p = p_ref[...]
    ds = (p * (dp - over_frames(jnp.add, p * dp, slot))).astype(BF)
    low = p.astype(BF)
    dq = [0.0] * fb
    for g in range(frames):
        gr = slice(g * P, (g + 1) * P)
        wide_p = mm(low, b_ref[:, g * D:(g + 1) * D], 1, 0)
        wide_s = mm(ds, b_ref[:, g * D:(g + 1) * D], 1, 0)
        k = qkv_ref[gr, D:2 * D].astype(F32)
        dk, dv = dk_ref[gr, :], dv_ref[gr, :]
        for f in range(fb):
            fr = pl.ds(base + f * P, P)
            wp, ws = wide_p[f * P:(f + 1) * P], wide_s[f * P:(f + 1) * P]
            dv = dv + wp * do_ref[fr, :].astype(F32)
            dk = dk + ws * qkv_ref[fr, :D].astype(F32)
            dq[f] = dq[f] + ws * k
        dk_ref[gr, :] = dk
        dv_ref[gr, :] = dv
    for f in range(fb):
        low = (dq[f] * scale).astype(BF)
        add_sum(sums_ref, 2, low)
        dqkv_ref[pl.ds(base + f * P, P), :D] = low
    @pl.when(step == nb - 1)
    def _():
        for g in range(frames):
            gr = slice(g * P, (g + 1) * P)
            dqkv_ref[gr, D:2 * D] = (dk_ref[gr, :] * scale).astype(BF)
            low = dv_ref[gr, :].astype(BF)
            add_sum(sums_ref, 3, low)
            dqkv_ref[gr, 2 * D:] = low

def temporal_backward(do, qkv, p, *, frames, head, scale, fb=4):
    T, D = do.shape
    M = T // frames * fb
    nb = frames // fb
    return call(partial(tb_kernel, fb=fb, nb=nb, frames=frames, slot=LANES // frames, head=head, scale=scale), 20, nb,
        [once(T, D), once(T, 3 * D), pl.BlockSpec((M, LANES), lambda j: (j, 0))],
        [once(T, 3 * D), once(8, D)], (sds(T, 3 * D), sds(8, D, t=F32)),
        [pltpu.VMEM((T, D), F32), pltpu.VMEM((T, D), F32), pltpu.VMEM((M, frames * D), BF),
         pltpu.VMEM((frames * D, LANES), BF), pltpu.VMEM((LANES, frames * D), BF)])(do, qkv, p)

def end_kernel(dqkv_ref, x_ref, g1_ref, gain_ref, wqkv_ref, out_ref, sums_ref):
    zero_first(sums_ref)
    da = mm(dqkv_ref[...], wqkv_ref[...], 1, 1)
    out = norm_back_store(x_ref[...].astype(F32), gain_ref[...], da, g1_ref[...], sums_ref, 0)
    out_ref[...] = out.astype(BF)

def temporal_end(dqkv, x, g1, gain, w, *, blocks=2):
    T, D = x.shape
    blk = lambda w: pl.BlockSpec((T // blocks, w), lambda j: (j, 0))
    return call(end_kernel, 7, blocks, [blk(3 * D), blk(D), blk(D), once(1, D), column(D, 3 * D, 0)], [blk(D), once(8, D)],
                (sds(T, D), sds(8, D, t=F32)))(dqkv, x, g1, gain, w)

def wg_kernel(core_ref, *refs, starts, counts, halves, rows):
    n = sum(counts)
    many_out = 2 if rows else 1
    a_refs, b_refs, out_refs, t_refs = refs[:n], refs[n:2 * n], refs[2 * n:2 * n + many_out], refs[2 * n + many_out:]
    step = pl.program_id(0)
    at = 0
    for i, many in enumerate(counts):
        mine = range(at, at + many)
        at += many
        @pl.when(step == starts[i])
        def _():
            for t_ref, n_at in zip(t_refs, mine):
                t_ref[...] = a_refs[n_at][...].T
        stop = starts[i + 1] if i + 1 < len(counts) else step + 1
        @pl.when((step >= starts[i]) & (step < stop))
        def _():
            res = sum(mm(t_ref[...], b_refs[n_at][...], 1, 0) for t_ref, n_at in zip(t_refs, mine))
            if rows:
                parts = res.reshape(-1, halves, rows, res.shape[-1])
                low, high = [parts[:, h].reshape(-1, res.shape[-1]) for h in range(2)]
                first = core_ref[0, 0] == 0
                out_refs[0][...] = jnp.where(first, low, high).astype(BF)
                out_refs[1][...] = jnp.where(first, high, low).astype(BF)
            else:
                out_refs[0][...] = res.astype(BF)

def weight_grads(pairs, core, halves, rows, us):
    D = pairs[0][0][0].shape[1]
    starts, steps, specs, b_specs = [], 0, [], []
    for many_a, many_b in pairs:
        starts.append(steps)
        chunks = many_b[0].shape[1] // D
        for a in many_a:
            specs.append(once(*a.shape))
            b_specs.append(chunk_spec(a.shape[0], D, steps, chunks))
        steps += chunks
    cols = steps * D
    fits = rows % 8 == 0 and halves == 2
    groups = 2 if fits else 1
    counts = [len(many_a) for many_a, _ in pairs]
    lefts = [a for many_a, _ in pairs for a in many_a]
    rights = [b for _, many_b in pairs for b in many_b]
    out = call(partial(wg_kernel, starts=starts, counts=counts, halves=halves, rows=rows if fits else 0), us, steps,
        [pl.BlockSpec(memory_space=pltpu.SMEM)] + specs + b_specs,
        [pl.BlockSpec((D // groups, D), lambda j: (0, j))] * groups, [sds(D // groups, cols)] * groups,
        [pltpu.VMEM((D, a.shape[0]), BF) for a in pairs[0][0]])(core.reshape(1, 1), *lefts, *rights)
    if fits:
        return [part.reshape(-1, rows, cols) for part in out]
    parts = jnp.swapaxes(out[0].reshape(-1, halves, rows, cols), 0, 1)
    return [lax.dynamic_index_in_dim(parts, core ^ d, 0, keepdims=False) for d in range(halves)]

def chunk_spec(rows, cols, start, many):
    return pl.BlockSpec((rows, cols), lambda j: (0, jnp.clip(j - start, 0, many - 1)))


def exchange(pieces, axis):
    size = len(pieces)
    return [pieces[0]] + [
        lax.ppermute(pieces[d], axis, [(i, i ^ d) for i in range(size)]) for d in range(1, size)
    ]


def in_order(pieces, axis, step=1):
    while step < len(pieces):
        swap = (lax.axis_index(axis) // step) % 2 == 1
        pieces = [jnp.where(swap, pieces[c ^ step], pieces[c]) for c in range(len(pieces))]
        step *= 2
    return pieces


def collect(array, axis, at=0, hold=()):
    pieces = exchange([array] * lax.axis_size(axis), axis)
    pieces = pieces[:1] + [after(piece, *hold) for piece in pieces[1:]]
    return jnp.stack(in_order(pieces, axis), axis=at)


def partner(array, axis, step):
    size = lax.axis_size(axis)
    return lax.ppermute(array, axis, [(i, i ^ step) for i in range(size)])


def far_first(array, axis):
    size = lax.axis_size(axis)
    step = size // 2
    out = array[None]
    while step:
        other = partner(out, axis, step)
        low = (lax.axis_index(axis) // step) % 2 == 0
        out = jnp.stack((jnp.where(low, out, other), jnp.where(low, other, out)), axis=1)
        out = out.reshape((-1,) + array.shape)
        step //= 2
    return out


def bit_step(array, axis, step, hold):
    blocks = array.reshape((-1, 2) + array.shape[1:])
    mine = (lax.axis_index(axis) // step) % 2
    send = lax.dynamic_index_in_dim(blocks, 1 - mine, 1, keepdims=False)
    keep = lax.dynamic_index_in_dim(blocks, mine, 1, keepdims=False)
    came = after(partner(send, axis, step), hold)
    return (keep.astype(F32) + came.astype(F32)).astype(BF)


def later_bits(array, axis, hold):
    step = 2
    while step < lax.axis_size(axis):
        array = bit_step(array, axis, step, hold)
        step *= 2
    return array[0]


def split_off(array, axis):
    place = lax.axis_index(axis)
    pieces = [
        lax.dynamic_index_in_dim(array, place ^ d, 0, keepdims=False)
        for d in range(lax.axis_size(axis))
    ]
    return exchange(pieces[:1] + [piece.astype(BF) for piece in pieces[1:]], axis)


def added(pieces, *hold):
    out = pieces[0].astype(F32)
    for piece in pieces[1:]:
        out = out + after(piece, *hold).astype(F32)
    return out


def shed(array, axis, hold=()):
    return added(split_off(array, axis), *hold)


def shed_at_once(array, axis, *hold):
    came = lax.all_to_all(array.astype(BF), axis, split_axis=0, concat_axis=0, tiled=True)
    came = after(came, *hold)
    return jnp.sum(came.astype(F32), axis=0)


def after(array, *others):
    return lax.optimization_barrier((array,) + others)[0]


def plus_others(array, axis):
    came = exchange([array] * lax.axis_size(axis), axis)
    return sum(came[1:], came[0])


def local(
    clips_in,
    valid_clips,
    norm_gains,
    norm_shifts,
    temporal_qkv,
    temporal_proj,
    temporal_fc,
    spatial_qkv,
    spatial_proj,
    mlp_in,
    mlp_out,
    head_bias,
    width_bias,
    fc_bias,
    hidden_bias,
    cotangent,
):
    held, frames_held, places, width = clips_in.shape
    head = width // HEADS
    scale = head ** (-0.5)
    across = lax.axis_size("context")
    halves = lax.axis_size("tensor")
    place = lax.axis_index("context")
    own_rows = temporal_qkv.shape[0]
    in_rows, in_cols = mlp_in.shape
    spread = held % across == 0
    clips = held // across if spread else held
    share = 1.0 if spread else 1.0 / across
    frames = frames_held * across
    first_places = places // 32 * 16
    cuts = (slice(0, first_places), slice(first_places, places))

    def to_clips(array):
        array = jnp.swapaxes(array, 1, 2)
        if spread:
            array = lax.all_to_all(array, "context", split_axis=0, concat_axis=0, tiled=True)
            return array.reshape((across, clips) + array.shape[1:])
        return lax.all_gather(array, "context", axis=0)

    def fill(array):
        array = jnp.swapaxes(array, 1, 2).reshape(frames, array.shape[1], width)
        array = jnp.pad(array, ((0, 0), (0, -array.shape[1] % 16), (0, 0)))
        return array.reshape(-1, width)

    def by_place(array, real):
        array = array.reshape(across, frames_held, -1, width)[:, :, :real]
        return jnp.swapaxes(array, 1, 2)

    def from_clips(array):
        if spread:
            array = lax.all_to_all(array, "context", split_axis=0, concat_axis=0, tiled=True)
        else:
            array = lax.dynamic_slice_in_dim(array, place, 1, 0)
        return array

    def send_back(array):
        array = by_place(array, places)
        if spread:
            return split_off(array, "context")
        return [lax.dynamic_index_in_dim(array, place, 0, keepdims=False)]

    def sent_back(pieces):
        return jnp.swapaxes(jnp.stack(in_order(pieces, "context")), 1, 2)

    if spread:
        valid = lax.dynamic_slice_in_dim(valid_clips, place * clips, clips, 0)
    else:
        valid = valid_clips
    keep = valid.astype(F32)

    def flat3(weight):
        return weight.reshape(own_rows, 3 * width)

    def by_shard(d):
        return d.reshape((lax.axis_size("shard"), across) + d.shape[1:])

    t_own = jnp.concatenate((flat3(temporal_qkv), temporal_proj, temporal_fc), axis=1).astype(BF)
    s_own = jnp.concatenate((flat3(spatial_qkv), spatial_proj), axis=1).astype(BF)
    mlp_own = jnp.concatenate((mlp_in, mlp_out), axis=0).astype(BF)
    clip_parts = [clips_in[:, :, cut] for cut in cuts]
    pull_parts = [cotangent[:, :, cut] for cut in cuts]
    gain = [norm_gains[i : i + 1] for i in range(3)]
    shift = [norm_shifts[i : i + 1] for i in range(3)]
    wide = [width_bias[i : i + 1] for i in range(3)]
    head_pairs, fc_row, hidden_row = [head_bias[0], head_bias[1]], fc_bias[None], hidden_bias[None]
    early = clip_parts + pull_parts + gain + shift + wide + head_pairs + [fc_row, hidden_row]
    first = collect(jnp.concatenate((t_own, s_own), axis=1), "context", hold=early)
    t_first, s_first = first[..., : t_own.shape[1]], first[..., t_own.shape[1] :]
    rows_a = to_clips(after(clip_parts[0], first))
    mlp_all = lax.all_gather(after(mlp_own, first), ALL, axis=0, tiled=True)
    mlp_all = mlp_all.reshape(-1, halves, 2 * in_rows, in_cols)
    t_chips = collect(t_first, "shard", hold=(rows_a,))
    t_all = collect(t_chips, "tensor", 2).reshape(-1, t_own.shape[1])
    rows_b = to_clips(after(clip_parts[1], rows_a))
    pull_a = to_clips(after(pull_parts[0], rows_b))
    pull_b = to_clips(after(pull_parts[1], pull_a))

    def one_clip(x_a, x_b, pull_a, pull_b, keep_one):
        sizes = dict(frames=frames, head=head, scale=scale)
        forward_t = partial(
            temporal_forward, gain=gain[0], shift=shift[0], w=t_all, hb=head_pairs[0], wb=wide[0],
            fcb=fc_row, **sizes,
        )
        x_a = fill(x_a)
        at_a, qkv_a, probs_a, o_a, y_a, x1_a = forward_t(x_a)
        s_all = collect(after(s_first, rows_a), "shard", hold=(x1_a,))
        x_b = fill(after(x_b, x1_a, s_all))
        at_b, qkv_b, probs_b, o_b, y_b, x1_b = forward_t(x_b)
        s_all = collect(s_all, "tensor", 2, hold=(x1_b,)).reshape(-1, s_own.shape[1])
        pull_a = after(pull_a, x1_b)
        sizes_s = dict(sizes, real=places)
        a_s, qkv_s, o_s, x2, x1 = spatial_forward(
            x1_a, after(x1_b, pull_a), gain[1], shift[1], s_all, head_pairs[1], wide[1], **sizes_s
        )
        out, g2, db, d_m, d_hidden, sums_m = mlp(
            x2, fill(pull_a), fill(after(pull_b, x2)), keep_one.reshape(1, 1), gain[2], shift[2], mlp_all, hidden_row, wide[2],
            frames=frames,
        )
        back_s = partial(spatial_backward, gain=gain[1], w=s_all, first=first_places, **sizes_s)
        core = lax.axis_index("tensor")

        def grads_of(pairs, us):
            pieces = weight_grads(pairs, core, halves, own_rows, us)
            return [(share * p).astype(BF) for p in pieces] if share != 1.0 else pieces

        d_m = (share * d_m if share != 1.0 else d_m).astype(BF).reshape(-1, in_cols)
        d_m = lax.psum_scatter(d_m, ALL, scatter_dimension=0, tiled=True)
        back = send_back(out)
        half = back_s(g2, db, qkv_s, x1, part=0)
        tied = after(db, half[0], *back[1:2])
        d_qkv_s, g1_a, g1_b, dz_a, dz_b, sums_s = back_s(g2, tied, qkv_s, x1, part=1, held=half)
        sums_s = sums_s + half[5]
        tied = after(d_qkv_s, *back[2:3])
        d_s = grads_of([([a_s], [tied]), ([db], [o_s])], us=12)
        tied = after(dz_a, *d_s)
        d_s = exchange(d_s, "tensor")
        dy_a, do_a, sums_y = temporal_pull(tied, t_all)
        dy_b, do_b, sums_yb = temporal_pull(after(dz_b, dy_a), t_all)
        d_s = added(d_s, dy_b).astype(BF)
        tied = after(dy_b, d_s, *back[3:])
        d_s = split_off(by_shard(d_s), "shard")
        d_r = grads_of([([dy_a, tied], [o_a, o_b]), ([y_a, y_b], [dz_a, dz_b])], us=6)
        tied = after(do_a, *d_r)
        d_r = exchange(d_r, "tensor")
        d_qkv_a, sums_q = temporal_backward(tied, qkv_a, probs_a, **sizes)
        d_r = added(d_r, d_qkv_a).astype(BF)
        into_a, sums_x = temporal_end(after(d_qkv_a, d_r), x_a, g1_a, gain[0], t_all)
        d_s = added(d_s, into_a).astype(BF)
        swap_a = by_place(into_a, first_places)
        into_a = from_clips(swap_a)
        tied = after(do_b, swap_a, d_s)
        d_s = split_off(d_s, "context")
        d_qkv_b, sums_qb = temporal_backward(tied, qkv_b, probs_b, **sizes)
        d_r_first = bit_step(by_shard(d_r), "shard", 1, d_qkv_b)
        d_q = grads_of([([at_a, at_b], [d_qkv_a, after(d_qkv_b, d_r_first)])], us=9)
        d_m = d_m.astype(F32)
        d_r = later_bits(d_r_first, "shard", d_q[0])
        tied = lax.optimization_barrier((d_qkv_b, *d_q, into_a, d_r, d_m))[0]
        d_q = exchange(d_q, "tensor")
        into_b, sums_xb = temporal_end(tied, x_b, g1_b, gain[0], t_all)
        swap_b = by_place(into_b, places - first_places)
        d_s = added(d_s, into_b)
        into_b = from_clips(after(swap_b, into_a, d_s))
        t, m = sums_y + sums_yb + sums_q + sums_qb + sums_x + sums_xb, sums_m
        rows = [v[n : n + 1] for n in (0, 1) for v in (t, sums_s, m)] + [t[2:4], sums_s[2:4]]
        rows = rows + [t[4:5], m[3:4], m[2:3], sums_s[4:5], d_hidden.reshape(-1, width)]
        small = plus_others(share * jnp.concatenate(rows, axis=0), "tensor")
        d_q = added(d_q, swap_b).astype(BF)
        small = plus_others(small, "shard")
        d_q = added(split_off(by_shard(d_q), "shard"), small).astype(BF)
        output = sent_back([after(piece, d_q) for piece in back])
        small = plus_others(after(small, d_q), "context")
        d_q = shed(jnp.concatenate((d_r, d_q), axis=-1), "context")
        into = jnp.swapaxes(jnp.concatenate((into_a, after(into_b, output, d_q)), axis=1), 1, 2)
        return output, into, (d_q, d_s, d_m, small)

    given = (rows_a, rows_b, pull_a, pull_b)
    parts = [one_clip(*[v[:, i] for v in given], keep[i]) for i in range(clips)]
    output, input_grad = [
        jnp.stack([part[n] for part in parts], axis=1).reshape(clips_in.shape) for n in (0, 1)
    ]
    grads = parts[0][2]
    for part in parts[1:]:
        grads = jax.tree.map(jnp.add, grads, part[2])
    d_t, d_s, d_mlp, small = grads
    d_t_rest, d_t_qkv = d_t[:, : 2 * width], d_t[:, 2 * width :]
    return (
        output,
        input_grad,
        small[0:3],
        small[3:6],
        d_t_qkv.reshape(own_rows, 3, width),
        d_t_rest[:, :width],
        d_t_rest[:, width:],
        d_s[:, : 3 * width].reshape(own_rows, 3, width),
        d_s[:, 3 * width :],
        d_mlp[:in_rows],
        d_mlp[in_rows:],
        small[6:10].reshape(2, 2, width),
        small[10:13],
        small[13],
        small[14:].reshape(-1),
    )


def solution(mesh):
    clip = P(("shard", "tensor"), "context", None, None)
    row, block = P(ALL, None), P(("shard", "context"), "tensor")
    deep, whole = P(ALL, None, None), P()
    weights = (deep, row, row, deep, row, block, block)
    in_specs = (clip, P(("shard", "tensor")), whole, whole) + weights + (whole,) * 4 + (clip,)
    out_specs = (clip, clip, whole, whole) + weights + (whole,) * 4
    return jax.shard_map(local, mesh=mesh, in_specs=in_specs, out_specs=out_specs, check_vma=False)
```

```python
from functools import partial

import jax
import jax.numpy as jnp
from jax import lax
from jax.experimental import pallas as pl
from jax.experimental.pallas import tpu as pltpu
from jax.sharding import PartitionSpec as P

HEADS = 12
EPS = 1e-05
ALL = ("shard", "context", "tensor")
BF = jnp.bfloat16
F32 = jnp.float32
VMEM = 60 * 2**20

def mm(left, right, left_dim, right_dim):
    return lax.dot_general(left, right, (((left_dim,), (right_dim,)), ((), ())), preferred_element_type=F32)

def norm_stats(rows):
    centered = rows - jnp.mean(rows, axis=-1, keepdims=True)
    inv = lax.rsqrt(jnp.mean(centered * centered, axis=-1, keepdims=True) + EPS)
    return centered * inv, inv

def mlp_kernel(x_ref, cota_ref, cotb_ref, keep_ref, gain_ref, shift_ref, w_ref, hb_ref, wb_ref,
               out_ref, g2_ref, db_ref, dw_ref, dhb_ref, sums_ref,
               a_ref, at_ref, dm_ref, dmt_ref, m_ref, da_ref, h_ref, du_ref, *, rb, chunks, frames):
    step = pl.program_id(0)
    T, D = x_ref.shape
    cot_ref = out_ref
    nb = T // rb
    blocks, _, both, hc = w_ref.shape
    half = both // 2

    @pl.when(step == 0)
    def _():
        merge(cot_ref, (cota_ref, cotb_ref), frames)
        def body(i, c):
            r = pl.ds(pl.multiple_of(i * rb, 16), rb)
            unit, _ = norm_stats(x_ref[r, :])
            a = (unit * gain_ref[...] + shift_ref[...]).astype(BF)
            a_ref[r, :] = a
            dm = (keep_ref[0, 0] * cot_ref[r, :].astype(F32)).astype(BF)
            dm_ref[r, :] = dm
            return c
        lax.fori_loop(0, nb, body, 0)
        at_ref[...] = a_ref[...].T
        dmt_ref[...] = dm_ref[...].T

    win = w_ref[:, 0, :half, :].reshape(D, hc)
    wout = w_ref[:, 0, half:, :].reshape(D, hc)
    hb = hb_ref[...]
    tot = jnp.zeros((1, hc), F32)
    for i in range(nb):
        r = slice(i * rb, (i + 1) * rb)
        u = mm(a_ref[r, :], win, 1, 0) + hb
        cdf = 0.5 * (1.0 + lax.erf(u * (2 ** -0.5)))
        h = (u * cdf).astype(BF)
        pdf = jnp.exp(-0.5 * u * u) * ((2 * jnp.pi) ** -0.5)
        dh = mm(dm_ref[r, :], wout, 1, 0)
        du = ((cdf + u * pdf) * dh).astype(BF)
        h_ref[r, :] = h
        du_ref[r, :] = du
        tot += jnp.sum(du.astype(F32), axis=0, keepdims=True)
        m = mm(h, wout, 1, 1)
        da = mm(du, win, 1, 1)
        @pl.when(step == 0)
        def _():
            m_ref[r, :] = m
            da_ref[r, :] = da
        @pl.when(step > 0)
        def _():
            m_ref[r, :] += m
            da_ref[r, :] += da
    dhb_ref[...] = tot
    dw_ref[:, 0, :half, :] = mm(at_ref[...], du_ref[...], 1, 0).astype(BF).reshape(blocks, half, hc)
    dw_ref[:, 0, half:, :] = mm(dmt_ref[...], h_ref[...], 1, 0).astype(BF).reshape(blocks, half, hc)

    @pl.when(step == chunks - 1)
    def _():
        k = keep_ref[0, 0]
        def body(i, c):
            r = pl.ds(pl.multiple_of(i * rb, 16), rb)
            x = x_ref[r, :]
            g3 = k * cot_ref[r, :].astype(F32)
            out_ref[r, :] = (k * (x + (m_ref[r, :] + wb_ref[...]))).astype(BF)
            da = da_ref[r, :]
            unit, inv = norm_stats(x)
            sc = da * gain_ref[...]
            into = inv * (sc - jnp.mean(sc, axis=-1, keepdims=True) - unit * jnp.mean(sc * unit, axis=-1, keepdims=True))
            g2 = g3 + into
            g2_ref[r, :] = g2
            low = g2.astype(BF)
            db_ref[r, :] = low
            return (c[0] + jnp.sum(da * unit, axis=0, keepdims=True),
                    c[1] + jnp.sum(da, axis=0, keepdims=True),
                    c[2] + jnp.sum(dm_ref[r, :].astype(F32), axis=0, keepdims=True),
                    c[3] + jnp.sum(low.astype(F32), axis=0, keepdims=True))
        z = jnp.zeros((1, D), F32)
        c = lax.fori_loop(0, nb, body, (z, z, z, z))
        for j in range(4):
            sums_ref[j:j+1, :] = c[j]

def mlp(x2, cot_a, cot_b, keep, gain, shift, w4, hb, wb, *, frames):
    T, D = x2.shape
    B, H2, R, C = w4.shape
    rb = T // 4 if T % 64 == 0 else T
    hc = next(w for w in (768, 512, 384, 256, 128) if C % w == 0)
    per = C // hc
    chunks = H2 * per
    full = lambda *s: pl.BlockSpec(s, lambda j: (0,) * len(s), pipeline_mode=pl.Buffered(1))
    wspec = pl.BlockSpec((B, 1, R, hc), lambda j: (0, j // per, 0, j % per))
    hspec = pl.BlockSpec((1, hc), lambda j: (0, j))
    return pl.pallas_call(
        partial(mlp_kernel, rb=rb, chunks=chunks, frames=frames),
        grid=(chunks,),
        in_specs=[full(T, D), full(*cot_a.shape), full(*cot_b.shape), pl.BlockSpec(memory_space=pltpu.SMEM), full(1, D), full(1, D), wspec, hspec, full(1, D)],
        out_specs=[full(T, D), full(T, D), full(T, D), wspec, hspec, full(8, D)],
        out_shape=(sds(T, D), sds(T, D, t=F32), sds(T, D), sds(*w4.shape), sds(1, H2 * C, t=F32), sds(8, D, t=F32)),
        scratch_shapes=[pltpu.VMEM((T, D), BF), pltpu.VMEM((D, T), BF), pltpu.VMEM((T, D), BF), pltpu.VMEM((D, T), BF),
                        pltpu.VMEM((T, D), F32), pltpu.VMEM((T, D), F32), pltpu.VMEM((T, hc), BF), pltpu.VMEM((T, hc), BF)],
        compiler_params=pltpu.CompilerParams(vmem_limit_bytes=VMEM),
        cost_estimate=cost(75),
    )(x2, cot_a, cot_b, keep, gain, shift, w4, hb, wb)
LANES = 128
LOW = -1e30

def once(*s):
    return pl.BlockSpec(s, lambda j: (0,) * len(s), pipeline_mode=pl.Buffered(1))

def column(rows, cols, at):
    return pl.BlockSpec((rows, cols), lambda j: (0, at), pipeline_mode=pl.Buffered(1))

def sds(*s, t=BF):
    return jax.ShapeDtypeStruct(s, t)

def cost(us):
    return pl.CostEstimate(flops=us * 10**9, bytes_accessed=0, transcendentals=0)

def call(body, us, grid, ins, outs, shapes, scratch=()):
    return pl.pallas_call(body, grid=(grid,), in_specs=ins, out_specs=outs, out_shape=shapes, scratch_shapes=list(scratch),
                          compiler_params=pltpu.CompilerParams(vmem_limit_bytes=VMEM), cost_estimate=cost(us))

def qkv_store(a, wqkv, hb_ref, dst, rows, D):
    packed = mm(a, wqkv, 1, 0)
    dst[rows, :D] = (packed[:, :D] + hb_ref[0:1, :]).astype(BF)
    dst[rows, D:2 * D] = packed[:, D:2 * D].astype(BF)
    dst[rows, 2 * D:] = (packed[:, 2 * D:] + hb_ref[1:2, :]).astype(BF)

def lane_masks(head, value):
    lane = lax.broadcasted_iota(jnp.int32, (1, LANES), 1)
    return [jnp.where(lane // head == i, value, 0.0).astype(BF) for i in range(LANES // head)]

def merge(dst_ref, parts, fb):
    P = dst_ref.shape[0] // fb
    for f in range(fb):
        at = f * P
        for part in parts:
            n = part.shape[0] // fb
            dst_ref[at:at + n, :] = part[f * n:(f + 1) * n, :]
            at += n

def split(value, dst_refs, fb):
    P = value.shape[0] // fb
    for f in range(fb):
        at = f * P
        for dst in dst_refs:
            n = dst.shape[0] // fb
            dst[f * n:(f + 1) * n, :] = value[at:at + n, :]
            at += n

def sf_kernel(xa_ref, xb_ref, gain_ref, shift_ref, wqkv_ref, wproj_ref, hb_ref, wb_ref, a_ref, qkv_ref, o_ref, x2_ref, x_ref, *, fb, real, head, scale):
    M, D = x_ref.shape
    P = M // fb
    merge(x_ref, (xa_ref, xb_ref), fb)
    unit, _ = norm_stats(x_ref[...])
    a = (unit * gain_ref[...] + shift_ref[...]).astype(BF)
    a_ref[...] = a
    qkv_store(a, wqkv_ref[...], hb_ref, qkv_ref, slice(0, M), D)
    col = lax.broadcasted_iota(jnp.int32, (1, P), 1)
    hide = jnp.where(col < real, 0.0, LOW)
    ones = lane_masks(head, 1.0)
    for f in range(fb):
        r = slice(f * P, (f + 1) * P)
        for j in range(D // LANES):
            q = qkv_ref[r, j * LANES:(j + 1) * LANES]
            k = qkv_ref[r, D + j * LANES:D + (j + 1) * LANES]
            v = qkv_ref[r, 2 * D + j * LANES:2 * D + (j + 1) * LANES]
            o = None
            for m in ones:
                s = mm(q * m, k, 1, 1) * scale + hide
                p = jnp.exp(s - jnp.max(s, axis=-1, keepdims=True))
                p = (p * (1.0 / jnp.sum(p, axis=-1, keepdims=True))).astype(BF)
                part = mm(p, v * m, 1, 0)
                o = part if o is None else o + part
            o_ref[r, j * LANES:(j + 1) * LANES] = o.astype(BF)
    x2_ref[...] = x_ref[...] + (mm(o_ref[...], wproj_ref[...], 1, 1) + wb_ref[...])

def frame_blocks(rows, width, at=0):
    return pl.BlockSpec((rows, width), lambda j: (j + at, 0))

def spatial_forward(xa, xb, gain, shift, w, hb, wb, *, frames, real, head, scale, fb=2):
    D = xa.shape[1]
    steps = frames // fb
    T = xa.shape[0] + xb.shape[0]
    blk = lambda width, rows=T: frame_blocks(rows // steps, width)
    return call(partial(sf_kernel, fb=fb, real=real, head=head, scale=scale), 30, steps,
        [blk(D, xa.shape[0]), blk(D, xb.shape[0]), once(1, D), once(1, D), column(D, 3 * D, 0), column(D, D, 3), once(2, D), once(1, D)],
        [blk(D), blk(3 * D), blk(D), blk(D), blk(D)], (sds(T, D), sds(T, 3 * D), sds(T, D), sds(T, D, t=F32), sds(T, D, t=F32)))(
        xa, xb, gain, shift, w, w, hb, wb)

def norm_back_store(x, gain, da, base, sums_ref, at):
    unit, inv = norm_stats(x)
    sc = da * gain
    into = inv * (sc - jnp.mean(sc, axis=-1, keepdims=True) - unit * jnp.mean(sc * unit, axis=-1, keepdims=True))
    sums_ref[at:at + 1, :] += jnp.sum(da * unit, axis=0, keepdims=True)
    sums_ref[at + 1:at + 2, :] += jnp.sum(da, axis=0, keepdims=True)
    return base + into

def add_sum(sums_ref, at, rows):
    sums_ref[at:at + 1, :] += jnp.sum(rows.astype(F32), axis=0, keepdims=True)

def sb_kernel(g2_ref, db_ref, qkv_ref, x_ref, gain_ref, wqkv_ref, wproj_ref, *rest, fb, real, head, scale):
    dqkv_ref, g1a_ref, g1b_ref, dza_ref, dzb_ref, sums_ref, do_ref = rest[-7:]
    M, D = x_ref.shape
    P = M // fb
    @pl.when(pl.program_id(0) == 0)
    def _():
        sums_ref[...] = jnp.zeros_like(sums_ref)
    do_ref[...] = mm(db_ref[...], wproj_ref[...], 1, 0).astype(BF)
    row = lax.broadcasted_iota(jnp.int32, (P, 1), 0)
    hide = jnp.where(row < real, 0.0, LOW)
    ones = lane_masks(head, 1.0)
    for f in range(fb):
        r = slice(f * P, (f + 1) * P)
        for j in range(D // LANES):
            ls = [slice(i * D + j * LANES, i * D + (j + 1) * LANES) for i in range(3)]
            q, k, v = [qkv_ref[r, l] for l in ls]
            do = do_ref[r, ls[0]]
            dq = dk = dv = 0.0
            for m in ones:
                qm = q * m
                dom = do * m
                s = mm(k, qm, 1, 1) * scale + hide
                p = jnp.exp(s - jnp.max(s, axis=0, keepdims=True))
                p = p * (1.0 / jnp.sum(p, axis=0, keepdims=True))
                dp = mm(v, dom, 1, 1)
                ds = (p * (dp - jnp.sum(p * dp, axis=0, keepdims=True))).astype(BF)
                dv = dv + mm(p.astype(BF), dom, 1, 0)
                dk = dk + mm(ds, qm, 1, 0)
                dq = dq + mm(ds, k * m, 0, 0)
            dqkv_ref[r, ls[0]] = (dq * scale).astype(BF)
            dqkv_ref[r, ls[1]] = (dk * scale).astype(BF)
            dqkv_ref[r, ls[2]] = dv.astype(BF)
    add_sum(sums_ref, 2, dqkv_ref[:, :D])
    add_sum(sums_ref, 3, dqkv_ref[:, 2 * D:])
    da = mm(dqkv_ref[...], wqkv_ref[...], 1, 1)
    g1 = norm_back_store(x_ref[...], gain_ref[...], da, g2_ref[...], sums_ref, 0)
    split(g1, (g1a_ref, g1b_ref), fb)
    low = g1.astype(BF)
    split(low, (dza_ref, dzb_ref), fb)
    add_sum(sums_ref, 4, low)

def spatial_backward(g2, db, qkv, x1, *, gain, w, first, frames, real, head, scale, part, held=None, fb=2):
    T, D = x1.shape
    M = T // frames * fb
    nb = frames // fb // 2
    blk = lambda width, rows=M: frame_blocks(rows, width, part * nb)
    kept = [] if held is None else list(held[:5])
    low, high = frames * first, T - frames * first
    ends = [blk(D, first * fb), blk(D, M - first * fb)]
    return pl.pallas_call(
        partial(sb_kernel, fb=fb, real=real, head=head, scale=scale), grid=(nb,),
        in_specs=[blk(D), blk(D), blk(3 * D), blk(D), once(1, D), column(D, 3 * D, 0), column(D, D, 3)]
        + [pl.BlockSpec(memory_space=pl.ANY)] * len(kept),
        out_specs=[blk(3 * D)] + ends + ends + [once(8, D)],
        out_shape=(sds(T, 3 * D), sds(low, D, t=F32), sds(high, D, t=F32), sds(low, D), sds(high, D), sds(8, D, t=F32)),
        scratch_shapes=[pltpu.VMEM((M, D), BF)],
        input_output_aliases={7 + i: i for i in range(len(kept))},
        compiler_params=pltpu.CompilerParams(vmem_limit_bytes=VMEM), cost_estimate=cost(24),
    )(g2, db, qkv, x1, gain, w, w, *kept)

def over_frames(op, rows, slot):
    shift = slot
    while shift < LANES:
        rows = op(rows, pltpu.roll(rows, shift, 1))
        shift *= 2
    return rows

def tf_kernel(x_ref, gain_ref, shift_ref, wqkv_ref, wproj_ref, wfc_ref, hb_ref, wb_ref, fcb_ref,
              a_ref, qkv_ref, p_ref, o_ref, y_ref, x1_ref, all_ref, prod_ref, xs_ref, e_ref, b_ref, *, fb, nb, frames, slot, head, scale):
    M, D = x_ref.shape
    P = M // fb
    step = pl.program_id(0)
    @pl.when(step == 0)
    def _():
        fill_tables(e_ref, b_ref, slot, head)
    @pl.when(step < nb)
    def _():
        x = x_ref[...].astype(F32)
        unit, _ = norm_stats(x)
        a = (unit * gain_ref[...] + shift_ref[...]).astype(BF)
        a_ref[...] = a
        qkv_store(a, wqkv_ref[...], hb_ref, qkv_ref, slice(0, M), D)
        all_ref[pl.ds(pl.multiple_of(step * M, M), M), :] = qkv_ref[...]
        xs_ref[pl.ds(pl.multiple_of(step * M, M), M), :] = x_ref[...]
    @pl.when(step >= nb)
    def _():
        base = pl.multiple_of((step - nb) * M, M)
        for f in range(fb):
            q = all_ref[pl.ds(base + f * P, P), :D]
            for g in range(frames):
                prod_ref[f * P:(f + 1) * P, g * D:(g + 1) * D] = q * all_ref[g * P:(g + 1) * P, D:2 * D]
        s = mm(prod_ref[...], e_ref[...], 1, 0) * scale
        p = jnp.exp(s - over_frames(jnp.maximum, s, slot))
        p = p * (1.0 / over_frames(jnp.add, p, slot))
        p_ref[...] = p
        low = p.astype(BF)
        o = [None] * fb
        for g in range(frames):
            wide = mm(low, b_ref[:, g * D:(g + 1) * D], 1, 0)
            v = all_ref[g * P:(g + 1) * P, 2 * D:].astype(F32)
            for f in range(fb):
                part = wide[f * P:(f + 1) * P] * v
                o[f] = part if g == 0 else o[f] + part
        for f in range(fb):
            o_ref[f * P:(f + 1) * P, :] = o[f].astype(BF)
        y = (mm(o_ref[...], wproj_ref[...], 1, 1) + wb_ref[...]).astype(BF)
        y_ref[...] = y
        z = (mm(y, wfc_ref[...], 1, 0) + fcb_ref[...]).astype(BF)
        x1_ref[...] = xs_ref[pl.ds(base, M), :].astype(F32) + z.astype(F32)

def fill_tables(e_ref, b_ref, slot, head):
    D = e_ref.shape[0] * slot // LANES
    for g in range(LANES // slot):
        for ref, at, wide in ((e_ref, 1, 0), (b_ref, 0, 1)):
            shape = (D, LANES) if wide == 0 else (LANES, D)
            lane = lax.broadcasted_iota(jnp.int32, shape, at)
            feature = lax.broadcasted_iota(jnp.int32, shape, wide)
            hit = ((lane // slot == g) & (lane % slot == feature // head)).astype(F32).astype(BF)
            if wide == 0:
                ref[g * D:(g + 1) * D, :] = hit
            else:
                ref[:, g * D:(g + 1) * D] = hit

def temporal_forward(x, gain, shift, w, hb, wb, fcb, *, frames, head, scale, fb=4):
    T, D = x.shape
    M = T // frames * fb
    nb = frames // fb
    first = lambda w: pl.BlockSpec((M, w), lambda j: (jnp.minimum(j, nb - 1), 0))
    last = lambda w: pl.BlockSpec((M, w), lambda j: (jnp.maximum(j - nb, 0), 0))
    return call(partial(tf_kernel, fb=fb, nb=nb, frames=frames, slot=LANES // frames, head=head, scale=scale), 22, 2 * nb,
        [first(D), once(1, D), once(1, D), column(D, 3 * D, 0), column(D, D, 3), column(D, D, 4), once(2, D), once(1, D), once(1, D)],
        [first(D), first(3 * D), last(LANES), last(D), last(D), last(D)],
        (sds(T, D), sds(T, 3 * D), sds(T, LANES, t=F32), sds(T, D), sds(T, D), sds(T, D, t=F32)),
        [pltpu.VMEM((T, 3 * D), BF), pltpu.VMEM((M, frames * D), BF), pltpu.VMEM((T, D), BF),
         pltpu.VMEM((frames * D, LANES), BF), pltpu.VMEM((LANES, frames * D), BF)])(
        x, gain, shift, w, w, w, hb, wb, fcb)

def zero_first(*refs):
    @pl.when(pl.program_id(0) == 0)
    def _():
        for ref in refs:
            ref[...] = jnp.zeros_like(ref)

def pull_kernel(dz_ref, wproj_ref, wfc_ref, dy_ref, do_ref, sums_ref):
    zero_first(sums_ref)
    dy = mm(dz_ref[...], wfc_ref[...], 1, 1).astype(BF)
    dy_ref[...] = dy
    add_sum(sums_ref, 4, dy)
    do_ref[...] = mm(dy, wproj_ref[...], 1, 0).astype(BF)

def temporal_pull(dz, w, *, blocks=2):
    T, D = dz.shape
    blk = pl.BlockSpec((T // blocks, D), lambda j: (j, 0))
    return call(pull_kernel, 4, blocks, [blk, column(D, D, 3), column(D, D, 4)], [blk, blk, once(8, D)],
                (sds(T, D), sds(T, D), sds(8, D, t=F32)))(dz, w, w)

def tb_kernel(do_ref, qkv_ref, p_ref, dqkv_ref, sums_ref, dk_ref, dv_ref, prod_ref, e_ref, b_ref, *, fb, nb, frames, slot, head, scale):
    M = p_ref.shape[0]
    T, D = do_ref.shape
    P = M // fb
    step = pl.program_id(0)
    zero_first(sums_ref, dk_ref, dv_ref)
    @pl.when(step == 0)
    def _():
        fill_tables(e_ref, b_ref, slot, head)
    base = pl.multiple_of(step * M, M)
    for f in range(fb):
        do = do_ref[pl.ds(base + f * P, P), :]
        for g in range(frames):
            prod_ref[f * P:(f + 1) * P, g * D:(g + 1) * D] = do * qkv_ref[g * P:(g + 1) * P, 2 * D:]
    dp = mm(prod_ref[...], e_ref[...], 1, 0)
    p = p_ref[...]
    ds = (p * (dp - over_frames(jnp.add, p * dp, slot))).astype(BF)
    low = p.astype(BF)
    dq = [0.0] * fb
    for g in range(frames):
        gr = slice(g * P, (g + 1) * P)
        wide_p = mm(low, b_ref[:, g * D:(g + 1) * D], 1, 0)
        wide_s = mm(ds, b_ref[:, g * D:(g + 1) * D], 1, 0)
        k = qkv_ref[gr, D:2 * D].astype(F32)
        dk, dv = dk_ref[gr, :], dv_ref[gr, :]
        for f in range(fb):
            fr = pl.ds(base + f * P, P)
            wp, ws = wide_p[f * P:(f + 1) * P], wide_s[f * P:(f + 1) * P]
            dv = dv + wp * do_ref[fr, :].astype(F32)
            dk = dk + ws * qkv_ref[fr, :D].astype(F32)
            dq[f] = dq[f] + ws * k
        dk_ref[gr, :] = dk
        dv_ref[gr, :] = dv
    for f in range(fb):
        low = (dq[f] * scale).astype(BF)
        add_sum(sums_ref, 2, low)
        dqkv_ref[pl.ds(base + f * P, P), :D] = low
    @pl.when(step == nb - 1)
    def _():
        for g in range(frames):
            gr = slice(g * P, (g + 1) * P)
            dqkv_ref[gr, D:2 * D] = (dk_ref[gr, :] * scale).astype(BF)
            low = dv_ref[gr, :].astype(BF)
            add_sum(sums_ref, 3, low)
            dqkv_ref[gr, 2 * D:] = low

def temporal_backward(do, qkv, p, *, frames, head, scale, fb=4):
    T, D = do.shape
    M = T // frames * fb
    nb = frames // fb
    return call(partial(tb_kernel, fb=fb, nb=nb, frames=frames, slot=LANES // frames, head=head, scale=scale), 20, nb,
        [once(T, D), once(T, 3 * D), pl.BlockSpec((M, LANES), lambda j: (j, 0))],
        [once(T, 3 * D), once(8, D)], (sds(T, 3 * D), sds(8, D, t=F32)),
        [pltpu.VMEM((T, D), F32), pltpu.VMEM((T, D), F32), pltpu.VMEM((M, frames * D), BF),
         pltpu.VMEM((frames * D, LANES), BF), pltpu.VMEM((LANES, frames * D), BF)])(do, qkv, p)

def end_kernel(dqkv_ref, x_ref, g1_ref, gain_ref, wqkv_ref, out_ref, sums_ref):
    zero_first(sums_ref)
    da = mm(dqkv_ref[...], wqkv_ref[...], 1, 1)
    out = norm_back_store(x_ref[...].astype(F32), gain_ref[...], da, g1_ref[...], sums_ref, 0)
    out_ref[...] = out.astype(BF)

def temporal_end(dqkv, x, g1, gain, w, *, blocks=2):
    T, D = x.shape
    blk = lambda w: pl.BlockSpec((T // blocks, w), lambda j: (j, 0))
    return call(end_kernel, 7, blocks, [blk(3 * D), blk(D), blk(D), once(1, D), column(D, 3 * D, 0)], [blk(D), once(8, D)],
                (sds(T, D), sds(8, D, t=F32)))(dqkv, x, g1, gain, w)

def wg_kernel(core_ref, *refs, starts, counts, halves, rows):
    n = sum(counts)
    many_out = 2 if rows else 1
    a_refs, b_refs, out_refs, t_refs = refs[:n], refs[n:2 * n], refs[2 * n:2 * n + many_out], refs[2 * n + many_out:]
    step = pl.program_id(0)
    at = 0
    for i, many in enumerate(counts):
        mine = range(at, at + many)
        at += many
        @pl.when(step == starts[i])
        def _():
            for t_ref, n_at in zip(t_refs, mine):
                t_ref[...] = a_refs[n_at][...].T
        stop = starts[i + 1] if i + 1 < len(counts) else step + 1
        @pl.when((step >= starts[i]) & (step < stop))
        def _():
            res = sum(mm(t_ref[...], b_refs[n_at][...], 1, 0) for t_ref, n_at in zip(t_refs, mine))
            if rows:
                parts = res.reshape(-1, halves, rows, res.shape[-1])
                low, high = [parts[:, h].reshape(-1, res.shape[-1]) for h in range(2)]
                first = core_ref[0, 0] == 0
                out_refs[0][...] = jnp.where(first, low, high).astype(BF)
                out_refs[1][...] = jnp.where(first, high, low).astype(BF)
            else:
                out_refs[0][...] = res.astype(BF)

def weight_grads(pairs, core, halves, rows, us):
    D = pairs[0][0][0].shape[1]
    starts, steps, specs, b_specs = [], 0, [], []
    for many_a, many_b in pairs:
        starts.append(steps)
        chunks = many_b[0].shape[1] // D
        for a in many_a:
            specs.append(once(*a.shape))
            b_specs.append(chunk_spec(a.shape[0], D, steps, chunks))
        steps += chunks
    cols = steps * D
    fits = rows % 8 == 0 and halves == 2
    groups = 2 if fits else 1
    counts = [len(many_a) for many_a, _ in pairs]
    lefts = [a for many_a, _ in pairs for a in many_a]
    rights = [b for _, many_b in pairs for b in many_b]
    out = call(partial(wg_kernel, starts=starts, counts=counts, halves=halves, rows=rows if fits else 0), us, steps,
        [pl.BlockSpec(memory_space=pltpu.SMEM)] + specs + b_specs,
        [pl.BlockSpec((D // groups, D), lambda j: (0, j))] * groups, [sds(D // groups, cols)] * groups,
        [pltpu.VMEM((D, a.shape[0]), BF) for a in pairs[0][0]])(core.reshape(1, 1), *lefts, *rights)
    if fits:
        return [part.reshape(-1, rows, cols) for part in out]
    parts = jnp.swapaxes(out[0].reshape(-1, halves, rows, cols), 0, 1)
    return [lax.dynamic_index_in_dim(parts, core ^ d, 0, keepdims=False) for d in range(halves)]

def chunk_spec(rows, cols, start, many):
    return pl.BlockSpec((rows, cols), lambda j: (0, jnp.clip(j - start, 0, many - 1)))


def exchange(pieces, axis):
    size = len(pieces)
    return [pieces[0]] + [
        lax.ppermute(pieces[d], axis, [(i, i ^ d) for i in range(size)]) for d in range(1, size)
    ]


def in_order(pieces, axis, step=1):
    while step < len(pieces):
        swap = (lax.axis_index(axis) // step) % 2 == 1
        pieces = [jnp.where(swap, pieces[c ^ step], pieces[c]) for c in range(len(pieces))]
        step *= 2
    return pieces


def collect(array, axis, at=0, hold=()):
    pieces = exchange([array] * lax.axis_size(axis), axis)
    pieces = pieces[:1] + [after(piece, *hold) for piece in pieces[1:]]
    return jnp.stack(in_order(pieces, axis), axis=at)


def partner(array, axis, step):
    size = lax.axis_size(axis)
    return lax.ppermute(array, axis, [(i, i ^ step) for i in range(size)])


def far_first(array, axis):
    size = lax.axis_size(axis)
    step = size // 2
    out = array[None]
    while step:
        other = partner(out, axis, step)
        low = (lax.axis_index(axis) // step) % 2 == 0
        out = jnp.stack((jnp.where(low, out, other), jnp.where(low, other, out)), axis=1)
        out = out.reshape((-1,) + array.shape)
        step //= 2
    return out


def bit_step(array, axis, step, hold):
    blocks = array.reshape((-1, 2) + array.shape[1:])
    mine = (lax.axis_index(axis) // step) % 2
    send = lax.dynamic_index_in_dim(blocks, 1 - mine, 1, keepdims=False)
    keep = lax.dynamic_index_in_dim(blocks, mine, 1, keepdims=False)
    came = after(partner(send, axis, step), hold)
    return (keep.astype(F32) + came.astype(F32)).astype(BF)


def later_bits(array, axis, hold):
    step = 2
    while step < lax.axis_size(axis):
        array = bit_step(array, axis, step, hold)
        step *= 2
    return array[0]


def split_off(array, axis):
    place = lax.axis_index(axis)
    pieces = [
        lax.dynamic_index_in_dim(array, place ^ d, 0, keepdims=False)
        for d in range(lax.axis_size(axis))
    ]
    return exchange(pieces[:1] + [piece.astype(BF) for piece in pieces[1:]], axis)


def added(pieces, *hold):
    out = pieces[0].astype(F32)
    for piece in pieces[1:]:
        out = out + after(piece, *hold).astype(F32)
    return out


def shed(array, axis, hold=()):
    return added(split_off(array, axis), *hold)


def shed_at_once(array, axis, *hold):
    came = lax.all_to_all(array.astype(BF), axis, split_axis=0, concat_axis=0, tiled=True)
    came = after(came, *hold)
    return jnp.sum(came.astype(F32), axis=0)


def after(array, *others):
    return lax.optimization_barrier((array,) + others)[0]


def plus_others(array, axis):
    came = exchange([array] * lax.axis_size(axis), axis)
    return sum(came[1:], came[0])


def local(
    clips_in,
    valid_clips,
    norm_gains,
    norm_shifts,
    temporal_qkv,
    temporal_proj,
    temporal_fc,
    spatial_qkv,
    spatial_proj,
    mlp_in,
    mlp_out,
    head_bias,
    width_bias,
    fc_bias,
    hidden_bias,
    cotangent,
):
    held, frames_held, places, width = clips_in.shape
    head = width // HEADS
    scale = head ** (-0.5)
    across = lax.axis_size("context")
    halves = lax.axis_size("tensor")
    place = lax.axis_index("context")
    own_rows = temporal_qkv.shape[0]
    in_rows, in_cols = mlp_in.shape
    spread = held % across == 0
    clips = held // across if spread else held
    share = 1.0 if spread else 1.0 / across
    frames = frames_held * across
    first_places = -(-places // 32) * 16
    cuts = (slice(0, first_places), slice(first_places, places))

    def to_clips(array):
        array = jnp.swapaxes(array, 1, 2)
        if spread:
            array = lax.all_to_all(array, "context", split_axis=0, concat_axis=0, tiled=True)
            return array.reshape((across, clips) + array.shape[1:])
        return lax.all_gather(array, "context", axis=0)

    def fill(array):
        array = jnp.swapaxes(array, 1, 2).reshape(frames, array.shape[1], width)
        array = jnp.pad(array, ((0, 0), (0, -array.shape[1] % 16), (0, 0)))
        return array.reshape(-1, width)

    def by_place(array, real):
        array = array.reshape(across, frames_held, -1, width)[:, :, :real]
        return jnp.swapaxes(array, 1, 2)

    def from_clips(array):
        if spread:
            array = lax.all_to_all(array, "context", split_axis=0, concat_axis=0, tiled=True)
        else:
            array = lax.dynamic_slice_in_dim(array, place, 1, 0)
        return array

    def send_back(array):
        array = by_place(array, places)
        if spread:
            return split_off(array, "context")
        return [lax.dynamic_index_in_dim(array, place, 0, keepdims=False)]

    def sent_back(pieces):
        return jnp.swapaxes(jnp.stack(in_order(pieces, "context")), 1, 2)

    if spread:
        valid = lax.dynamic_slice_in_dim(valid_clips, place * clips, clips, 0)
    else:
        valid = valid_clips
    keep = valid.astype(F32)

    def flat3(weight):
        return weight.reshape(own_rows, 3 * width)

    def by_shard(d):
        return d.reshape((lax.axis_size("shard"), across) + d.shape[1:])

    t_own = jnp.concatenate((flat3(temporal_qkv), temporal_proj, temporal_fc), axis=1).astype(BF)
    s_own = jnp.concatenate((flat3(spatial_qkv), spatial_proj), axis=1).astype(BF)
    mlp_own = jnp.concatenate((mlp_in, mlp_out), axis=0).astype(BF)
    clip_parts = [clips_in[:, :, cut] for cut in cuts]
    pull_parts = [cotangent[:, :, cut] for cut in cuts]
    gain = [norm_gains[i : i + 1] for i in range(3)]
    shift = [norm_shifts[i : i + 1] for i in range(3)]
    wide = [width_bias[i : i + 1] for i in range(3)]
    head_pairs, fc_row, hidden_row = [head_bias[0], head_bias[1]], fc_bias[None], hidden_bias[None]
    early = clip_parts + pull_parts + gain + shift + wide + head_pairs + [fc_row, hidden_row]
    first = collect(jnp.concatenate((t_own, s_own), axis=1), "context", hold=early)
    t_first, s_first = first[..., : t_own.shape[1]], first[..., t_own.shape[1] :]
    rows_a = to_clips(after(clip_parts[0], first))
    mlp_all = lax.all_gather(after(mlp_own, first), ALL, axis=0, tiled=True)
    mlp_all = mlp_all.reshape(-1, halves, 2 * in_rows, in_cols)
    t_chips = collect(t_first, "shard", hold=(rows_a,))
    t_all = collect(t_chips, "tensor", 2).reshape(-1, t_own.shape[1])
    rows_b = to_clips(after(clip_parts[1], rows_a))
    pull_a = to_clips(after(pull_parts[0], rows_b))
    pull_b = to_clips(after(pull_parts[1], pull_a))

    def one_clip(x_a, x_b, pull_a, pull_b, keep_one):
        sizes = dict(frames=frames, head=head, scale=scale)
        forward_t = partial(
            temporal_forward, gain=gain[0], shift=shift[0], w=t_all, hb=head_pairs[0], wb=wide[0],
            fcb=fc_row, **sizes,
        )
        x_a = fill(x_a)
        at_a, qkv_a, probs_a, o_a, y_a, x1_a = forward_t(x_a)
        s_all = collect(after(s_first, rows_a), "shard", hold=(x1_a,))
        x_b = fill(after(x_b, x1_a, s_all))
        at_b, qkv_b, probs_b, o_b, y_b, x1_b = forward_t(x_b)
        s_all = collect(s_all, "tensor", 2, hold=(x1_b,)).reshape(-1, s_own.shape[1])
        pull_a = after(pull_a, x1_b)
        sizes_s = dict(sizes, real=places)
        a_s, qkv_s, o_s, x2, x1 = spatial_forward(
            x1_a, after(x1_b, pull_a), gain[1], shift[1], s_all, head_pairs[1], wide[1], **sizes_s
        )
        out, g2, db, d_m, d_hidden, sums_m = mlp(
            x2, fill(pull_a), fill(after(pull_b, x2)), keep_one.reshape(1, 1), gain[2], shift[2], mlp_all, hidden_row, wide[2],
            frames=frames,
        )
        back_s = partial(spatial_backward, gain=gain[1], w=s_all, first=first_places, **sizes_s)
        core = lax.axis_index("tensor")

        def grads_of(pairs, us):
            pieces = weight_grads(pairs, core, halves, own_rows, us)
            return [(share * p).astype(BF) for p in pieces] if share != 1.0 else pieces

        d_m = (share * d_m if share != 1.0 else d_m).astype(BF).reshape(-1, in_cols)
        d_m = lax.psum_scatter(d_m, ALL, scatter_dimension=0, tiled=True)
        back = send_back(out)
        half = back_s(g2, db, qkv_s, x1, part=0)
        tied = after(db, half[0], *back[1:2])
        d_qkv_s, g1_a, g1_b, dz_a, dz_b, sums_s = back_s(g2, tied, qkv_s, x1, part=1, held=half)
        sums_s = sums_s + half[5]
        tied = after(d_qkv_s, *back[2:3])
        d_s = grads_of([([a_s], [tied]), ([db], [o_s])], us=12)
        tied = after(dz_a, *d_s)
        d_s = exchange(d_s, "tensor")
        dy_a, do_a, sums_y = temporal_pull(tied, t_all)
        dy_b, do_b, sums_yb = temporal_pull(after(dz_b, dy_a), t_all)
        d_s = added(d_s, dy_b).astype(BF)
        tied = after(dy_b, d_s, *back[3:])
        d_s = split_off(by_shard(d_s), "shard")
        d_r = grads_of([([dy_a, tied], [o_a, o_b]), ([y_a, y_b], [dz_a, dz_b])], us=6)
        tied = after(do_a, *d_r)
        d_r = exchange(d_r, "tensor")
        d_qkv_a, sums_q = temporal_backward(tied, qkv_a, probs_a, **sizes)
        d_r = added(d_r, d_qkv_a).astype(BF)
        into_a, sums_x = temporal_end(after(d_qkv_a, d_r), x_a, g1_a, gain[0], t_all)
        d_s = added(d_s, into_a).astype(BF)
        swap_a = by_place(into_a, first_places)
        into_a = from_clips(swap_a)
        tied = after(do_b, swap_a, d_s)
        d_s = split_off(d_s, "context")
        d_qkv_b, sums_qb = temporal_backward(tied, qkv_b, probs_b, **sizes)
        d_r_first = bit_step(by_shard(d_r), "shard", 1, d_qkv_b)
        d_q = grads_of([([at_a, at_b], [d_qkv_a, after(d_qkv_b, d_r_first)])], us=9)
        d_m = d_m.astype(F32)
        d_r = later_bits(d_r_first, "shard", d_q[0])
        tied = lax.optimization_barrier((d_qkv_b, *d_q, into_a, d_r, d_m))[0]
        d_q = exchange(d_q, "tensor")
        into_b, sums_xb = temporal_end(tied, x_b, g1_b, gain[0], t_all)
        swap_b = by_place(into_b, places - first_places)
        d_s = added(d_s, into_b)
        into_b = from_clips(after(swap_b, into_a, d_s))
        t, m = sums_y + sums_yb + sums_q + sums_qb + sums_x + sums_xb, sums_m
        rows = [v[n : n + 1] for n in (0, 1) for v in (t, sums_s, m)] + [t[2:4], sums_s[2:4]]
        rows = rows + [t[4:5], m[3:4], m[2:3], sums_s[4:5], d_hidden.reshape(-1, width)]
        small = plus_others(share * jnp.concatenate(rows, axis=0), "tensor")
        d_q = added(d_q, swap_b).astype(BF)
        small = plus_others(small, "shard")
        d_q = added(split_off(by_shard(d_q), "shard"), small).astype(BF)
        output = sent_back([after(piece, d_q) for piece in back])
        small = plus_others(after(small, d_q), "context")
        d_q = shed(jnp.concatenate((d_r, d_q), axis=-1), "context")
        into = jnp.swapaxes(jnp.concatenate((into_a, after(into_b, output, d_q)), axis=1), 1, 2)
        return output, into, (d_q, d_s, d_m, small)

    given = (rows_a, rows_b, pull_a, pull_b)
    parts = [one_clip(*[v[:, i] for v in given], keep[i]) for i in range(clips)]
    output, input_grad = [
        jnp.stack([part[n] for part in parts], axis=1).reshape(clips_in.shape) for n in (0, 1)
    ]
    grads = parts[0][2]
    for part in parts[1:]:
        grads = jax.tree.map(jnp.add, grads, part[2])
    d_t, d_s, d_mlp, small = grads
    d_t_rest, d_t_qkv = d_t[:, : 2 * width], d_t[:, 2 * width :]
    return (
        output,
        input_grad,
        small[0:3],
        small[3:6],
        d_t_qkv.reshape(own_rows, 3, width),
        d_t_rest[:, :width],
        d_t_rest[:, width:],
        d_s[:, : 3 * width].reshape(own_rows, 3, width),
        d_s[:, 3 * width :],
        d_mlp[:in_rows],
        d_mlp[in_rows:],
        small[6:10].reshape(2, 2, width),
        small[10:13],
        small[13],
        small[14:].reshape(-1),
    )


def solution(mesh):
    clip = P(("shard", "tensor"), "context", None, None)
    row, block = P(ALL, None), P(("shard", "context"), "tensor")
    deep, whole = P(ALL, None, None), P()
    weights = (deep, row, row, deep, row, block, block)
    in_specs = (clip, P(("shard", "tensor")), whole, whole) + weights + (whole,) * 4 + (clip,)
    out_specs = (clip, clip, whole, whole) + weights + (whole,) * 4
    return jax.shard_map(local, mesh=mesh, in_specs=in_specs, out_specs=out_specs, check_vma=False)
```

```python
from functools import partial

import jax
import jax.numpy as jnp
from jax import lax
from jax.experimental import pallas as pl
from jax.experimental.pallas import tpu as pltpu
from jax.sharding import PartitionSpec as P

HEADS = 12
EPS = 1e-05
ALL = ("shard", "context", "tensor")
BF = jnp.bfloat16
F32 = jnp.float32
VMEM = 60 * 2**20

def mm(left, right, left_dim, right_dim):
    return lax.dot_general(left, right, (((left_dim,), (right_dim,)), ((), ())), preferred_element_type=F32)

def norm_stats(rows):
    centered = rows - jnp.mean(rows, axis=-1, keepdims=True)
    inv = lax.rsqrt(jnp.mean(centered * centered, axis=-1, keepdims=True) + EPS)
    return centered * inv, inv

def mlp_kernel(x_ref, cota_ref, cotb_ref, keep_ref, gain_ref, shift_ref, w_ref, hb_ref, wb_ref,
               out_ref, g2_ref, db_ref, dw_ref, dhb_ref, sums_ref,
               a_ref, at_ref, dm_ref, dmt_ref, m_ref, da_ref, h_ref, du_ref, *, rb, chunks, frames):
    step = pl.program_id(0)
    T, D = x_ref.shape
    cot_ref = out_ref
    nb = T // rb
    blocks, _, both, hc = w_ref.shape
    half = both // 2

    @pl.when(step == 0)
    def _():
        merge(cot_ref, (cota_ref, cotb_ref), frames)
        def body(i, c):
            r = pl.ds(pl.multiple_of(i * rb, 16), rb)
            unit, _ = norm_stats(x_ref[r, :])
            a = (unit * gain_ref[...] + shift_ref[...]).astype(BF)
            a_ref[r, :] = a
            dm = (keep_ref[0, 0] * cot_ref[r, :].astype(F32)).astype(BF)
            dm_ref[r, :] = dm
            return c
        lax.fori_loop(0, nb, body, 0)
        at_ref[...] = a_ref[...].T
        dmt_ref[...] = dm_ref[...].T

    win = w_ref[:, 0, :half, :].reshape(D, hc)
    wout = w_ref[:, 0, half:, :].reshape(D, hc)
    hb = hb_ref[...]
    tot = jnp.zeros((1, hc), F32)
    for i in range(nb):
        r = slice(i * rb, (i + 1) * rb)
        u = mm(a_ref[r, :], win, 1, 0) + hb
        cdf = 0.5 * (1.0 + lax.erf(u * (2 ** -0.5)))
        h = (u * cdf).astype(BF)
        pdf = jnp.exp(-0.5 * u * u) * ((2 * jnp.pi) ** -0.5)
        dh = mm(dm_ref[r, :], wout, 1, 0)
        du = ((cdf + u * pdf) * dh).astype(BF)
        h_ref[r, :] = h
        du_ref[r, :] = du
        tot += jnp.sum(du.astype(F32), axis=0, keepdims=True)
        m = mm(h, wout, 1, 1)
        da = mm(du, win, 1, 1)
        @pl.when(step == 0)
        def _():
            m_ref[r, :] = m
            da_ref[r, :] = da
        @pl.when(step > 0)
        def _():
            m_ref[r, :] += m
            da_ref[r, :] += da
    dhb_ref[...] = tot
    dw_ref[:, 0, :half, :] = mm(at_ref[...], du_ref[...], 1, 0).astype(BF).reshape(blocks, half, hc)
    dw_ref[:, 0, half:, :] = mm(dmt_ref[...], h_ref[...], 1, 0).astype(BF).reshape(blocks, half, hc)

    @pl.when(step == chunks - 1)
    def _():
        k = keep_ref[0, 0]
        def body(i, c):
            r = pl.ds(pl.multiple_of(i * rb, 16), rb)
            x = x_ref[r, :]
            g3 = k * cot_ref[r, :].astype(F32)
            out_ref[r, :] = (k * (x + (m_ref[r, :] + wb_ref[...]))).astype(BF)
            da = da_ref[r, :]
            unit, inv = norm_stats(x)
            sc = da * gain_ref[...]
            into = inv * (sc - jnp.mean(sc, axis=-1, keepdims=True) - unit * jnp.mean(sc * unit, axis=-1, keepdims=True))
            g2 = g3 + into
            g2_ref[r, :] = g2
            low = g2.astype(BF)
            db_ref[r, :] = low
            return (c[0] + jnp.sum(da * unit, axis=0, keepdims=True),
                    c[1] + jnp.sum(da, axis=0, keepdims=True),
                    c[2] + jnp.sum(dm_ref[r, :].astype(F32), axis=0, keepdims=True),
                    c[3] + jnp.sum(low.astype(F32), axis=0, keepdims=True))
        z = jnp.zeros((1, D), F32)
        c = lax.fori_loop(0, nb, body, (z, z, z, z))
        for j in range(4):
            sums_ref[j:j+1, :] = c[j]

def mlp(x2, cot_a, cot_b, keep, gain, shift, w4, hb, wb, *, frames):
    T, D = x2.shape
    B, H2, R, C = w4.shape
    rb = T // 4 if T % 64 == 0 else T
    hc = next(w for w in (768, 512, 384, 256, 128) if C % w == 0)
    per = C // hc
    chunks = H2 * per
    full = lambda *s: pl.BlockSpec(s, lambda j: (0,) * len(s), pipeline_mode=pl.Buffered(1))
    wspec = pl.BlockSpec((B, 1, R, hc), lambda j: (0, j // per, 0, j % per))
    hspec = pl.BlockSpec((1, hc), lambda j: (0, j))
    return pl.pallas_call(
        partial(mlp_kernel, rb=rb, chunks=chunks, frames=frames),
        grid=(chunks,),
        in_specs=[full(T, D), full(*cot_a.shape), full(*cot_b.shape), pl.BlockSpec(memory_space=pltpu.SMEM), full(1, D), full(1, D), wspec, hspec, full(1, D)],
        out_specs=[full(T, D), full(T, D), full(T, D), wspec, hspec, full(8, D)],
        out_shape=(sds(T, D), sds(T, D, t=F32), sds(T, D), sds(*w4.shape), sds(1, H2 * C, t=F32), sds(8, D, t=F32)),
        scratch_shapes=[pltpu.VMEM((T, D), BF), pltpu.VMEM((D, T), BF), pltpu.VMEM((T, D), BF), pltpu.VMEM((D, T), BF),
                        pltpu.VMEM((T, D), F32), pltpu.VMEM((T, D), F32), pltpu.VMEM((T, hc), BF), pltpu.VMEM((T, hc), BF)],
        compiler_params=pltpu.CompilerParams(vmem_limit_bytes=VMEM),
        cost_estimate=cost(75),
    )(x2, cot_a, cot_b, keep, gain, shift, w4, hb, wb)
LANES = 128
LOW = -1e30

def once(*s):
    return pl.BlockSpec(s, lambda j: (0,) * len(s), pipeline_mode=pl.Buffered(1))

def column(rows, cols, at):
    return pl.BlockSpec((rows, cols), lambda j: (0, at), pipeline_mode=pl.Buffered(1))

def sds(*s, t=BF):
    return jax.ShapeDtypeStruct(s, t)

def cost(us):
    return pl.CostEstimate(flops=us * 10**9, bytes_accessed=0, transcendentals=0)

def call(body, us, grid, ins, outs, shapes, scratch=()):
    return pl.pallas_call(body, grid=(grid,), in_specs=ins, out_specs=outs, out_shape=shapes, scratch_shapes=list(scratch),
                          compiler_params=pltpu.CompilerParams(vmem_limit_bytes=VMEM), cost_estimate=cost(us))

def qkv_store(a, wqkv, hb_ref, dst, rows, D):
    packed = mm(a, wqkv, 1, 0)
    dst[rows, :D] = (packed[:, :D] + hb_ref[0:1, :]).astype(BF)
    dst[rows, D:2 * D] = packed[:, D:2 * D].astype(BF)
    dst[rows, 2 * D:] = (packed[:, 2 * D:] + hb_ref[1:2, :]).astype(BF)

def lane_masks(head, value):
    lane = lax.broadcasted_iota(jnp.int32, (1, LANES), 1)
    return [jnp.where(lane // head == i, value, 0.0).astype(BF) for i in range(LANES // head)]

def merge(dst_ref, parts, fb):
    P = dst_ref.shape[0] // fb
    for f in range(fb):
        at = f * P
        for part in parts:
            n = part.shape[0] // fb
            dst_ref[at:at + n, :] = part[f * n:(f + 1) * n, :]
            at += n

def split(value, dst_refs, fb):
    P = value.shape[0] // fb
    for f in range(fb):
        at = f * P
        for dst in dst_refs:
            n = dst.shape[0] // fb
            dst[f * n:(f + 1) * n, :] = value[at:at + n, :]
            at += n

def sf_kernel(xa_ref, xb_ref, gain_ref, shift_ref, wqkv_ref, wproj_ref, hb_ref, wb_ref, a_ref, qkv_ref, o_ref, x2_ref, x_ref, *, fb, real, head, scale):
    M, D = x_ref.shape
    P = M // fb
    merge(x_ref, (xa_ref, xb_ref), fb)
    unit, _ = norm_stats(x_ref[...])
    a = (unit * gain_ref[...] + shift_ref[...]).astype(BF)
    a_ref[...] = a
    qkv_store(a, wqkv_ref[...], hb_ref, qkv_ref, slice(0, M), D)
    col = lax.broadcasted_iota(jnp.int32, (1, P), 1)
    hide = jnp.where(col < real, 0.0, LOW)
    ones = lane_masks(head, 1.0)
    for f in range(fb):
        r = slice(f * P, (f + 1) * P)
        for j in range(D // LANES):
            q = qkv_ref[r, j * LANES:(j + 1) * LANES]
            k = qkv_ref[r, D + j * LANES:D + (j + 1) * LANES]
            v = qkv_ref[r, 2 * D + j * LANES:2 * D + (j + 1) * LANES]
            o = None
            for m in ones:
                s = mm(q * m, k, 1, 1) * scale + hide
                p = jnp.exp(s - jnp.max(s, axis=-1, keepdims=True))
                p = (p * (1.0 / jnp.sum(p, axis=-1, keepdims=True))).astype(BF)
                part = mm(p, v * m, 1, 0)
                o = part if o is None else o + part
            o_ref[r, j * LANES:(j + 1) * LANES] = o.astype(BF)
    x2_ref[...] = x_ref[...] + (mm(o_ref[...], wproj_ref[...], 1, 1) + wb_ref[...])

def frame_blocks(rows, width, at=0):
    return pl.BlockSpec((rows, width), lambda j: (j + at, 0))

def spatial_forward(xa, xb, gain, shift, w, hb, wb, *, frames, real, head, scale, fb=2):
    D = xa.shape[1]
    steps = frames // fb
    T = xa.shape[0] + xb.shape[0]
    blk = lambda width, rows=T: frame_blocks(rows // steps, width)
    return call(partial(sf_kernel, fb=fb, real=real, head=head, scale=scale), 30, steps,
        [blk(D, xa.shape[0]), blk(D, xb.shape[0]), once(1, D), once(1, D), column(D, 3 * D, 0), column(D, D, 3), once(2, D), once(1, D)],
        [blk(D), blk(3 * D), blk(D), blk(D), blk(D)], (sds(T, D), sds(T, 3 * D), sds(T, D), sds(T, D, t=F32), sds(T, D, t=F32)))(
        xa, xb, gain, shift, w, w, hb, wb)

def norm_back_store(x, gain, da, base, sums_ref, at):
    unit, inv = norm_stats(x)
    sc = da * gain
    into = inv * (sc - jnp.mean(sc, axis=-1, keepdims=True) - unit * jnp.mean(sc * unit, axis=-1, keepdims=True))
    sums_ref[at:at + 1, :] += jnp.sum(da * unit, axis=0, keepdims=True)
    sums_ref[at + 1:at + 2, :] += jnp.sum(da, axis=0, keepdims=True)
    return base + into

def add_sum(sums_ref, at, rows):
    sums_ref[at:at + 1, :] += jnp.sum(rows.astype(F32), axis=0, keepdims=True)

def sb_kernel(g2_ref, db_ref, qkv_ref, x_ref, gain_ref, wqkv_ref, wproj_ref, *rest, fb, real, head, scale):
    dqkv_ref, g1a_ref, g1b_ref, dza_ref, dzb_ref, sums_ref, do_ref = rest[-7:]
    M, D = x_ref.shape
    P = M // fb
    @pl.when(pl.program_id(0) == 0)
    def _():
        sums_ref[...] = jnp.zeros_like(sums_ref)
    do_ref[...] = mm(db_ref[...], wproj_ref[...], 1, 0).astype(BF)
    row = lax.broadcasted_iota(jnp.int32, (P, 1), 0)
    hide = jnp.where(row < real, 0.0, LOW)
    ones = lane_masks(head, 1.0)
    for f in range(fb):
        r = slice(f * P, (f + 1) * P)
        for j in range(D // LANES):
            ls = [slice(i * D + j * LANES, i * D + (j + 1) * LANES) for i in range(3)]
            q, k, v = [qkv_ref[r, l] for l in ls]
            do = do_ref[r, ls[0]]
            dq = dk = dv = 0.0
            for m in ones:
                qm = q * m
                dom = do * m
                s = mm(k, qm, 1, 1) * scale + hide
                p = jnp.exp(s - jnp.max(s, axis=0, keepdims=True))
                p = p * (1.0 / jnp.sum(p, axis=0, keepdims=True))
                dp = mm(v, dom, 1, 1)
                ds = (p * (dp - jnp.sum(p * dp, axis=0, keepdims=True))).astype(BF)
                dv = dv + mm(p.astype(BF), dom, 1, 0)
                dk = dk + mm(ds, qm, 1, 0)
                dq = dq + mm(ds, k * m, 0, 0)
            dqkv_ref[r, ls[0]] = (dq * scale).astype(BF)
            dqkv_ref[r, ls[1]] = (dk * scale).astype(BF)
            dqkv_ref[r, ls[2]] = dv.astype(BF)
    add_sum(sums_ref, 2, dqkv_ref[:, :D])
    add_sum(sums_ref, 3, dqkv_ref[:, 2 * D:])
    da = mm(dqkv_ref[...], wqkv_ref[...], 1, 1)
    g1 = norm_back_store(x_ref[...], gain_ref[...], da, g2_ref[...], sums_ref, 0)
    split(g1, (g1a_ref, g1b_ref), fb)
    low = g1.astype(BF)
    split(low, (dza_ref, dzb_ref), fb)
    add_sum(sums_ref, 4, low)

def spatial_backward(g2, db, qkv, x1, *, gain, w, first, frames, real, head, scale, part, held=None, fb=2):
    T, D = x1.shape
    M = T // frames * fb
    nb = frames // fb // 2
    blk = lambda width, rows=M: frame_blocks(rows, width, part * nb)
    kept = [] if held is None else list(held[:5])
    low, high = frames * first, T - frames * first
    ends = [blk(D, first * fb), blk(D, M - first * fb)]
    return pl.pallas_call(
        partial(sb_kernel, fb=fb, real=real, head=head, scale=scale), grid=(nb,),
        in_specs=[blk(D), blk(D), blk(3 * D), blk(D), once(1, D), column(D, 3 * D, 0), column(D, D, 3)]
        + [pl.BlockSpec(memory_space=pl.ANY)] * len(kept),
        out_specs=[blk(3 * D)] + ends + ends + [once(8, D)],
        out_shape=(sds(T, 3 * D), sds(low, D, t=F32), sds(high, D, t=F32), sds(low, D), sds(high, D), sds(8, D, t=F32)),
        scratch_shapes=[pltpu.VMEM((M, D), BF)],
        input_output_aliases={7 + i: i for i in range(len(kept))},
        compiler_params=pltpu.CompilerParams(vmem_limit_bytes=VMEM), cost_estimate=cost(24),
    )(g2, db, qkv, x1, gain, w, w, *kept)

def over_frames(op, rows, slot):
    shift = slot
    while shift < LANES:
        rows = op(rows, pltpu.roll(rows, shift, 1))
        shift *= 2
    return rows

def tf_kernel(x_ref, gain_ref, shift_ref, wqkv_ref, wproj_ref, wfc_ref, hb_ref, wb_ref, fcb_ref,
              a_ref, qkv_ref, p_ref, o_ref, y_ref, x1_ref, all_ref, prod_ref, xs_ref, e_ref, b_ref, *, fb, nb, frames, slot, head, scale):
    M, D = x_ref.shape
    P = M // fb
    step = pl.program_id(0)
    @pl.when(step == 0)
    def _():
        fill_tables(e_ref, b_ref, slot, head)
    @pl.when(step < nb)
    def _():
        x = x_ref[...].astype(F32)
        unit, _ = norm_stats(x)
        a = (unit * gain_ref[...] + shift_ref[...]).astype(BF)
        a_ref[...] = a
        qkv_store(a, wqkv_ref[...], hb_ref, qkv_ref, slice(0, M), D)
        all_ref[pl.ds(pl.multiple_of(step * M, M), M), :] = qkv_ref[...]
        xs_ref[pl.ds(pl.multiple_of(step * M, M), M), :] = x_ref[...]
    @pl.when(step >= nb)
    def _():
        base = pl.multiple_of((step - nb) * M, M)
        for f in range(fb):
            q = all_ref[pl.ds(base + f * P, P), :D]
            for g in range(frames):
                prod_ref[f * P:(f + 1) * P, g * D:(g + 1) * D] = q * all_ref[g * P:(g + 1) * P, D:2 * D]
        s = mm(prod_ref[...], e_ref[...], 1, 0) * scale
        p = jnp.exp(s - over_frames(jnp.maximum, s, slot))
        p = p * (1.0 / over_frames(jnp.add, p, slot))
        p_ref[...] = p
        low = p.astype(BF)
        o = [None] * fb
        for g in range(frames):
            wide = mm(low, b_ref[:, g * D:(g + 1) * D], 1, 0)
            v = all_ref[g * P:(g + 1) * P, 2 * D:].astype(F32)
            for f in range(fb):
                part = wide[f * P:(f + 1) * P] * v
                o[f] = part if g == 0 else o[f] + part
        for f in range(fb):
            o_ref[f * P:(f + 1) * P, :] = o[f].astype(BF)
        y = (mm(o_ref[...], wproj_ref[...], 1, 1) + wb_ref[...]).astype(BF)
        y_ref[...] = y
        z = (mm(y, wfc_ref[...], 1, 0) + fcb_ref[...]).astype(BF)
        x1_ref[...] = xs_ref[pl.ds(base, M), :].astype(F32) + z.astype(F32)

def fill_tables(e_ref, b_ref, slot, head):
    D = e_ref.shape[0] * slot // LANES
    for g in range(LANES // slot):
        for ref, at, wide in ((e_ref, 1, 0), (b_ref, 0, 1)):
            shape = (D, LANES) if wide == 0 else (LANES, D)
            lane = lax.broadcasted_iota(jnp.int32, shape, at)
            feature = lax.broadcasted_iota(jnp.int32, shape, wide)
            hit = ((lane // slot == g) & (lane % slot == feature // head)).astype(F32).astype(BF)
            if wide == 0:
                ref[g * D:(g + 1) * D, :] = hit
            else:
                ref[:, g * D:(g + 1) * D] = hit

def temporal_forward(x, gain, shift, w, hb, wb, fcb, *, frames, head, scale, fb=4):
    T, D = x.shape
    M = T // frames * fb
    nb = frames // fb
    first = lambda w: pl.BlockSpec((M, w), lambda j: (jnp.minimum(j, nb - 1), 0))
    last = lambda w: pl.BlockSpec((M, w), lambda j: (jnp.maximum(j - nb, 0), 0))
    return call(partial(tf_kernel, fb=fb, nb=nb, frames=frames, slot=LANES // frames, head=head, scale=scale), 22, 2 * nb,
        [first(D), once(1, D), once(1, D), column(D, 3 * D, 0), column(D, D, 3), column(D, D, 4), once(2, D), once(1, D), once(1, D)],
        [first(D), first(3 * D), last(LANES), last(D), last(D), last(D)],
        (sds(T, D), sds(T, 3 * D), sds(T, LANES, t=F32), sds(T, D), sds(T, D), sds(T, D, t=F32)),
        [pltpu.VMEM((T, 3 * D), BF), pltpu.VMEM((M, frames * D), BF), pltpu.VMEM((T, D), BF),
         pltpu.VMEM((frames * D, LANES), BF), pltpu.VMEM((LANES, frames * D), BF)])(
        x, gain, shift, w, w, w, hb, wb, fcb)

def zero_first(*refs):
    @pl.when(pl.program_id(0) == 0)
    def _():
        for ref in refs:
            ref[...] = jnp.zeros_like(ref)

def pull_kernel(dz_ref, wproj_ref, wfc_ref, dy_ref, do_ref, sums_ref):
    zero_first(sums_ref)
    dy = mm(dz_ref[...], wfc_ref[...], 1, 1).astype(BF)
    dy_ref[...] = dy
    add_sum(sums_ref, 4, dy)
    do_ref[...] = mm(dy, wproj_ref[...], 1, 0).astype(BF)

def temporal_pull(dz, w, *, blocks=2):
    T, D = dz.shape
    blk = pl.BlockSpec((T // blocks, D), lambda j: (j, 0))
    return call(pull_kernel, 4, blocks, [blk, column(D, D, 3), column(D, D, 4)], [blk, blk, once(8, D)],
                (sds(T, D), sds(T, D), sds(8, D, t=F32)))(dz, w, w)

def tb_kernel(do_ref, qkv_ref, p_ref, dqkv_ref, sums_ref, dk_ref, dv_ref, prod_ref, e_ref, b_ref, *, fb, nb, frames, slot, head, scale):
    M = p_ref.shape[0]
    T, D = do_ref.shape
    P = M // fb
    step = pl.program_id(0)
    zero_first(sums_ref, dk_ref, dv_ref)
    @pl.when(step == 0)
    def _():
        fill_tables(e_ref, b_ref, slot, head)
    base = pl.multiple_of(step * M, M)
    for f in range(fb):
        do = do_ref[pl.ds(base + f * P, P), :]
        for g in range(frames):
            prod_ref[f * P:(f + 1) * P, g * D:(g + 1) * D] = do * qkv_ref[g * P:(g + 1) * P, 2 * D:]
    dp = mm(prod_ref[...], e_ref[...], 1, 0)
    p = p_ref[...]
    ds = (p * (dp - over_frames(jnp.add, p * dp, slot))).astype(BF)
    low = p.astype(BF)
    dq = [0.0] * fb
    for g in range(frames):
        gr = slice(g * P, (g + 1) * P)
        wide_p = mm(low, b_ref[:, g * D:(g + 1) * D], 1, 0)
        wide_s = mm(ds, b_ref[:, g * D:(g + 1) * D], 1, 0)
        k = qkv_ref[gr, D:2 * D].astype(F32)
        dk, dv = dk_ref[gr, :], dv_ref[gr, :]
        for f in range(fb):
            fr = pl.ds(base + f * P, P)
            wp, ws = wide_p[f * P:(f + 1) * P], wide_s[f * P:(f + 1) * P]
            dv = dv + wp * do_ref[fr, :].astype(F32)
            dk = dk + ws * qkv_ref[fr, :D].astype(F32)
            dq[f] = dq[f] + ws * k
        dk_ref[gr, :] = dk
        dv_ref[gr, :] = dv
    for f in range(fb):
        low = (dq[f] * scale).astype(BF)
        add_sum(sums_ref, 2, low)
        dqkv_ref[pl.ds(base + f * P, P), :D] = low
    @pl.when(step == nb - 1)
    def _():
        for g in range(frames):
            gr = slice(g * P, (g + 1) * P)
            dqkv_ref[gr, D:2 * D] = (dk_ref[gr, :] * scale).astype(BF)
            low = dv_ref[gr, :].astype(BF)
            add_sum(sums_ref, 3, low)
            dqkv_ref[gr, 2 * D:] = low

def temporal_backward(do, qkv, p, *, frames, head, scale, fb=4):
    T, D = do.shape
    M = T // frames * fb
    nb = frames // fb
    return call(partial(tb_kernel, fb=fb, nb=nb, frames=frames, slot=LANES // frames, head=head, scale=scale), 20, nb,
        [once(T, D), once(T, 3 * D), pl.BlockSpec((M, LANES), lambda j: (j, 0))],
        [once(T, 3 * D), once(8, D)], (sds(T, 3 * D), sds(8, D, t=F32)),
        [pltpu.VMEM((T, D), F32), pltpu.VMEM((T, D), F32), pltpu.VMEM((M, frames * D), BF),
         pltpu.VMEM((frames * D, LANES), BF), pltpu.VMEM((LANES, frames * D), BF)])(do, qkv, p)

def end_kernel(dqkv_ref, x_ref, g1_ref, gain_ref, wqkv_ref, out_ref, sums_ref):
    zero_first(sums_ref)
    da = mm(dqkv_ref[...], wqkv_ref[...], 1, 1)
    out = norm_back_store(x_ref[...].astype(F32), gain_ref[...], da, g1_ref[...], sums_ref, 0)
    out_ref[...] = out.astype(BF)

def temporal_end(dqkv, x, g1, gain, w, *, blocks=2):
    T, D = x.shape
    blk = lambda w: pl.BlockSpec((T // blocks, w), lambda j: (j, 0))
    return call(end_kernel, 7, blocks, [blk(3 * D), blk(D), blk(D), once(1, D), column(D, 3 * D, 0)], [blk(D), once(8, D)],
                (sds(T, D), sds(8, D, t=F32)))(dqkv, x, g1, gain, w)

def wg_kernel(core_ref, *refs, starts, counts, halves, rows):
    n = sum(counts)
    many_out = 2 if rows else 1
    a_refs, b_refs, out_refs, t_refs = refs[:n], refs[n:2 * n], refs[2 * n:2 * n + many_out], refs[2 * n + many_out:]
    step = pl.program_id(0)
    at = 0
    for i, many in enumerate(counts):
        mine = range(at, at + many)
        at += many
        @pl.when(step == starts[i])
        def _():
            for t_ref, n_at in zip(t_refs, mine):
                t_ref[...] = a_refs[n_at][...].T
        stop = starts[i + 1] if i + 1 < len(counts) else step + 1
        @pl.when((step >= starts[i]) & (step < stop))
        def _():
            res = sum(mm(t_ref[...], b_refs[n_at][...], 1, 0) for t_ref, n_at in zip(t_refs, mine))
            if rows:
                parts = res.reshape(-1, halves, rows, res.shape[-1])
                low, high = [parts[:, h].reshape(-1, res.shape[-1]) for h in range(2)]
                first = core_ref[0, 0] == 0
                out_refs[0][...] = jnp.where(first, low, high).astype(BF)
                out_refs[1][...] = jnp.where(first, high, low).astype(BF)
            else:
                out_refs[0][...] = res.astype(BF)

def weight_grads(pairs, core, halves, rows, us):
    D = pairs[0][0][0].shape[1]
    starts, steps, specs, b_specs = [], 0, [], []
    for many_a, many_b in pairs:
        starts.append(steps)
        chunks = many_b[0].shape[1] // D
        for a in many_a:
            specs.append(once(*a.shape))
            b_specs.append(chunk_spec(a.shape[0], D, steps, chunks))
        steps += chunks
    cols = steps * D
    fits = rows % 8 == 0 and halves == 2
    groups = 2 if fits else 1
    counts = [len(many_a) for many_a, _ in pairs]
    lefts = [a for many_a, _ in pairs for a in many_a]
    rights = [b for _, many_b in pairs for b in many_b]
    out = call(partial(wg_kernel, starts=starts, counts=counts, halves=halves, rows=rows if fits else 0), us, steps,
        [pl.BlockSpec(memory_space=pltpu.SMEM)] + specs + b_specs,
        [pl.BlockSpec((D // groups, D), lambda j: (0, j))] * groups, [sds(D // groups, cols)] * groups,
        [pltpu.VMEM((D, a.shape[0]), BF) for a in pairs[0][0]])(core.reshape(1, 1), *lefts, *rights)
    if fits:
        return [part.reshape(-1, rows, cols) for part in out]
    parts = jnp.swapaxes(out[0].reshape(-1, halves, rows, cols), 0, 1)
    return [lax.dynamic_index_in_dim(parts, core ^ d, 0, keepdims=False) for d in range(halves)]

def chunk_spec(rows, cols, start, many):
    return pl.BlockSpec((rows, cols), lambda j: (0, jnp.clip(j - start, 0, many - 1)))


def exchange(pieces, axis):
    size = len(pieces)
    return [pieces[0]] + [
        lax.ppermute(pieces[d], axis, [(i, i ^ d) for i in range(size)]) for d in range(1, size)
    ]


def in_order(pieces, axis, step=1):
    while step < len(pieces):
        swap = (lax.axis_index(axis) // step) % 2 == 1
        pieces = [jnp.where(swap, pieces[c ^ step], pieces[c]) for c in range(len(pieces))]
        step *= 2
    return pieces


def collect(array, axis, at=0, hold=()):
    pieces = exchange([array] * lax.axis_size(axis), axis)
    pieces = pieces[:1] + [after(piece, *hold) for piece in pieces[1:]]
    return jnp.stack(in_order(pieces, axis), axis=at)


def partner(array, axis, step):
    size = lax.axis_size(axis)
    return lax.ppermute(array, axis, [(i, i ^ step) for i in range(size)])


def far_first(array, axis):
    size = lax.axis_size(axis)
    step = size // 2
    out = array[None]
    while step:
        other = partner(out, axis, step)
        low = (lax.axis_index(axis) // step) % 2 == 0
        out = jnp.stack((jnp.where(low, out, other), jnp.where(low, other, out)), axis=1)
        out = out.reshape((-1,) + array.shape)
        step //= 2
    return out


def bit_step(array, axis, step, hold):
    blocks = array.reshape((-1, 2) + array.shape[1:])
    mine = (lax.axis_index(axis) // step) % 2
    send = lax.dynamic_index_in_dim(blocks, 1 - mine, 1, keepdims=False)
    keep = lax.dynamic_index_in_dim(blocks, mine, 1, keepdims=False)
    came = after(partner(send, axis, step), hold)
    return (keep.astype(F32) + came.astype(F32)).astype(BF)


def later_bits(array, axis, hold):
    step = 2
    while step < lax.axis_size(axis):
        array = bit_step(array, axis, step, hold)
        step *= 2
    return array[0]


def split_off(array, axis):
    place = lax.axis_index(axis)
    pieces = [
        lax.dynamic_index_in_dim(array, place ^ d, 0, keepdims=False)
        for d in range(lax.axis_size(axis))
    ]
    return exchange(pieces[:1] + [piece.astype(BF) for piece in pieces[1:]], axis)


def added(pieces, *hold):
    out = pieces[0].astype(F32)
    for piece in pieces[1:]:
        out = out + after(piece, *hold).astype(F32)
    return out


def shed(array, axis, hold=()):
    return added(split_off(array, axis), *hold)


def shed_at_once(array, axis, *hold):
    came = lax.all_to_all(array.astype(BF), axis, split_axis=0, concat_axis=0, tiled=True)
    came = after(came, *hold)
    return jnp.sum(came.astype(F32), axis=0)


def after(array, *others):
    return lax.optimization_barrier((array,) + others)[0]


def plus_others(array, axis):
    came = exchange([array] * lax.axis_size(axis), axis)
    return sum(came[1:], came[0])


def local(
    clips_in,
    valid_clips,
    norm_gains,
    norm_shifts,
    temporal_qkv,
    temporal_proj,
    temporal_fc,
    spatial_qkv,
    spatial_proj,
    mlp_in,
    mlp_out,
    head_bias,
    width_bias,
    fc_bias,
    hidden_bias,
    cotangent,
):
    held, frames_held, places, width = clips_in.shape
    head = width // HEADS
    scale = head ** (-0.5)
    across = lax.axis_size("context")
    halves = lax.axis_size("tensor")
    place = lax.axis_index("context")
    own_rows = temporal_qkv.shape[0]
    in_rows, in_cols = mlp_in.shape
    spread = held % across == 0
    clips = held // across if spread else held
    share = 1.0 if spread else 1.0 / across
    frames = frames_held * across
    first_places = -(-places // 32) * 16
    cuts = (slice(0, first_places), slice(first_places, places))

    def to_clips(array):
        array = jnp.swapaxes(array, 1, 2)
        if spread:
            array = lax.all_to_all(array, "context", split_axis=0, concat_axis=0, tiled=True)
            return array.reshape((across, clips) + array.shape[1:])
        return lax.all_gather(array, "context", axis=0)

    def fill(array):
        array = jnp.swapaxes(array, 1, 2).reshape(frames, array.shape[1], width)
        array = jnp.pad(array, ((0, 0), (0, -array.shape[1] % 16), (0, 0)))
        return array.reshape(-1, width)

    def by_place(array, real):
        array = array.reshape(across, frames_held, -1, width)[:, :, :real]
        return jnp.swapaxes(array, 1, 2)

    def from_clips(array):
        if spread:
            array = lax.all_to_all(array, "context", split_axis=0, concat_axis=0, tiled=True)
        else:
            array = lax.dynamic_slice_in_dim(array, place, 1, 0)
        return array

    def send_back(array):
        array = by_place(array, places)
        if spread:
            return split_off(array, "context")
        return [lax.dynamic_index_in_dim(array, place, 0, keepdims=False)]

    def sent_back(pieces):
        return jnp.swapaxes(jnp.stack(in_order(pieces, "context")), 1, 2)

    if spread:
        valid = lax.dynamic_slice_in_dim(valid_clips, place * clips, clips, 0)
    else:
        valid = valid_clips
    keep = valid.astype(F32)

    def flat3(weight):
        return weight.reshape(own_rows, 3 * width)

    def by_shard(d):
        return d.reshape((lax.axis_size("shard"), across) + d.shape[1:])

    t_own = jnp.concatenate((flat3(temporal_qkv), temporal_proj, temporal_fc), axis=1).astype(BF)
    s_own = jnp.concatenate((flat3(spatial_qkv), spatial_proj), axis=1).astype(BF)
    mlp_own = jnp.concatenate((mlp_in, mlp_out), axis=0).astype(BF)
    clip_parts = [clips_in[:, :, cut] for cut in cuts]
    pull_parts = [cotangent[:, :, cut] for cut in cuts]
    gain = [norm_gains[i : i + 1] for i in range(3)]
    shift = [norm_shifts[i : i + 1] for i in range(3)]
    wide = [width_bias[i : i + 1] for i in range(3)]
    head_pairs, fc_row, hidden_row = [head_bias[0], head_bias[1]], fc_bias[None], hidden_bias[None]
    early = clip_parts + pull_parts + gain + shift + wide + head_pairs + [fc_row, hidden_row]
    first = collect(jnp.concatenate((t_own, s_own), axis=1), "context", hold=early)
    t_first, s_first = first[..., : t_own.shape[1]], first[..., t_own.shape[1] :]
    rows_a = to_clips(after(clip_parts[0], first))
    t_chips = collect(t_first, "shard", hold=(rows_a,))
    t_all = collect(t_chips, "tensor", 2).reshape(-1, t_own.shape[1])
    mlp_all = lax.all_gather(after(mlp_own, t_chips), ALL, axis=0, tiled=True)
    mlp_all = mlp_all.reshape(-1, halves, 2 * in_rows, in_cols)
    rows_b = to_clips(after(clip_parts[1], rows_a))
    pull_a = to_clips(after(pull_parts[0], rows_b))
    pull_b = to_clips(after(pull_parts[1], pull_a))

    def one_clip(x_a, x_b, pull_a, pull_b, keep_one):
        sizes = dict(frames=frames, head=head, scale=scale)
        forward_t = partial(
            temporal_forward, gain=gain[0], shift=shift[0], w=t_all, hb=head_pairs[0], wb=wide[0],
            fcb=fc_row, **sizes,
        )
        x_a = fill(x_a)
        at_a, qkv_a, probs_a, o_a, y_a, x1_a = forward_t(x_a)
        s_all = collect(after(s_first, rows_a), "shard", hold=(x1_a,))
        x_b = fill(after(x_b, x1_a, s_all))
        at_b, qkv_b, probs_b, o_b, y_b, x1_b = forward_t(x_b)
        s_all = collect(s_all, "tensor", 2, hold=(x1_b,)).reshape(-1, s_own.shape[1])
        pull_a = after(pull_a, x1_b)
        sizes_s = dict(sizes, real=places)
        a_s, qkv_s, o_s, x2, x1 = spatial_forward(
            x1_a, after(x1_b, pull_a), gain[1], shift[1], s_all, head_pairs[1], wide[1], **sizes_s
        )
        out, g2, db, d_m, d_hidden, sums_m = mlp(
            x2, fill(pull_a), fill(after(pull_b, x2)), keep_one.reshape(1, 1), gain[2], shift[2], mlp_all, hidden_row, wide[2],
            frames=frames,
        )
        back_s = partial(spatial_backward, gain=gain[1], w=s_all, first=first_places, **sizes_s)
        core = lax.axis_index("tensor")

        def grads_of(pairs, us):
            pieces = weight_grads(pairs, core, halves, own_rows, us)
            return [(share * p).astype(BF) for p in pieces] if share != 1.0 else pieces

        d_m = (share * d_m if share != 1.0 else d_m).astype(BF).reshape(-1, in_cols)
        d_m = lax.psum_scatter(d_m, ALL, scatter_dimension=0, tiled=True)
        back = send_back(out)
        half = back_s(g2, db, qkv_s, x1, part=0)
        tied = after(db, half[0], *back[1:2])
        d_qkv_s, g1_a, g1_b, dz_a, dz_b, sums_s = back_s(g2, tied, qkv_s, x1, part=1, held=half)
        sums_s = sums_s + half[5]
        tied = after(d_qkv_s, *back[2:3])
        d_s = grads_of([([a_s], [tied]), ([db], [o_s])], us=12)
        tied = after(dz_a, *d_s)
        d_s = exchange(d_s, "tensor")
        dy_a, do_a, sums_y = temporal_pull(tied, t_all)
        dy_b, do_b, sums_yb = temporal_pull(after(dz_b, dy_a), t_all)
        d_s = added(d_s, dy_b).astype(BF)
        tied = after(dy_b, d_s, *back[3:])
        d_s = split_off(by_shard(d_s), "shard")
        d_r = grads_of([([dy_a, tied], [o_a, o_b]), ([y_a, y_b], [dz_a, dz_b])], us=6)
        tied = after(do_a, *d_r)
        d_r = exchange(d_r, "tensor")
        d_qkv_a, sums_q = temporal_backward(tied, qkv_a, probs_a, **sizes)
        d_r = added(d_r, d_qkv_a).astype(BF)
        into_a, sums_x = temporal_end(after(d_qkv_a, d_r), x_a, g1_a, gain[0], t_all)
        d_s = added(d_s, into_a).astype(BF)
        swap_a = by_place(into_a, first_places)
        into_a = from_clips(swap_a)
        tied = after(do_b, swap_a, d_s)
        d_s = split_off(d_s, "context")
        d_qkv_b, sums_qb = temporal_backward(tied, qkv_b, probs_b, **sizes)
        d_r_first = bit_step(by_shard(d_r), "shard", 1, d_qkv_b)
        d_q = grads_of([([at_a, at_b], [d_qkv_a, after(d_qkv_b, d_r_first)])], us=9)
        d_m = d_m.astype(F32)
        d_r = later_bits(d_r_first, "shard", d_q[0])
        tied = lax.optimization_barrier((d_qkv_b, *d_q, into_a, d_r, d_m))[0]
        d_q = exchange(d_q, "tensor")
        into_b, sums_xb = temporal_end(tied, x_b, g1_b, gain[0], t_all)
        swap_b = by_place(into_b, places - first_places)
        d_s = added(d_s, into_b)
        into_b = from_clips(after(swap_b, into_a, d_s))
        t, m = sums_y + sums_yb + sums_q + sums_qb + sums_x + sums_xb, sums_m
        rows = [v[n : n + 1] for n in (0, 1) for v in (t, sums_s, m)] + [t[2:4], sums_s[2:4]]
        rows = rows + [t[4:5], m[3:4], m[2:3], sums_s[4:5], d_hidden.reshape(-1, width)]
        small = plus_others(share * jnp.concatenate(rows, axis=0), "tensor")
        d_q = added(d_q, swap_b).astype(BF)
        small = plus_others(small, "shard")
        d_q = added(split_off(by_shard(d_q), "shard"), small).astype(BF)
        output = sent_back([after(piece, d_q) for piece in back])
        small = plus_others(after(small, d_q), "context")
        d_q = shed(jnp.concatenate((d_r, d_q), axis=-1), "context")
        into = jnp.swapaxes(jnp.concatenate((into_a, after(into_b, output, d_q)), axis=1), 1, 2)
        return output, into, (d_q, d_s, d_m, small)

    given = (rows_a, rows_b, pull_a, pull_b)
    parts = [one_clip(*[v[:, i] for v in given], keep[i]) for i in range(clips)]
    output, input_grad = [
        jnp.stack([part[n] for part in parts], axis=1).reshape(clips_in.shape) for n in (0, 1)
    ]
    grads = parts[0][2]
    for part in parts[1:]:
        grads = jax.tree.map(jnp.add, grads, part[2])
    d_t, d_s, d_mlp, small = grads
    d_t_rest, d_t_qkv = d_t[:, : 2 * width], d_t[:, 2 * width :]
    return (
        output,
        input_grad,
        small[0:3],
        small[3:6],
        d_t_qkv.reshape(own_rows, 3, width),
        d_t_rest[:, :width],
        d_t_rest[:, width:],
        d_s[:, : 3 * width].reshape(own_rows, 3, width),
        d_s[:, 3 * width :],
        d_mlp[:in_rows],
        d_mlp[in_rows:],
        small[6:10].reshape(2, 2, width),
        small[10:13],
        small[13],
        small[14:].reshape(-1),
    )


def solution(mesh):
    clip = P(("shard", "tensor"), "context", None, None)
    row, block = P(ALL, None), P(("shard", "context"), "tensor")
    deep, whole = P(ALL, None, None), P()
    weights = (deep, row, row, deep, row, block, block)
    in_specs = (clip, P(("shard", "tensor")), whole, whole) + weights + (whole,) * 4 + (clip,)
    out_specs = (clip, clip, whole, whole) + weights + (whole,) * 4
    return jax.shard_map(local, mesh=mesh, in_specs=in_specs, out_specs=out_specs, check_vma=False)
```
